128 devices in a mesh: lon: 16 (over z_hi, x, core), lat: 8 (over y, z_lo).
Axes of the slice: x: 4, y: 4, z: 4 (z_hi: 2, z_lo: 2; z = z_hi * 2 + z_lo), core: 2. Of those that a mesh axis runs over, the one named last changes fastest.
Arguments:
- tokens: bfloat16 [1024, 256, 512], P('lon', 'lat'), may hold values from -6 to 6
- pad_mask: int32 [1024, 256], replicated, may hold values 0 or 1
- shifts: int32 [2], replicated, may hold values from 1 to 7
- bias_table: float32 [8, 225], replicated, may hold values from -4 to 4
- rel_index: int32 [64, 64], replicated, may hold values from 0 to 224
- w_qkv: bfloat16 [512, 1536], replicated, may hold values from -0.25 to 0.25
- w_out: bfloat16 [512, 512], replicated, may hold values from -0.25 to 0.25
- grad_out: bfloat16 [1024, 256, 512], P('lon', 'lat'), may hold values from -6 to 6
Outputs:
- updated: bfloat16 [1024, 256, 512], P('lon', 'lat')
- tokens_grad: bfloat16 [1024, 256, 512], P('lon', 'lat')
- qkv_weight_grad: float32 [512, 1536], P(('lon', 'lat'))
- out_weight_grad: float32 [512, 512], P(('lon', 'lat'))
The draws below stay inside these ranges and needn't reach their ends.
All inputs are finite; a program needn't handle non-finite values.
Results may differ from the reference program's by a relative error of at most 0.009.
Values may be sent and summed in bfloat16 or wider, within the bound.
No kernel may reach another device: no remote copies, remote signals or barrier semaphores. Data moves between devices by JAX's collectives and lax.ppermute only.
A program may use at most 128 MiB of HBM per device.

```python
import jax
import jax.numpy as jnp
from jax import lax

D = 512
HEADS = 8
WIN = 8
NREL = 225
NLON = 1024
NLAT = 256


def plant(result, key, low, largest):
    spot = [jax.random.randint(jax.random.fold_in(key, axis), (), 0, length) for axis, length in enumerate(result.shape)]
    longest = result.shape.index(max(result.shape))
    neighbour = spot[:longest] + [(spot[longest] + 1) % result.shape[longest]] + spot[longest + 1:]
    return result.at[tuple(spot)].set(low).at[tuple(neighbour)].set(largest)


def steps_of(key, shape, shards, least, top_value):
    loudness = 1.0
    for axis_at, shards_of in shards:
        heights = jax.random.uniform(jax.random.fold_in(jax.random.fold_in(key, 6), axis_at), (shards_of,), jnp.float32, least / len(shards), top_value / len(shards))
        loudness = loudness * jnp.repeat(jnp.exp(heights), shape[axis_at] // shards_of).reshape((-1,) + (1,) * (len(shape) - 1 - axis_at))
    return loudness


def scatter_about(rng, shape, scale, limit, cuts=(), kind=jnp.bfloat16):
    result = scale * jax.random.normal(rng, shape, jnp.float32)
    if cuts:
        result = result * steps_of(rng, shape, cuts, -0.22, 0.18)
    return jnp.clip(result, -limit, limit).astype(kind)


def setup_inputs(seed: int = 0) -> dict:
    key_of = jax.random.split(jax.random.key(seed), 9)
    tokens = scatter_about(key_of[0], (NLON, NLAT, D), 1.0, 6.0, ((0, 16), (1, 8)))
    pad_mask = plant((jax.random.randint(key_of[1], (NLON, NLAT), 0, 8) < 7).astype(jnp.int32), jax.random.fold_in(key_of[1], 1), 0, 1)
    shifts = jax.random.randint(key_of[2], (2,), 1, WIN).astype(jnp.int32)
    bias_table = scatter_about(key_of[3], (HEADS, NREL), 1.0, 4.0, (), jnp.float32)
    rel_index = plant(jax.random.randint(key_of[4], (WIN * WIN, WIN * WIN), 0, NREL), jax.random.fold_in(key_of[4], 1), 0, NREL - 1).astype(jnp.int32)
    w_qkv = scatter_about(key_of[5], (D, 3 * D), D ** -0.5, 0.25)
    w_out = scatter_about(key_of[6], (D, D), D ** -0.5, 0.25)
    grad_out = scatter_about(key_of[7], (NLON, NLAT, D), 1.0, 6.0, ((0, 16), (1, 8)))
    return dict(tokens=tokens, pad_mask=pad_mask, shifts=shifts, bias_table=bias_table, rel_index=rel_index, w_qkv=w_qkv, w_out=w_out, grad_out=grad_out)


def norm_rows(values):
    floats = values.astype(jnp.float32)
    center = floats - lax.optimization_barrier(jnp.mean(floats, axis=-1, keepdims=True))
    inv_std = lax.rsqrt(lax.optimization_barrier(jnp.mean(center * center, axis=-1, keepdims=True)) + 1e-05)
    return (center * inv_std, inv_std)

def to_windows(field_in, window):
    span_a, span_b, channels_all = field_in.shape
    blocks = field_in.reshape(span_a // window, window, span_b // window, window, channels_all)
    return blocks.transpose(0, 2, 1, 3, 4).reshape(span_a // window, span_b // window, window * window, channels_all)

def from_windows(blocks, window):
    count_a, count_b, window_cells, channels_all = blocks.shape
    field_out = blocks.reshape(count_a, count_b, window, window, channels_all).transpose(0, 2, 1, 3, 4)
    return field_out.reshape(count_a * window, count_b * window, channels_all)

def window_masks(valid_cells, wrapped, window):
    mark_windows = to_windows(jnp.stack([valid_cells, wrapped], axis=-1), window)
    key_valid = mark_windows[..., 0] == 1
    side_marks = mark_windows[..., 1]
    same_side = side_marks[..., :, None] == side_marks[..., None, :]
    diagonal = jnp.eye(window * window, dtype=bool)
    return key_valid[..., None, :] & same_side | diagonal

def attend(packed, allowed, position_bias, head_count):
    window_count, window_cells, channels_all = packed.shape
    channels = channels_all // 4
    head_size = channels // head_count
    score_scale = head_size ** (-0.5)
    heads_view = packed.astype(jnp.float32).reshape(window_count, window_cells, 4, head_count, head_size)
    queries = heads_view[:, :, 0]
    key_part = heads_view[:, :, 1]
    values = heads_view[:, :, 2]
    attn_grad = heads_view[:, :, 3]
    scores = jnp.einsum('nqhd,nkhd->nhqk', queries, key_part) * score_scale + position_bias[None]
    unnormed = jnp.where(allowed[:, None], jnp.exp(scores), 0.0)
    normalized = unnormed / lax.optimization_barrier(jnp.sum(unnormed, axis=-1, keepdims=True))
    normalized_low = lax.optimization_barrier(normalized.astype(jnp.bfloat16)).astype(jnp.float32)
    mixed_out = jnp.einsum('nhqk,nkhd->nqhd', normalized_low, values).astype(jnp.bfloat16)
    prob_grad = jnp.einsum('nqhd,nkhd->nhqk', attn_grad, values)
    value_grad = jnp.einsum('nhqk,nqhd->nkhd', normalized_low, attn_grad)
    score_grad = normalized * (prob_grad - lax.optimization_barrier(jnp.sum(normalized * prob_grad, axis=-1, keepdims=True)))
    score_low = lax.optimization_barrier((score_grad * score_scale).astype(jnp.bfloat16)).astype(jnp.float32)
    query_grad = jnp.einsum('nhqk,nkhd->nqhd', score_low, key_part)
    key_grad = jnp.einsum('nhqk,nqhd->nkhd', score_low, queries)
    window_grads = jnp.stack([query_grad, key_grad, value_grad], axis=2)
    window_grads = window_grads.reshape(window_count, window_cells, 3 * channels).astype(jnp.bfloat16)
    return (mixed_out.reshape(window_count, window_cells, channels), window_grads)

def reference(tokens, pad_mask, shifts, bias_table, rel_index, w_qkv, w_out, grad_out):
    offset_lon = shifts[0]
    offset_lat = shifts[1]
    flat_tokens = tokens.reshape(-1, D)
    flat_grad = grad_out.reshape(-1, D)
    normed, inv_std = norm_rows(flat_tokens)
    hidden = normed.astype(jnp.bfloat16)
    qkv_rows = jnp.dot(hidden, w_qkv, preferred_element_type=jnp.float32).astype(jnp.bfloat16)
    attn_grad = jnp.dot(flat_grad, w_out.T, preferred_element_type=jnp.float32).astype(jnp.bfloat16)
    packed = jnp.concatenate([qkv_rows, attn_grad], axis=-1).reshape(NLON, NLAT, 4 * D)
    rolled = jnp.roll(packed, (-offset_lon, -offset_lat), axis=(0, 1))
    valid_cells = jnp.roll(pad_mask, (-offset_lon, -offset_lat), axis=(0, 1))
    side_row = (jnp.arange(NLAT, dtype=jnp.int32) + offset_lat >= NLAT).astype(jnp.int32)
    wrapped = jnp.broadcast_to(side_row[None, :], (NLON, NLAT))
    allowed = window_masks(valid_cells, wrapped, WIN)
    position_bias = bias_table[:, rel_index]
    windows = to_windows(rolled, WIN)

    def window_row(pair):
        row_packed, row_allowed = pair
        mixed_part, grad_part = attend(row_packed, row_allowed, position_bias, HEADS)
        return jnp.concatenate([mixed_part, grad_part], axis=-1)
    results = lax.map(window_row, (windows, allowed))
    restored = jnp.roll(from_windows(results, WIN), (offset_lon, offset_lat), axis=(0, 1)).reshape(-1, 4 * D)
    mixed_out = restored[:, :D]
    qkv_grad = restored[:, D:]
    updated = (flat_tokens.astype(jnp.float32) + jnp.dot(mixed_out, w_out, preferred_element_type=jnp.float32)).astype(jnp.bfloat16)
    normed_grad = jnp.dot(qkv_grad, w_qkv.T, preferred_element_type=jnp.float32)
    centred = normed_grad - lax.optimization_barrier(jnp.mean(normed_grad, axis=-1, keepdims=True))
    centred = centred - normed * lax.optimization_barrier(jnp.mean(normed_grad * normed, axis=-1, keepdims=True))
    tokens_grad = (flat_grad.astype(jnp.float32) + inv_std * centred).astype(jnp.bfloat16)
    qkv_weight_grad = jnp.dot(hidden.T, qkv_grad, preferred_element_type=jnp.float32)
    out_weight_grad = jnp.dot(mixed_out.T, flat_grad, preferred_element_type=jnp.float32)
    return (updated.reshape(NLON, NLAT, D), tokens_grad.reshape(NLON, NLAT, D), qkv_weight_grad, out_weight_grad)
```

```python
import jax
import jax.numpy as jnp
from jax import lax
from jax.experimental import pallas as pl
from jax.experimental.pallas import tpu as pltpu
from jax.sharding import Mesh, PartitionSpec as P

WIN = 8
CELLS = 64
D = 512
HEADS = 8
GROUP = 256
BF = jnp.bfloat16
F32 = jnp.float32
LOG2E = 1.4426950408889634
SCALE = 0.125
VMEM_LIMIT = 56 * 2**20


def dot_nn(a, b):
    return lax.dot_general(a, b, (((1,), (0,)), ((), ())), preferred_element_type=F32)


def dot_nt(a, b):
    return lax.dot_general(a, b, (((1,), (1,)), ((), ())), preferred_element_type=F32)


def dot_tn(a, b):
    return lax.dot_general(a, b, (((0,), (0,)), ((), ())), preferred_element_type=F32)


def iota(shape, dim):
    return lax.broadcasted_iota(jnp.int32, shape, dim)


def load_window(tok, grad, i, j, row, xg, hid, istd):
    x = tok[pl.ds(i, WIN), pl.ds(j, WIN), :].reshape(CELLS, D)
    center = x - jnp.mean(x, axis=-1, keepdims=True)
    inv = lax.rsqrt(jnp.mean(center * center, axis=-1, keepdims=True) + 1e-05)
    hid[pl.ds(row, CELLS), :] = (center * inv).astype(BF)
    istd[pl.ds(row, CELLS), :] = jnp.broadcast_to(inv, (CELLS, 128))
    xg[pl.ds(row, CELLS), :] = grad[pl.ds(i, WIN), pl.ds(j, WIN), :].reshape(CELLS, D).astype(BF)


def project(rows, chunk, hid, xg, w_qkv, w_out, qkvg):
    def step(c, carry):
        at = pl.ds(pl.multiple_of(c * chunk, 64), chunk)
        qkvg[at, : 3 * D] = dot_nn(hid[at, :], w_qkv[...]).astype(BF)
        qkvg[at, 3 * D :] = dot_nt(xg[at, :], w_out[...]).astype(BF)
        return carry

    lax.fori_loop(0, rows // chunk, step, 0)


def attend(first, count, thr_of, keys, bias, qkvg, mix, dq):
    lane = iota((CELLS, 128), 1)
    cell = iota((CELLS, 128), 0)
    diag = (lane & 63) == cell
    block = (iota((GROUP, GROUP), 0) >> 6) == (iota((GROUP, GROUP), 1) >> 6)
    ones = jnp.where(block, 1.0, 0.0).astype(BF)
    zero = jnp.zeros((GROUP, GROUP), BF)
    low_half = lane < 64
    units = []
    for w in range(count):
        row = pl.multiple_of((first + w) * CELLS, CELLS)
        thr = thr_of(w)
        same = ((lane & 7) >= thr) == ((cell & 7) >= thr)
        valid = jnp.broadcast_to(keys[pl.ds(first + w, 1), :], (CELLS, 128)) > 0
        ok = (valid & same) | diag
        ok = jnp.concatenate([ok, ok], axis=1)
        for h in range(2):
            c = h * GROUP
            at = pl.ds(row, CELLS)
            q = qkvg[at, c : c + GROUP]
            k = qkvg[at, D + c : D + c + GROUP]
            v = qkvg[at, 2 * D + c : 2 * D + c + GROUP]
            g = qkvg[at, 3 * D + c : 3 * D + c + GROUP]
            kbd = jnp.where(block, jnp.concatenate([k] * 4, axis=0), zero)
            vbd = jnp.where(block, jnp.concatenate([v] * 4, axis=0), zero)
            s = dot_nt(q, kbd)
            pg = dot_nt(g, vbd)
            e = jnp.where(ok, jnp.exp2(s * (SCALE * LOG2E) + bias[:, c : c + GROUP]), 0.0)
            units.append((at, c, q, g, kbd, vbd, e, pg))
    total = dot_nn(jnp.concatenate([u[6].astype(BF) for u in units], axis=0), ones)
    probs = []
    for n, u in enumerate(units):
        probs.append(u[6] / total[n * CELLS : (n + 1) * CELLS])
    dots = dot_nn(
        jnp.concatenate([(p * u[7]).astype(BF) for p, u in zip(probs, units)], axis=0), ones
    )
    for n, (at, c, q, g, kbd, vbd, e, pg) in enumerate(units):
        p = probs[n]
        p_low = p.astype(BF)
        ds = (p * (pg - dots[n * CELLS : (n + 1) * CELLS]) * SCALE).astype(BF)
        mix[at, c : c + GROUP] = dot_nn(p_low, vbd).astype(BF)
        dq[at, c : c + GROUP] = dot_nn(ds, kbd).astype(BF)
        for t in range(2):
            lo, hi = t * 128, t * 128 + 128
            kg = dot_tn(ds[:, lo:hi], q[:, lo:hi])
            vg = dot_tn(p_low[:, lo:hi], g[:, lo:hi])
            dq[at, D + c + lo : D + c + hi] = jnp.where(low_half, kg[:64], kg[64:]).astype(BF)
            dq[at, 2 * D + c + lo : 2 * D + c + hi] = jnp.where(low_half, vg[:64], vg[64:]).astype(BF)


def finish_window(tok, grad, i, j, update, normed_grad, hidden, inv):
    at = (pl.ds(i, WIN), pl.ds(j, WIN), slice(None))
    tok[at] = tok[at] + update.reshape(WIN, WIN, D)
    normed = hidden.astype(F32)
    centred = normed_grad - jnp.mean(normed_grad, axis=-1, keepdims=True)
    centred = centred - normed * jnp.mean(normed_grad * normed, axis=-1, keepdims=True)
    grad[at] = grad[at] + (inv * centred).reshape(WIN, WIN, D)


def interior_kernel(
    sc, tokens, grads, keys, bias, w_qkv, w_out,
    updated, tokens_grad, w_part,
    tok, grad, xg, hid, istd, qkvg, mix, dq,
):
    s0, s1 = sc[0], sc[1]

    def fill(n, carry):
        at = pl.ds(n * 4, 4)
        for ref, src in ((tok, tokens), (grad, grads)):
            ref[at, :, :] = pltpu.roll(src[at, :, :].astype(F32), 32 - s1, 1)
        return carry

    lax.fori_loop(0, 16, fill, 0)

    def load(a, carry):
        for b in range(3):
            row = pl.multiple_of((a * 3 + b) * CELLS, CELLS)
            load_window(tok, grad, s0 + a * WIN, b * WIN, row, xg, hid, istd)
        return carry

    lax.fori_loop(0, 7, load, 0)
    project(21 * CELLS, 448, hid, xg, w_qkv, w_out, qkvg)

    def windows(a, carry):
        attend(a * 3, 3, lambda w: 8, keys, bias, qkvg, mix, dq)
        return carry

    lax.fori_loop(0, 7, windows, 0)

    def finish(a, carry):
        at = pl.ds(pl.multiple_of(a * 192, 64), 192)
        update = dot_nn(mix[at, :], w_out[...])
        normed_grad = dot_nt(dq[at, :], w_qkv[...])
        hidden = hid[at, :]
        inv = istd[at, :]
        for b in range(3):
            r = slice(b * CELLS, (b + 1) * CELLS)
            finish_window(
                tok, grad, s0 + a * WIN, b * WIN,
                update[r], normed_grad[r], hidden[r], inv[r, :1],
            )
        return carry

    lax.fori_loop(0, 7, finish, 0)
    for b in range(2):
        r = slice(b * 256, (b + 1) * 256)
        w_part[r, : 3 * D] = dot_tn(hid[:, r], dq[...])
        w_part[r, 3 * D :] = dot_tn(mix[:, r], xg[...])

    def store(n, carry):
        at = pl.ds(n * 4, 4)
        for ref, out in ((tok, updated), (grad, tokens_grad)):
            out[at, :, :] = pltpu.roll(ref[at, :, :], s1, 1).astype(BF)
        return carry

    lax.fori_loop(0, 16, store, 0)


def edge_kernel(
    sc, tokens, grads, halo_lon, halo_lat, halo_cor, keys, bias, w_qkv, w_out, w_first,
    edge_lat, edge_lon, out_lat, out_lon, out_cor, w_mine, w_other,
    tok, grad, xg, hid, istd, qkvg, mix, dq, w_sum,
):
    s0, s1, core, thr_edge = sc[0], sc[1], sc[2], sc[3]

    def fill(n, carry):
        at = pl.ds(n * 8, 8)
        for ref, src, c in ((tok, tokens, 0), (grad, grads, D)):
            rows = [src[at, 24:32, :].astype(F32), halo_lat[at, :, c : c + D].astype(F32)]
            ref[at, 24:32, :] = pltpu.roll(jnp.concatenate(rows, axis=1), 16 - s1, 1)[:, :8]
        return carry

    lax.fori_loop(0, 7, fill, 0)
    for r in range(0, 8, 4):
        for ref, src, c in ((tok, tokens, 0), (grad, grads, D)):
            rows = [src[56 + r : 60 + r], halo_lat[56 + r : 60 + r, :, c : c + D]]
            rows = jnp.concatenate([part.astype(F32) for part in rows], axis=1)
            ref[56 + r : 60 + r] = pltpu.roll(rows, 40 - s1, 1)[:, :32]
            rows = [halo_lon[r : r + 4, :, c : c + D], halo_cor[r : r + 4, :, c : c + D]]
            rows = jnp.concatenate([part.astype(F32) for part in rows], axis=1)
            ref[64 + r : 68 + r] = pltpu.roll(rows, 40 - s1, 1)[:, :32]

    def load_side(a, carry):
        row = pl.multiple_of(a * CELLS, CELLS)
        load_window(tok, grad, s0 + a * WIN, 24, row, xg, hid, istd)
        return carry

    lax.fori_loop(0, 7, load_side, 0)
    for b in range(4):
        load_window(tok, grad, s0 + 56, b * WIN, (7 + b) * CELLS, xg, hid, istd)
    tail = slice(11 * CELLS, 12 * CELLS)
    xg[tail, :] = jnp.zeros((CELLS, D), BF)
    hid[tail, :] = jnp.zeros((CELLS, D), BF)
    istd[tail, :] = jnp.zeros((CELLS, 128), F32)
    project(12 * CELLS, 384, hid, xg, w_qkv, w_out, qkvg)

    def windows(a, carry):
        def thr_of(w):
            n = a * 3 + w
            return jnp.where((n < 7) | (n == 10), thr_edge, 8)

        attend(a * 3, 3, thr_of, keys, bias, qkvg, mix, dq)
        return carry

    lax.fori_loop(0, 4, windows, 0)
    for b in range(2):
        r = slice(b * 256, (b + 1) * 256)
        w_sum[r, : 3 * D] = w_first[r, : 3 * D] + dot_tn(hid[:, r], dq[...])
        w_sum[r, 3 * D :] = w_first[r, 3 * D :] + dot_tn(mix[:, r], xg[...])

    def split(n, carry):
        to = pl.ds(pl.multiple_of(n * 32, 32), 32)
        w_mine[to, :] = w_sum[pl.ds(pl.multiple_of((2 * n + core) * 32, 32), 32), :].astype(BF)
        w_other[to, :] = w_sum[pl.ds(pl.multiple_of((2 * n + 1 - core) * 32, 32), 32), :].astype(BF)
        return carry

    lax.fori_loop(0, 8, split, 0)

    for base, count in ((0, 4), (4, 4), (8, 3)):
        at = slice(base * CELLS, (base + count) * CELLS)
        update = dot_nn(mix[at, :], w_out[...])
        normed_grad = dot_nt(dq[at, :], w_qkv[...])
        for b in range(count):
            r = slice(b * CELLS, (b + 1) * CELLS)
            rr = slice((base + b) * CELLS, (base + b + 1) * CELLS)
            n = base + b
            a, c = (n, 3) if n < 7 else (7, n - 7)
            finish_window(
                tok, grad, s0 + a * WIN, c * WIN,
                update[r], normed_grad[r], hid[rr, :], istd[rr, :1],
            )

    def store(n, carry):
        at = pl.ds(n * 8, 8)
        for ref, c in ((tok, 0), (grad, D)):
            rows = ref[at, 24:32, :]
            rows = jnp.concatenate([rows, jnp.zeros_like(rows)], axis=1)
            rows = pltpu.roll(rows, s1, 1).astype(BF)
            edge_lat[at, :, c : c + D] = rows[:, :8]
            out_lat[at, :, c : c + D] = rows[:, 8:]
        return carry

    lax.fori_loop(0, 7, store, 0)
    for r in range(0, 8, 4):
        for ref, c in ((tok, 0), (grad, D)):
            cols = slice(c, c + D)
            pad = jnp.zeros((4, 8, D), F32)
            rows = pltpu.roll(jnp.concatenate([ref[56 + r : 60 + r], pad], axis=1), s1, 1)
            rows = rows.astype(BF)
            edge_lon[r : r + 4, :, cols] = rows[:, :32]
            edge_lat[56 + r : 60 + r, :, cols] = rows[:, 24:32]
            out_lat[56 + r : 60 + r, :, cols] = rows[:, 32:]
            rows = pltpu.roll(jnp.concatenate([ref[64 + r : 68 + r], pad], axis=1), s1, 1)
            rows = rows.astype(BF)
            out_lon[r : r + 4, :, cols] = rows[:, :32]
            out_cor[r : r + 4, :, cols] = rows[:, 32:]


def merge_kernel(
    sc, updated, tokens_grad, edge_lat, edge_lon, in_lat, in_lon, in_cor, out_updated, out_grad
):
    s0, s1 = sc[0], sc[1]
    for src, out, c in ((updated, out_updated, 0), (tokens_grad, out_grad, D)):
        cols = slice(c, c + D)
        out[:, 8:24, :] = src[:, 8:24, :]
        lat = iota((64, 8, D), 1)
        lon = iota((64, 8, D), 0)
        left = jnp.where(lat < s1, in_lat[:, :, cols].astype(F32), src[:, 0:8, :].astype(F32))
        out[:, 0:8, :] = left.astype(BF)
        right = jnp.where(lat >= s1, edge_lat[:, :, cols].astype(F32), src[:, 24:32, :].astype(F32))
        out[:, 24:32, :] = right.astype(BF)
        lat = iota((8, 32, D), 1)
        lon = iota((8, 32, D), 0)
        low = out[56:64, :, :].astype(F32)
        low = jnp.where((lon >= s0) & (lat >= s1), edge_lon[:, :, cols].astype(F32), low)
        out[56:64, :, :] = low.astype(BF)
        top = out[0:8, :, :].astype(F32)
        top = jnp.where((lon < s0) & (lat >= s1), in_lon[:, :, cols].astype(F32), top)
        out[0:8, :, :] = top.astype(BF)
        lat = iota((8, 8, D), 1)
        lon = iota((8, 8, D), 0)
        spot = out[0:8, 0:8, :].astype(F32)
        spot = jnp.where((lon < s0) & (lat < s1), in_cor[:, :, cols].astype(F32), spot)
        out[0:8, 0:8, :] = spot.astype(BF)


def vmem(shape, dtype):
    return pltpu.VMEM(shape, dtype)


def sds(shape, dtype):
    return jax.ShapeDtypeStruct(shape, dtype)


def call(kernel, out_shape, scratch, count):
    in_specs = [pl.BlockSpec(memory_space=pltpu.SMEM)]
    in_specs += [pl.BlockSpec(memory_space=pltpu.VMEM)] * (count - 1)
    return pl.pallas_call(
        kernel,
        out_shape=out_shape,
        in_specs=in_specs,
        out_specs=[pl.BlockSpec(memory_space=pltpu.VMEM)] * len(out_shape),
        scratch_shapes=scratch,
        compiler_params=pltpu.CompilerParams(vmem_limit_bytes=VMEM_LIMIT),
    )


def window_scratch(lon, lat, rows):
    return [
        vmem((lon, lat, D), F32),
        vmem((lon, lat, D), F32),
        vmem((rows, D), BF),
        vmem((rows, D), BF),
        vmem((rows, 128), F32),
        vmem((rows, 4 * D), BF),
        vmem((rows, D), BF),
        vmem((rows, 3 * D), BF),
    ]


LON = ("zh", "x", "core")
LAT = ("y", "zl")
ALL = LON + LAT


def shift_to(value, d_lon, d_lat):
    pairs = []
    for a in range(16):
        for b in range(8):
            pairs.append((a * 8 + b, ((a + d_lon) % 16) * 8 + (b + d_lat) % 8))
    return lax.ppermute(value, ALL, pairs)


def scatter_sum(blocks, axes, count):
    here = lax.axis_index(axes)
    total = lax.dynamic_index_in_dim(blocks, here, 0, keepdims=False).astype(F32)
    for step in range(1, count):
        block = lax.dynamic_index_in_dim(blocks, (here + step) % count, 0, keepdims=False)
        pairs = [(n, (n + step) % count) for n in range(count)]
        total = total + lax.ppermute(block, axes, pairs).astype(F32)
    return total


def bias_lookup(bias_table, rel_index):
    one_hot = (
        rel_index.reshape(-1)[:, None] == jnp.arange(bias_table.shape[1], dtype=jnp.int32)[None, :]
    ).astype(F32)
    rows = jnp.dot(one_hot, bias_table.T, precision=lax.Precision.HIGHEST)
    return rows.reshape(CELLS, CELLS, HEADS).transpose(0, 2, 1).reshape(CELLS, HEADS * CELLS)


def local(tokens, pad_mask, shifts, bias_table, rel_index, w_qkv, w_out, grad_out):
    lon_at = lax.axis_index(LON)
    lat_at = lax.axis_index(LAT)
    core = lax.axis_index("core")
    s0, s1 = shifts[0], shifts[1]

    both = lambda a, b: jnp.concatenate([tokens[a, b], grad_out[a, b]], axis=-1)
    halo_lat = shift_to(both(slice(None), slice(0, 8)), 0, -1)
    halo_lon = shift_to(both(slice(0, 8), slice(None)), -1, 0)
    halo_cor = shift_to(both(slice(0, 8), slice(0, 8)), -1, -1)

    bias = bias_lookup(bias_table, rel_index) * LOG2E
    lon_places = (lon_at * 64 + s0 + jnp.arange(64, dtype=jnp.int32)) % 1024
    lat_places = (lat_at * 32 + s1 + jnp.arange(32, dtype=jnp.int32)) % 256
    valid = jnp.take(jnp.take(pad_mask, lon_places, axis=0), lat_places, axis=1)
    keys = valid.reshape(8, 8, 4, 8).transpose(0, 2, 1, 3).reshape(8, 4, CELLS)
    keys = jnp.concatenate([keys, keys], axis=-1)
    inner_keys = keys[:7, :3].reshape(21, 128)
    edge_keys = jnp.concatenate([keys[:7, 3], keys[7], jnp.zeros((1, 128), jnp.int32)], axis=0)
    thr = jnp.where(lat_at == 7, 8 - s1, 8)
    sc = jnp.stack([s0, s1, core, thr]).astype(jnp.int32)

    updated, tokens_grad, w_first = call(
        interior_kernel,
        [sds((64, 32, D), BF), sds((64, 32, D), BF), sds((D, 4 * D), F32)],
        window_scratch(64, 32, 21 * CELLS),
        7,
    )(sc, tokens, grad_out, inner_keys, bias, w_qkv, w_out)

    edge_lat, edge_lon, out_lat, out_lon, out_cor, w_mine, w_other = call(
        edge_kernel,
        [
            sds((64, 8, 2 * D), BF),
            sds((8, 32, 2 * D), BF),
            sds((64, 8, 2 * D), BF),
            sds((8, 32, 2 * D), BF),
            sds((8, 8, 2 * D), BF),
            sds((D // 2, 4 * D), BF),
            sds((D // 2, 4 * D), BF),
        ],
        window_scratch(72, 32, 12 * CELLS) + [vmem((D, 4 * D), F32)],
        11,
    )(sc, tokens, grad_out, halo_lon, halo_lat, halo_cor, edge_keys, bias, w_qkv, w_out, w_first)

    w_got = lax.ppermute(w_other, "core", [(0, 1), (1, 0)])
    in_lat = shift_to(out_lat, 0, 1)
    in_lon = shift_to(out_lon, 1, 0)
    in_cor = shift_to(out_cor, 1, 1)
    total = (w_mine.astype(F32) + w_got.astype(F32)).astype(BF)
    total = total.reshape(2, 4, 32, 4 * D).transpose(1, 0, 2, 3)
    total = scatter_sum(total, "x", 4).astype(BF)
    total = total.reshape(2, 4, 8, 4 * D).transpose(1, 0, 2, 3)
    total = scatter_sum(total, "y", 4).astype(BF)
    total = scatter_sum(total.reshape(4, 4, 4 * D), ("zh", "zl"), 4)

    updated, tokens_grad = call(
        merge_kernel, [sds((64, 32, D), BF), sds((64, 32, D), BF)], [], 8
    )(sc, updated, tokens_grad, edge_lat, edge_lon, in_lat, in_lon, in_cor)
    return (updated, tokens_grad, total[:, : 3 * D], total[:, 3 * D :])


def solution(mesh):
    fine = Mesh(mesh.devices.reshape(2, 4, 2, 4, 2), ALL)
    in_specs = (P(LON, LAT, None), P(), P(), P(), P(), P(), P(), P(LON, LAT, None))
    out_specs = (P(LON, LAT, None), P(LON, LAT, None), P(ALL, None), P(ALL, None))
    return jax.shard_map(local, mesh=fine, in_specs=in_specs, out_specs=out_specs, check_vma=False)
```

```python
import jax
import jax.numpy as jnp
from jax import lax
from jax.experimental import pallas as pl
from jax.experimental.pallas import tpu as pltpu
from jax.sharding import Mesh, PartitionSpec as P

WIN = 8
CELLS = 64
D = 512
HEADS = 8
GROUP = 256
BF = jnp.bfloat16
F32 = jnp.float32
LOG2E = 1.4426950408889634
SCALE = 0.125
VMEM_LIMIT = 56 * 2**20
LON = ("zh", "x", "core")
LAT = ("y", "zl")
ALL = LON + LAT


def dot_nn(a, b):
    return lax.dot_general(a, b, (((1,), (0,)), ((), ())), preferred_element_type=F32)


def dot_nt(a, b):
    return lax.dot_general(a, b, (((1,), (1,)), ((), ())), preferred_element_type=F32)


def dot_tn(a, b):
    return lax.dot_general(a, b, (((0,), (0,)), ((), ())), preferred_element_type=F32)


def iota(shape, dim):
    return lax.broadcasted_iota(jnp.int32, shape, dim)


def load_window(tok, grad, i, j, row, xg, hid, istd):
    x = tok[pl.ds(i, WIN), pl.ds(j, WIN), :].reshape(CELLS, D)
    center = x - jnp.mean(x, axis=-1, keepdims=True)
    inv = lax.rsqrt(jnp.mean(center * center, axis=-1, keepdims=True) + 1e-05)
    hid[pl.ds(row, CELLS), :] = (center * inv).astype(BF)
    istd[pl.ds(row, CELLS), :] = jnp.broadcast_to(inv, (CELLS, 128))
    xg[pl.ds(row, CELLS), :] = grad[pl.ds(i, WIN), pl.ds(j, WIN), :].reshape(CELLS, D).astype(BF)


def project(rows, chunk, hid, xg, w_qkv, w_out, qkvg):
    def step(c, carry):
        at = pl.ds(pl.multiple_of(c * chunk, 64), chunk)
        qkvg[at, : 3 * D] = dot_nn(hid[at, :], w_qkv[...]).astype(BF)
        qkvg[at, 3 * D :] = dot_nt(xg[at, :], w_out[...]).astype(BF)
        return carry

    lax.fori_loop(0, rows // chunk, step, 0)


def attend(first, marks, thrs, bias, qkvg, mix, dq):
    lane = iota((CELLS, 128), 1)
    cell = iota((CELLS, 128), 0)
    diag = (lane & 63) == cell
    block = (iota((GROUP, GROUP), 0) >> 6) == (iota((GROUP, GROUP), 1) >> 6)
    ones = jnp.where(block, 1.0, 0.0).astype(BF)
    zero = jnp.zeros((GROUP, GROUP), BF)
    low_half = lane < 64
    units = []
    for w, (mark, thr) in enumerate(zip(marks, thrs)):
        row = pl.multiple_of((first + w) * CELLS, CELLS)
        same = ((lane & 7) >= thr) == ((cell & 7) >= thr)
        valid = jnp.broadcast_to(mark, (CELLS, 128)) > 0.5
        ok = (valid & same) | diag
        ok = jnp.concatenate([ok, ok], axis=1)
        for h in range(2):
            c = h * GROUP
            at = pl.ds(row, CELLS)
            q = qkvg[at, c : c + GROUP]
            k = qkvg[at, D + c : D + c + GROUP]
            v = qkvg[at, 2 * D + c : 2 * D + c + GROUP]
            g = qkvg[at, 3 * D + c : 3 * D + c + GROUP]
            kbd = jnp.where(block, jnp.concatenate([k] * 4, axis=0), zero)
            vbd = jnp.where(block, jnp.concatenate([v] * 4, axis=0), zero)
            s = dot_nt(q, kbd)
            pg = dot_nt(g, vbd)
            e = jnp.where(ok, jnp.exp2(s * (SCALE * LOG2E) + bias[:, c : c + GROUP]), 0.0)
            units.append((at, c, q, g, kbd, vbd, e, pg))
    total = dot_nn(jnp.concatenate([u[6].astype(BF) for u in units], axis=0), ones)
    probs = []
    for n, u in enumerate(units):
        probs.append(u[6] / total[n * CELLS : (n + 1) * CELLS])
    dots = dot_nn(
        jnp.concatenate([(p * u[7]).astype(BF) for p, u in zip(probs, units)], axis=0), ones
    )
    for n, (at, c, q, g, kbd, vbd, e, pg) in enumerate(units):
        p = probs[n]
        p_low = p.astype(BF)
        ds = (p * (pg - dots[n * CELLS : (n + 1) * CELLS]) * SCALE).astype(BF)
        mix[at, c : c + GROUP] = dot_nn(p_low, vbd).astype(BF)
        dq[at, c : c + GROUP] = dot_nn(ds, kbd).astype(BF)
        for t in range(2):
            lo, hi = t * 128, t * 128 + 128
            kg = dot_tn(ds[:, lo:hi], q[:, lo:hi])
            vg = dot_tn(p_low[:, lo:hi], g[:, lo:hi])
            dq[at, D + c + lo : D + c + hi] = jnp.where(low_half, kg[:64], kg[64:]).astype(BF)
            dq[at, 2 * D + c + lo : 2 * D + c + hi] = jnp.where(low_half, vg[:64], vg[64:]).astype(BF)


def finish_window(tok, grad, i, j, update, normed_grad, hidden, inv):
    at = (pl.ds(i, WIN), pl.ds(j, WIN), slice(None))
    tok[at] = tok[at] + update.reshape(WIN, WIN, D)
    finish_grad(grad, i, j, normed_grad, hidden, inv)


def finish_grad(grad, i, j, normed_grad, hidden, inv):
    at = (pl.ds(i, WIN), pl.ds(j, WIN), slice(None))
    normed = hidden.astype(F32)
    centred = normed_grad - jnp.mean(normed_grad, axis=-1, keepdims=True)
    centred = centred - normed * jnp.mean(normed_grad * normed, axis=-1, keepdims=True)
    grad[at] = grad[at] + (inv * centred).reshape(WIN, WIN, D)


def make_tables(pad_mask, bias_table, rel_index, s0, s1, keys, bias, table, rel):
    base = lax.axis_index(LON) * 64
    first = pad_mask[pl.ds(pl.multiple_of(base, 8), 64), :].astype(F32)
    after = pad_mask[pl.ds(pl.multiple_of((base + 64) & 1023, 8), 8), :].astype(F32)
    rows = pltpu.roll(jnp.concatenate([first, after], axis=0), 72 - s0, 0)[:64]
    lane = iota((256, 512), 1)
    place = (lax.axis_index(LAT) * 32 + s1 + (lane >> 7) * 8 + (lane & 7)) & 255
    pick = jnp.where(iota((256, 512), 0) == place, 1.0, 0.0).astype(BF)
    marks = dot_nn(rows.astype(BF), pick)
    own = (iota((64, 512), 0) & 7) == ((iota((64, 512), 1) & 63) >> 3)
    marks = jnp.sum(jnp.where(own, marks, 0.0).reshape(8, 8, 512), axis=1)
    for b in range(4):
        keys[8 * b : 8 * b + 8, :] = marks[:, 128 * b : 128 * b + 128]

    table[...] = jnp.zeros((8, 256), F32)
    table[:, :225] = bias_table[...] * LOG2E
    rel[:, :64] = rel_index[...]
    rel[:, 64:] = rel_index[...]
    at = rel[...]
    low = at < 128
    at = at & 127
    left = iota((CELLS, 128), 1) < 64
    for pair in range(4):
        found = []
        for h in (2 * pair, 2 * pair + 1):
            half = [
                jnp.take_along_axis(
                    jnp.broadcast_to(table[h : h + 1, c : c + 128], (CELLS, 128)), at, axis=1
                )
                for c in (0, 128)
            ]
            found.append(jnp.where(low, half[0], half[1]))
        bias[:, pair * 128 : pair * 128 + 128] = jnp.where(left, found[0], found[1])


def fill_shifted(s1, src, ref):
    def fill(n, carry):
        at = pl.ds(n * 4, 4)
        ref[at, :, :] = pltpu.roll(src[at, :, :].astype(F32), 32 - s1, 1)
        return carry

    lax.fori_loop(0, 16, fill, 0)


def interior_kernel(
    shifts, tokens, grads, pad_mask, bias_table, rel_index, w_qkv, w_out,
    w_part, mix_out, dq_out, hid_out, istd_out, keys, bias,
    tok, grad, xg, hid, istd, qkvg, mix, dq, table, rel, w_sum, sems,
):
    s0, s1 = shifts[0], shifts[1]
    make_tables(pad_mask, bias_table, rel_index, s0, s1, keys, bias, table, rel)
    fill_shifted(s1, tokens, tok)
    fill_shifted(s1, grads, grad)

    def load(a, carry):
        for b in range(3):
            row = pl.multiple_of((a * 3 + b) * CELLS, CELLS)
            load_window(tok, grad, s0 + a * WIN, b * WIN, row, xg, hid, istd)
        return carry

    lax.fori_loop(0, 7, load, 0)
    project(21 * CELLS, 448, hid, xg, w_qkv, w_out, qkvg)

    def windows(a, carry):
        marks = [keys[pl.ds(8 * b + a, 1), :] for b in range(3)]
        attend(a * 3, marks, [8] * 3, bias, qkvg, mix, dq)
        return carry

    lax.fori_loop(0, 7, windows, 0)
    pairs = ((mix, mix_out), (dq, dq_out), (hid, hid_out), (istd, istd_out))
    copies = [pltpu.make_async_copy(a, b, sems.at[n]) for n, (a, b) in enumerate(pairs)]
    for copy in copies:
        copy.start()
    for b in range(2):
        r = slice(b * 256, (b + 1) * 256)
        w_sum[r, : 3 * D] = dot_tn(hid[:, r], dq[...])
        w_sum[r, 3 * D :] = dot_tn(mix[:, r], xg[...])
        copy = pltpu.make_async_copy(w_sum.at[r], w_part.at[r], sems.at[4 + b])
        copy.start()
        copies.append(copy)
    for copy in copies:
        copy.wait()


def store_interior(s0, s1, ref, edge_lat, edge_lon, out):
    lat = iota((4, 8, D), 1)

    def store(n, carry):
        at = pl.ds(n * 4, 4)
        rows = pltpu.roll(ref[at, :, :], s1, 1)
        last = jnp.where(lat >= s1, edge_lat[at, :, :].astype(F32), rows[:, 24:])
        out[at, :, :] = jnp.concatenate([rows[:, :24], last], axis=1).astype(BF)
        return carry

    lax.fori_loop(0, 16, store, 0)
    mark = (iota((8, 32, D), 0) >= s0) & (iota((8, 32, D), 1) >= s1)
    rows = out[56:64, :, :].astype(F32)
    out[56:64, :, :] = jnp.where(mark, edge_lon[...].astype(F32), rows).astype(BF)


def updated_kernel(shifts, tokens, mix, w_out, edge_lat, edge_lon, out, tok):
    s0, s1 = shifts[0], shifts[1]
    fill_shifted(s1, tokens, tok)

    def finish(a, carry):
        update = dot_nn(mix[pl.ds(pl.multiple_of(a * 192, 64), 192), :], w_out[...])
        for b in range(3):
            at = (pl.ds(s0 + a * WIN, WIN), pl.ds(b * WIN, WIN), slice(None))
            tok[at] = tok[at] + update[b * CELLS : (b + 1) * CELLS].reshape(WIN, WIN, D)
        return carry

    lax.fori_loop(0, 7, finish, 0)
    store_interior(s0, s1, tok, edge_lat, edge_lon, out)


def grad_kernel(shifts, grads, hid, istd, dq, w_qkv, edge_lat, edge_lon, out, grad):
    s0, s1 = shifts[0], shifts[1]
    fill_shifted(s1, grads, grad)

    def finish(a, carry):
        at = pl.ds(pl.multiple_of(a * 192, 64), 192)
        normed_grad = dot_nt(dq[at, :], w_qkv[...])
        hidden, inv = hid[at, :], istd[at, :]
        for b in range(3):
            r = slice(b * CELLS, (b + 1) * CELLS)
            finish_grad(grad, s0 + a * WIN, b * WIN, normed_grad[r], hidden[r], inv[r, :1])
        return carry

    lax.fori_loop(0, 7, finish, 0)
    store_interior(s0, s1, grad, edge_lat, edge_lon, out)


def edge_fill(s1, tokens, grads, halo_lon, halo_lat, halo_cor, tok, grad):
    def fill(n, carry):
        at = pl.ds(n * 8, 8)
        for ref, src, c in ((tok, tokens, 0), (grad, grads, D)):
            rows = [src[at, 24:32, :].astype(F32), halo_lat[at, :, c : c + D].astype(F32)]
            ref[at, 24:32, :] = pltpu.roll(jnp.concatenate(rows, axis=1), 16 - s1, 1)[:, :8]
        return carry

    lax.fori_loop(0, 7, fill, 0)
    for r in range(0, 8, 4):
        for ref, src, c in ((tok, tokens, 0), (grad, grads, D)):
            rows = [src[56 + r : 60 + r], halo_lat[56 + r : 60 + r, :, c : c + D]]
            rows = jnp.concatenate([part.astype(F32) for part in rows], axis=1)
            ref[56 + r : 60 + r] = pltpu.roll(rows, 40 - s1, 1)[:, :32]
            rows = [halo_lon[r : r + 4, :, c : c + D], halo_cor[r : r + 4, :, c : c + D]]
            rows = jnp.concatenate([part.astype(F32) for part in rows], axis=1)
            ref[64 + r : 68 + r] = pltpu.roll(rows, 40 - s1, 1)[:, :32]


def edge_load(s0, tok, grad, xg, hid, istd):
    def load_side(a, carry):
        row = pl.multiple_of(a * CELLS, CELLS)
        load_window(tok, grad, s0 + a * WIN, 24, row, xg, hid, istd)
        return carry

    lax.fori_loop(0, 7, load_side, 0)
    for b in range(4):
        load_window(tok, grad, s0 + 56, b * WIN, (7 + b) * CELLS, xg, hid, istd)


def edge_kernel(
    shifts, tokens, grads, halo_lon, halo_lat, halo_cor, keys, bias, w_qkv, w_out, w_part,
    edge_lat, edge_lon, out_lat, out_lon, out_cor, w_mine, w_other,
    tok, grad, xg, hid, istd, qkvg, mix, dq, w_sum, sem,
):
    s0, s1 = shifts[0], shifts[1]
    core = lax.axis_index("core")
    thr_edge = jnp.where(lax.axis_index(LAT) == 7, 8 - s1, 8)
    w_copy = pltpu.make_async_copy(w_part, w_sum, sem)
    w_copy.start()
    edge_fill(s1, tokens, grads, halo_lon, halo_lat, halo_cor, tok, grad)
    edge_load(s0, tok, grad, xg, hid, istd)
    tail = slice(11 * CELLS, 12 * CELLS)
    xg[tail, :] = jnp.zeros((CELLS, D), BF)
    hid[tail, :] = jnp.zeros((CELLS, D), BF)
    project(12 * CELLS, 384, hid, xg, w_qkv, w_out, qkvg)

    def windows(a, carry):
        seen, thr = [], []
        for w in range(3):
            n = a * 3 + w
            row = jnp.where(n < 7, 24 + n, jnp.minimum(8 * n - 49, 31))
            seen.append(keys[pl.ds(row, 1), :])
            thr.append(jnp.where((n < 7) | (n == 10), thr_edge, 8))
        attend(a * 3, seen, thr, bias, qkvg, mix, dq)
        return carry

    lax.fori_loop(0, 4, windows, 0)
    w_copy.wait()
    for b in range(2):
        r = slice(b * 256, (b + 1) * 256)
        w_sum[r, : 3 * D] += dot_tn(hid[:, r], dq[...])
        w_sum[r, 3 * D :] += dot_tn(mix[:, r], xg[...])

    def split(n, carry):
        to = pl.ds(pl.multiple_of(n * 32, 32), 32)
        w_mine[to, :] = w_sum[pl.ds(pl.multiple_of((2 * n + core) * 32, 32), 32), :].astype(BF)
        w_other[to, :] = w_sum[pl.ds(pl.multiple_of((2 * n + 1 - core) * 32, 32), 32), :].astype(BF)
        return carry

    lax.fori_loop(0, 8, split, 0)

    for base, count in ((0, 4), (4, 4), (8, 3)):
        at = slice(base * CELLS, (base + count) * CELLS)
        update = dot_nn(mix[at, :], w_out[...])
        normed_grad = dot_nt(dq[at, :], w_qkv[...])
        for b in range(count):
            r = slice(b * CELLS, (b + 1) * CELLS)
            rr = slice((base + b) * CELLS, (base + b + 1) * CELLS)
            n = base + b
            a, c = (n, 3) if n < 7 else (7, n - 7)
            finish_window(
                tok, grad, s0 + a * WIN, c * WIN,
                update[r], normed_grad[r], hid[rr, :], istd[rr, :1],
            )

    def store(n, carry):
        at = pl.ds(n * 8, 8)
        for ref, c in ((tok, 0), (grad, D)):
            rows = ref[at, 24:32, :]
            rows = jnp.concatenate([rows, jnp.zeros_like(rows)], axis=1)
            rows = pltpu.roll(rows, s1, 1).astype(BF)
            edge_lat[c // D, at, :, :] = rows[:, :8]
            out_lat[at, :, c : c + D] = rows[:, 8:]
        return carry

    lax.fori_loop(0, 7, store, 0)
    for r in range(0, 8, 4):
        for ref, c in ((tok, 0), (grad, D)):
            cols = slice(c, c + D)
            pad = jnp.zeros((4, 8, D), F32)
            rows = pltpu.roll(jnp.concatenate([ref[56 + r : 60 + r], pad], axis=1), s1, 1)
            rows = rows.astype(BF)
            edge_lon[c // D, r : r + 4, :, :] = rows[:, :32]
            edge_lat[c // D, 56 + r : 60 + r, :, :] = rows[:, 24:32]
            out_lat[56 + r : 60 + r, :, cols] = rows[:, 32:]
            rows = pltpu.roll(jnp.concatenate([ref[64 + r : 68 + r], pad], axis=1), s1, 1)
            rows = rows.astype(BF)
            out_lon[r : r + 4, :, cols] = rows[:, :32]
            out_cor[r : r + 4, :, cols] = rows[:, 32:]


def return_kernel(
    shifts, updated, tokens_grad, in_lat, in_lon, in_cor, out_updated, out_grad, side, top, sems
):
    s0, s1 = shifts[0], shifts[1]
    outs = (out_updated, out_grad)
    into = []
    for n, out in enumerate(outs):
        into.append(pltpu.make_async_copy(out.at[:, 0:16, :], side.at[n], sems.at[2 * n]))
        into.append(pltpu.make_async_copy(out.at[0:8, 16:32, :], top.at[n], sems.at[2 * n + 1]))
    for copy in into:
        copy.start()
    for copy in into:
        copy.wait()
    lat = iota((8, 8, D), 1)
    lon = iota((8, 8, D), 0)
    pick = lambda mark, new, old: jnp.where(mark, new.astype(F32), old)
    for n in range(2):
        cols = slice(n * D, n * D + D)

        def rest(r, carry, n=n, cols=cols):
            at = pl.ds(pl.multiple_of(r * 8, 8), 8)
            rows = side[n, at, 0:8, :].astype(F32)
            side[n, at, 0:8, :] = pick(lat < s1, in_lat[at, :, cols], rows).astype(BF)
            return carry

        lax.fori_loop(1, 8, rest, 0)
        rows = side[n, 0:8, 0:8, :].astype(F32)
        rows = pick((lat < s1) & (lon >= s0), in_lat[0:8, :, cols], rows)
        rows = pick((lat >= s1) & (lon < s0), in_lon[:, 0:8, cols], rows)
        rows = pick((lat < s1) & (lon < s0), in_cor[:, :, cols], rows)
        side[n, 0:8, 0:8, :] = rows.astype(BF)
        rows = side[n, 0:8, 8:16, :].astype(F32)
        side[n, 0:8, 8:16, :] = pick(lon < s0, in_lon[:, 8:16, cols], rows).astype(BF)
        rows = top[n].astype(F32)
        top[n] = pick(iota((8, 16, D), 0) < s0, in_lon[:, 16:32, cols], rows).astype(BF)
    back = []
    for n, out in enumerate(outs):
        back.append(pltpu.make_async_copy(side.at[n], out.at[:, 0:16, :], sems.at[2 * n]))
        back.append(pltpu.make_async_copy(top.at[n], out.at[0:8, 16:32, :], sems.at[2 * n + 1]))
    for copy in back:
        copy.start()
    for copy in back:
        copy.wait()


def vmem(shape, dtype):
    return pltpu.VMEM(shape, dtype)


def sds(shape, dtype):
    return jax.ShapeDtypeStruct(shape, dtype)


IN_VMEM = pl.BlockSpec(memory_space=pltpu.VMEM)
IN_SMEM = pl.BlockSpec(memory_space=pltpu.SMEM)
IN_HBM = pl.BlockSpec(memory_space=pl.ANY)


def call(kernel, out_shape, scratch, in_specs, out_specs, aliases=None):
    return pl.pallas_call(
        kernel,
        out_shape=out_shape,
        in_specs=[IN_SMEM] + in_specs,
        out_specs=out_specs,
        scratch_shapes=scratch,
        input_output_aliases=aliases or {},
        compiler_params=pltpu.CompilerParams(vmem_limit_bytes=VMEM_LIMIT),
    )


def window_scratch(lon, lat, rows):
    return [
        vmem((lon, lat, D), F32),
        vmem((lon, lat, D), F32),
        vmem((rows, D), BF),
        vmem((rows, D), BF),
        vmem((rows, 128), F32),
    ]


def attend_scratch(rows):
    return [
        vmem((rows, 4 * D), BF),
        vmem((rows, D), BF),
        vmem((rows, 3 * D), BF),
    ]


def shift_to(value, d_lon, d_lat):
    pairs = []
    for a in range(16):
        for b in range(8):
            pairs.append((a * 8 + b, ((a + d_lon) % 16) * 8 + (b + d_lat) % 8))
    return lax.ppermute(value, ALL, pairs)


def scatter_sum(blocks, axes, count, beside=None):
    here = lax.axis_index(axes)
    parts = [lax.dynamic_index_in_dim(blocks, here, 0, keepdims=False)]
    for step in range(1, count):
        block = lax.dynamic_index_in_dim(blocks, (here + step) % count, 0, keepdims=False)
        pairs = [(n, (n + step) % count) for n in range(count)]
        parts.append(lax.ppermute(block, axes, pairs))
    extra = None
    if beside is not None:
        extra = beside(blocks)
        *parts, extra = lax.optimization_barrier((*parts, extra))
    total = parts[0].astype(F32)
    for part in parts[1:]:
        total = total + part.astype(F32)
    return total, extra


def local(tokens, pad_mask, shifts, bias_table, rel_index, w_qkv, w_out, grad_out):
    both = lambda a, b: jnp.concatenate([tokens[a, b], grad_out[a, b]], axis=-1)
    halo_lat = shift_to(both(slice(None), slice(0, 8)), 0, -1)
    halo_lon = shift_to(both(slice(0, 8), slice(None)), -1, 0)
    halo_cor = shift_to(both(slice(0, 8), slice(0, 8)), -1, -1)
    inner, outer = 21 * CELLS, 12 * CELLS
    grid = sds((64, 32, D), BF)
    halos = (halo_lon, halo_lat, halo_cor)

    w_part, mix, dq, hid, istd, keys, bias = call(
        interior_kernel,
        [
            sds((D, 4 * D), F32),
            sds((inner, D), BF),
            sds((inner, 3 * D), BF),
            sds((inner, D), BF),
            sds((inner, 128), F32),
            sds((32, 128), F32),
            sds((64, 512), F32),
        ],
        window_scratch(64, 32, inner)
        + attend_scratch(inner)
        + [vmem((8, 256), F32), vmem((64, 128), jnp.int32), vmem((D, 4 * D), F32), pltpu.SemaphoreType.DMA((6,))],
        [IN_VMEM] * 7,
        [IN_HBM] * 5 + [IN_VMEM] * 2,
    )(shifts, tokens, grad_out, pad_mask, bias_table, rel_index, w_qkv, w_out)

    edge_lat, edge_lon, out_lat, out_lon, out_cor, w_mine, w_other = call(
        edge_kernel,
        [
            sds((2, 64, 8, D), BF),
            sds((2, 8, 32, D), BF),
            sds((64, 8, 2 * D), BF),
            sds((8, 32, 2 * D), BF),
            sds((8, 8, 2 * D), BF),
            sds((D // 2, 4 * D), BF),
            sds((D // 2, 4 * D), BF),
        ],
        window_scratch(72, 32, outer)
        + attend_scratch(outer)
        + [vmem((D, 4 * D), F32), pltpu.SemaphoreType.DMA],
        [IN_VMEM] * 9 + [IN_HBM],
        [IN_VMEM] * 7,
    )(shifts, tokens, grad_out, *halos, keys, bias, w_qkv, w_out, w_part)

    def grad_beside(blocks):
        _, rows = lax.optimization_barrier((blocks, dq))
        return call(grad_kernel, grid, [vmem((64, 32, D), F32)], [IN_VMEM] * 7, IN_VMEM)(
            shifts, grad_out, hid, istd, rows, w_qkv, edge_lat[1], edge_lon[1]
        )

    def updated_beside(blocks):
        _, rows = lax.optimization_barrier((blocks, mix))
        return call(updated_kernel, grid, [vmem((64, 32, D), F32)], [IN_VMEM] * 5, IN_VMEM)(
            shifts, tokens, rows, w_out, edge_lat[0], edge_lon[0]
        )

    w_got = lax.ppermute(w_other, "core", [(0, 1), (1, 0)])
    in_lat = shift_to(out_lat, 0, 1)
    in_lon = shift_to(out_lon, 1, 0)
    in_cor = shift_to(out_cor, 1, 1)
    total = (w_mine.astype(F32) + w_got.astype(F32)).astype(BF)
    total = total.reshape(2, 4, 32, 4 * D).transpose(1, 0, 2, 3)
    total, tokens_grad = scatter_sum(total, "x", 4, grad_beside)
    total = total.astype(BF).reshape(2, 4, 8, 4 * D).transpose(1, 0, 2, 3)
    total, updated = scatter_sum(total, "y", 4, updated_beside)
    total, _ = scatter_sum(total.astype(BF).reshape(4, 4, 4 * D), ("zh", "zl"), 4)

    updated, tokens_grad = call(
        return_kernel,
        [grid, grid],
        [vmem((2, 64, 16, D), BF), vmem((2, 8, 16, D), BF), pltpu.SemaphoreType.DMA((4,))],
        [IN_HBM] * 2 + [IN_VMEM] * 3,
        [IN_HBM] * 2,
        {1: 0, 2: 1},
    )(shifts, updated, tokens_grad, in_lat, in_lon, in_cor)
    return (updated, tokens_grad, total[:, : 3 * D], total[:, 3 * D :])


def solution(mesh):
    fine = Mesh(mesh.devices.reshape(2, 4, 2, 4, 2), ALL)
    in_specs = (P(LON, LAT, None), P(), P(), P(), P(), P(), P(), P(LON, LAT, None))
    out_specs = (P(LON, LAT, None), P(LON, LAT, None), P(ALL, None), P(ALL, None))
    return jax.shard_map(local, mesh=fine, in_specs=in_specs, out_specs=out_specs, check_vma=False)
```

```python
import jax
import jax.numpy as jnp
from jax import lax
from jax.experimental import pallas as pl
from jax.experimental.pallas import tpu as pltpu
from jax.sharding import Mesh, PartitionSpec as P

WIN = 8
CELLS = 64
D = 512
HEADS = 8
GROUP = 256
BF = jnp.bfloat16
F32 = jnp.float32
LOG2E = 1.4426950408889634
SCALE = 0.125
VMEM_LIMIT = 56 * 2**20
LON = ("zh", "x", "core")
LAT = ("y", "zl")
ALL = LON + LAT


def dot_nn(a, b):
    return lax.dot_general(a, b, (((1,), (0,)), ((), ())), preferred_element_type=F32)


def dot_nt(a, b):
    return lax.dot_general(a, b, (((1,), (1,)), ((), ())), preferred_element_type=F32)


def dot_tn(a, b):
    return lax.dot_general(a, b, (((0,), (0,)), ((), ())), preferred_element_type=F32)


def iota(shape, dim):
    return lax.broadcasted_iota(jnp.int32, shape, dim)


def keep_window(x, g, row, xt, xg, hid, istd):
    at = pl.ds(row, CELLS)
    center = x - jnp.mean(x, axis=-1, keepdims=True)
    inv = lax.rsqrt(jnp.mean(center * center, axis=-1, keepdims=True) + 1e-05)
    hid[at, :] = (center * inv).astype(BF)
    istd[at, :] = jnp.broadcast_to(inv, (CELLS, 128))
    xt[at, :] = x.astype(BF)
    xg[at, :] = g.astype(BF)


def project(rows, chunk, hid, xg, w_qkv, w_out, qkvg):
    def step(c, carry):
        at = pl.ds(pl.multiple_of(c * chunk, 64), chunk)
        qkvg[at, : 3 * D] = dot_nn(hid[at, :], w_qkv[...]).astype(BF)
        qkvg[at, 3 * D :] = dot_nt(xg[at, :], w_out[...]).astype(BF)
        return carry

    lax.fori_loop(0, rows // chunk, step, 0)


def fill_ones(ones):
    block = (iota((GROUP, GROUP), 0) >> 6) == (iota((GROUP, GROUP), 1) >> 6)
    ones[...] = jnp.where(block, 1.0, 0.0).astype(BF)


def attend(first, marks, thrs, bias, ones, qkvg, mix, dq):
    lane = iota((CELLS, 128), 1)
    cell = iota((CELLS, 128), 0)
    diag = (lane & 63) == cell
    low_half = lane < 64
    low_mask = jnp.where(low_half, 1.0, 0.0).astype(BF)
    high_mask = jnp.where(low_half, 0.0, 1.0).astype(BF)
    zero = jnp.zeros((CELLS, 128), BF)

    def by_head(x):
        a, b = x[:, :128], x[:, 128:]
        rows = [(a * low_mask, zero), (a * high_mask, zero), (zero, b * low_mask), (zero, b * high_mask)]
        return jnp.concatenate([jnp.concatenate(r, axis=1) for r in rows], axis=0)

    units = []
    for w, (mark, thr) in enumerate(zip(marks, thrs)):
        row = pl.multiple_of((first + w) * CELLS, CELLS)
        same = ((lane & 7) >= thr) == ((cell & 7) >= thr)
        valid = jnp.broadcast_to(mark, (CELLS, 128)) > 0.5
        ok = (valid & same) | diag
        ok = jnp.concatenate([ok, ok], axis=1)
        for h in range(2):
            c = h * GROUP
            at = pl.ds(row, CELLS)
            q = qkvg[at, c : c + GROUP]
            k = qkvg[at, D + c : D + c + GROUP]
            v = qkvg[at, 2 * D + c : 2 * D + c + GROUP]
            g = qkvg[at, 3 * D + c : 3 * D + c + GROUP]
            kbd, vbd = by_head(k), by_head(v)
            s = dot_nt(q, kbd)
            pg = dot_nt(g, vbd)
            e = jnp.where(ok, jnp.exp2(s * (SCALE * LOG2E) + bias[:, c : c + GROUP]), 0.0)
            units.append((at, c, q, g, kbd, vbd, e, pg))
    total = dot_nn(jnp.concatenate([u[6].astype(BF) for u in units], axis=0), ones[...])
    probs = []
    for n, u in enumerate(units):
        probs.append(u[6] / total[n * CELLS : (n + 1) * CELLS])
    dots = dot_nn(
        jnp.concatenate([(p * u[7]).astype(BF) for p, u in zip(probs, units)], axis=0), ones[...]
    )
    for n, (at, c, q, g, kbd, vbd, e, pg) in enumerate(units):
        p = probs[n]
        p_low = p.astype(BF)
        ds = (p * (pg - dots[n * CELLS : (n + 1) * CELLS]) * SCALE).astype(BF)
        mix[at, c : c + GROUP] = dot_nn(p_low, vbd).astype(BF)
        dq[at, c : c + GROUP] = dot_nn(ds, kbd).astype(BF)
        for t in range(2):
            lo, hi = t * 128, t * 128 + 128
            kg = dot_tn(ds[:, lo:hi], q[:, lo:hi])
            vg = dot_tn(p_low[:, lo:hi], g[:, lo:hi])
            dq[at, D + c + lo : D + c + hi] = jnp.where(low_half, kg[:64], kg[64:]).astype(BF)
            dq[at, 2 * D + c + lo : 2 * D + c + hi] = jnp.where(low_half, vg[:64], vg[64:]).astype(BF)


def finish(at, xt, xg, hid, istd, mix, dq, w_qkv, w_out):
    update = xt[at, :].astype(F32) + dot_nn(mix[at, :], w_out[...])
    normed_grad = dot_nt(dq[at, :], w_qkv[...])
    normed = hid[at, :].astype(F32)
    centred = normed_grad - jnp.mean(normed_grad, axis=-1, keepdims=True)
    centred = centred - normed * jnp.mean(normed_grad * normed, axis=-1, keepdims=True)
    inv = istd[at, :]
    return update, xg[at, :].astype(F32) + jnp.concatenate([inv] * 4, axis=1) * centred


def rows_of(strip):
    return strip.reshape(CELLS, D)


def strip_of(rows, count):
    parts = [rows[n * CELLS : (n + 1) * CELLS].reshape(WIN, WIN, D) for n in range(count)]
    return jnp.concatenate(parts + [jnp.zeros((WIN, WIN, D), F32)], axis=1)


def make_tables(marks_in, bias_table, rel_index, s0, s1, keys, bias, table, rel):
    rows = pltpu.roll(marks_in[...].astype(F32), 72 - s0, 0)[:64]
    lane = iota((256, 512), 1)
    place = (lax.axis_index(LAT) * 32 + s1 + (lane >> 7) * 8 + (lane & 7)) & 255
    pick = jnp.where(iota((256, 512), 0) == place, 1.0, 0.0).astype(BF)
    marks = dot_nn(rows.astype(BF), pick)
    own = (iota((64, 512), 0) & 7) == ((iota((64, 512), 1) & 63) >> 3)
    marks = jnp.sum(jnp.where(own, marks, 0.0).reshape(8, 8, 512), axis=1)
    for b in range(4):
        keys[8 * b : 8 * b + 8, :] = marks[:, 128 * b : 128 * b + 128]

    table[...] = jnp.zeros((8, 256), F32)
    table[:, :225] = bias_table[...] * LOG2E
    rel[:, :64] = rel_index[...]
    rel[:, 64:] = rel_index[...]
    at = rel[...]
    low = at < 128
    at = at & 127
    left = iota((CELLS, 128), 1) < 64
    for pair in range(4):
        found = []
        for h in (2 * pair, 2 * pair + 1):
            half = [
                jnp.take_along_axis(
                    jnp.broadcast_to(table[h : h + 1, c : c + 128], (CELLS, 128)), at, axis=1
                )
                for c in (0, 128)
            ]
            found.append(jnp.where(low, half[0], half[1]))
        bias[:, pair * 128 : pair * 128 + 128] = jnp.where(left, found[0], found[1])


def start_all(pairs, sems, first=0):
    copies = [pltpu.make_async_copy(a, b, sems.at[first + n]) for n, (a, b) in enumerate(pairs)]
    for copy in copies:
        copy.start()
    return copies


def wait_all(copies):
    for copy in copies:
        copy.wait()


def interior_kernel(
    shifts, tokens_in, grads_in, pad_in, bias_table, rel_index, w_qkv_in, w_out_in,
    updated_out, grad_out, w_part, keys, bias,
    tokens, grads, w_qkv, w_out, marks, updated, tokens_grad,
    xt, xg, hid, istd, qkvg, mix, dq, ones, table, rel, w_sum, sems,
):
    s0, s1 = shifts[0], shifts[1]
    base = lax.axis_index(LON) * 64
    mark_copies = start_all(
        [
            (pad_in.at[pl.ds(pl.multiple_of(base, 8), 64)], marks.at[0:64]),
            (pad_in.at[pl.ds(pl.multiple_of((base + 64) & 1023, 8), 8)], marks.at[64:72]),
        ],
        sems,
    )
    rows_in = start_all([(tokens_in, tokens), (grads_in, grads)], sems, 2)
    weights_in = start_all([(w_qkv_in, w_qkv), (w_out_in, w_out)], sems, 4)
    fill_ones(ones)
    wait_all(mark_copies)
    make_tables(marks, bias_table, rel_index, s0, s1, keys, bias, table, rel)
    wait_all(rows_in)

    def load(a, carry):
        at = pl.ds(s0 + a * WIN, WIN)
        x = pltpu.roll(tokens[at, :, :].astype(F32), 32 - s1, 1)
        g = pltpu.roll(grads[at, :, :].astype(F32), 32 - s1, 1)
        for b in range(3):
            row = pl.multiple_of((a * 3 + b) * CELLS, CELLS)
            c = slice(b * WIN, b * WIN + WIN)
            keep_window(rows_of(x[:, c]), rows_of(g[:, c]), row, xt, xg, hid, istd)
        return carry

    lax.fori_loop(0, 7, load, 0)
    wait_all(weights_in)
    project(21 * CELLS, 448, hid, xg, w_qkv, w_out, qkvg)

    def windows(a, carry):
        seen = [keys[pl.ds(8 * b + a, 1), :] for b in range(3)]
        attend(a * 3, seen, [8] * 3, bias, ones, qkvg, mix, dq)
        return carry

    lax.fori_loop(0, 7, windows, 0)
    copies = []
    for b in range(2):
        r = slice(b * 256, (b + 1) * 256)
        w_sum[r, : 3 * D] = dot_tn(hid[:, r], dq[...])
        w_sum[r, 3 * D :] = dot_tn(mix[:, r], xg[...])
        copies += start_all([(w_sum.at[r], w_part.at[r])], sems, b)

    def store(a, carry):
        at = pl.ds(pl.multiple_of(a * 192, 64), 192)
        to = pl.ds(s0 + a * WIN, WIN)
        for rows, out in zip(finish(at, xt, xg, hid, istd, mix, dq, w_qkv, w_out), (updated, tokens_grad)):
            out[to, :, :] = pltpu.roll(strip_of(rows, 3), s1, 1).astype(BF)
        return carry

    lax.fori_loop(0, 7, store, 0)
    copies += start_all([(updated, updated_out), (tokens_grad, grad_out)], sems, 2)
    wait_all(copies)


def edge_kernel(
    shifts, tokens_in, grads_in, halo_lon, halo_lat, halo_cor, keys, bias, w_qkv_in, w_out_in, w_part,
    lat_up, lon_up, lat_grad, lon_grad, out_lat, out_lon, out_cor, w_mine, w_other,
    tok, grad, far, low_tok, low_grad, low_far, w_qkv, w_out, to_lat, to_lon,
    xt, xg, hid, istd, qkvg, mix, dq, ones, w_sum, sems,
):
    s0, s1 = shifts[0], shifts[1]
    core = lax.axis_index("core")
    thr_edge = jnp.where(lax.axis_index(LAT) == 7, 8 - s1, 8)
    rows_in = start_all(
        [
            (tokens_in.at[:, 16:32, :], tok),
            (grads_in.at[:, 16:32, :], grad),
            (halo_lat, far),
            (tokens_in.at[56:64], low_tok.at[0:8]),
            (grads_in.at[56:64], low_grad.at[0:8]),
            (halo_lon.at[:, :, 0:D], low_tok.at[8:16]),
            (halo_lon.at[:, :, D : 2 * D], low_grad.at[8:16]),
            (halo_lat.at[56:64], low_far.at[0:8]),
            (halo_cor, low_far.at[8:16]),
        ],
        sems,
    )
    weights_in = start_all([(w_qkv_in, w_qkv), (w_out_in, w_out), (w_part, w_sum)], sems, 9)
    fill_ones(ones)
    tail = slice(11 * CELLS, 12 * CELLS)
    xg[tail, :] = jnp.zeros((CELLS, D), BF)
    hid[tail, :] = jnp.zeros((CELLS, D), BF)
    wait_all(rows_in)

    def load(a, carry):
        at = pl.ds(s0 + a * WIN, WIN)
        found = []
        for near, c in ((tok, 0), (grad, D)):
            rows = [near[at, 8:16, :].astype(F32), far[at, :, c : c + D].astype(F32)]
            found.append(rows_of(pltpu.roll(jnp.concatenate(rows, axis=1), 16 - s1, 1)[:, :8]))
        keep_window(*found, pl.multiple_of(a * CELLS, CELLS), xt, xg, hid, istd)
        return carry

    lax.fori_loop(0, 7, load, 0)
    at = pl.ds(s0, WIN)
    found = []
    for near, c in ((low_tok, 0), (low_grad, D)):
        rows = [near[at, :, :].astype(F32), low_far[at, :, c : c + D].astype(F32)]
        found.append(pltpu.roll(jnp.concatenate(rows, axis=1), 40 - s1, 1))
    for b in range(4):
        x, g = (rows_of(rows[:, b * WIN : b * WIN + WIN]) for rows in found)
        keep_window(x, g, (7 + b) * CELLS, xt, xg, hid, istd)
    wait_all(weights_in)
    project(12 * CELLS, 384, hid, xg, w_qkv, w_out, qkvg)

    def windows(a, carry):
        seen, thr = [], []
        for w in range(3):
            n = a * 3 + w
            row = jnp.where(n < 7, 24 + n, jnp.minimum(8 * n - 49, 31))
            seen.append(keys[pl.ds(row, 1), :])
            thr.append(jnp.where((n < 7) | (n == 10), thr_edge, 8))
        attend(a * 3, seen, thr, bias, ones, qkvg, mix, dq)
        return carry

    lax.fori_loop(0, 4, windows, 0)

    results = finish(slice(0, 7 * CELLS), xt, xg, hid, istd, mix, dq, w_qkv, w_out)
    for rows, near, c in zip(results, (tok, grad), (0, D)):
        for a in range(7):
            strip = strip_of(rows[a * CELLS : (a + 1) * CELLS], 1)
            strip = pltpu.roll(strip, s1, 1).astype(BF)
            near[pl.ds(s0 + a * WIN, WIN), 0:8, :] = strip[:, :8]
            to_lat[pl.ds(s0 + a * WIN, WIN), :, c : c + D] = strip[:, 8:]
    results = finish(slice(7 * CELLS, 11 * CELLS), xt, xg, hid, istd, mix, dq, w_qkv, w_out)
    for rows, low, c in zip(results, (low_tok, low_grad), (0, D)):
        strip = pltpu.roll(strip_of(rows, 4), s1, 1).astype(BF)
        low[pl.ds(s0, WIN), :, :] = strip[:, :32]
        to_lat[pl.ds(s0 + 56, WIN), :, c : c + D] = strip[:, 32:]
    to_lon[:, :, 0:D] = low_tok[8:16]
    to_lon[:, :, D : 2 * D] = low_grad[8:16]
    copies = start_all(
        [
            (tok, lat_up),
            (grad, lat_grad),
            (low_tok.at[0:8], lon_up),
            (low_grad.at[0:8], lon_grad),
            (to_lat.at[0:64], out_lat),
            (to_lat.at[64:72], out_cor),
            (to_lon, out_lon),
        ],
        sems,
    )
    for b in range(2):
        r = slice(b * 256, (b + 1) * 256)
        w_sum[r, : 3 * D] += dot_tn(hid[:, r], dq[...])
        w_sum[r, 3 * D :] += dot_tn(mix[:, r], xg[...])

    def split(n, carry):
        to = pl.ds(pl.multiple_of(n * 32, 32), 32)
        w_mine[to, :] = w_sum[pl.ds(pl.multiple_of((2 * n + core) * 32, 32), 32), :].astype(BF)
        w_other[to, :] = w_sum[pl.ds(pl.multiple_of((2 * n + 1 - core) * 32, 32), 32), :].astype(BF)
        return carry

    lax.fori_loop(0, 8, split, 0)
    wait_all(copies)


def edge_merge_kernel(
    shifts, updated, tokens_grad, lat_up, lon_up, lat_grad, lon_grad, out_updated, out_grad,
    side, low, sems,
):
    s0, s1 = shifts[0], shifts[1]
    pairs = []
    for n, out in enumerate((out_updated, out_grad)):
        pairs += [(out.at[:, 16:32, :], side.at[n]), (out.at[56:64, 0:16, :], low.at[n])]
    wait_all(start_all(pairs, sems))
    mark = iota((8, 8, D), 1) >= s1
    for n, (lat, lon) in enumerate(((lat_up, lon_up), (lat_grad, lon_grad))):

        def rest(r, carry, n=n, lat=lat):
            at = pl.ds(pl.multiple_of(r * 8, 8), 8)
            rows = side[n, at, 8:16, :].astype(F32)
            side[n, at, 8:16, :] = jnp.where(mark, lat[at, 0:8, :].astype(F32), rows).astype(BF)
            return carry

        lax.fori_loop(0, 8, rest, 0)
        later = iota((8, 16, D), 0) >= s0
        rows = side[n, 56:64, :, :].astype(F32)
        side[n, 56:64, :, :] = jnp.where(later, lon[:, 16:32, :].astype(F32), rows).astype(BF)
        later = later & (iota((8, 16, D), 1) >= s1)
        rows = low[n].astype(F32)
        low[n] = jnp.where(later, lon[:, 0:16, :].astype(F32), rows).astype(BF)
    wait_all(start_all([(b, a) for a, b in pairs], sems))


def return_kernel(
    shifts, updated, tokens_grad, in_lat, in_lon, in_cor, out_updated, out_grad, side, top, sems
):
    s0, s1 = shifts[0], shifts[1]
    outs = (out_updated, out_grad)
    into = []
    for n, out in enumerate(outs):
        into.append(pltpu.make_async_copy(out.at[:, 0:16, :], side.at[n], sems.at[2 * n]))
        into.append(pltpu.make_async_copy(out.at[0:8, 16:32, :], top.at[n], sems.at[2 * n + 1]))
    for copy in into:
        copy.start()
    for copy in into:
        copy.wait()
    lat = iota((8, 8, D), 1)
    lon = iota((8, 8, D), 0)
    pick = lambda mark, new, old: jnp.where(mark, new.astype(F32), old)
    for n in range(2):
        cols = slice(n * D, n * D + D)

        def rest(r, carry, n=n, cols=cols):
            at = pl.ds(pl.multiple_of(r * 8, 8), 8)
            rows = side[n, at, 0:8, :].astype(F32)
            side[n, at, 0:8, :] = pick(lat < s1, in_lat[at, :, cols], rows).astype(BF)
            return carry

        lax.fori_loop(1, 8, rest, 0)
        rows = side[n, 0:8, 0:8, :].astype(F32)
        rows = pick((lat < s1) & (lon >= s0), in_lat[0:8, :, cols], rows)
        rows = pick((lat >= s1) & (lon < s0), in_lon[:, 0:8, cols], rows)
        rows = pick((lat < s1) & (lon < s0), in_cor[:, :, cols], rows)
        side[n, 0:8, 0:8, :] = rows.astype(BF)
        rows = side[n, 0:8, 8:16, :].astype(F32)
        side[n, 0:8, 8:16, :] = pick(lon < s0, in_lon[:, 8:16, cols], rows).astype(BF)
        rows = top[n].astype(F32)
        top[n] = pick(iota((8, 16, D), 0) < s0, in_lon[:, 16:32, cols], rows).astype(BF)
    back = []
    for n, out in enumerate(outs):
        back.append(pltpu.make_async_copy(side.at[n], out.at[:, 0:16, :], sems.at[2 * n]))
        back.append(pltpu.make_async_copy(top.at[n], out.at[0:8, 16:32, :], sems.at[2 * n + 1]))
    for copy in back:
        copy.start()
    for copy in back:
        copy.wait()


def vmem(shape, dtype):
    return pltpu.VMEM(shape, dtype)


def sds(shape, dtype):
    return jax.ShapeDtypeStruct(shape, dtype)


IN_VMEM = pl.BlockSpec(memory_space=pltpu.VMEM)
IN_SMEM = pl.BlockSpec(memory_space=pltpu.SMEM)
IN_HBM = pl.BlockSpec(memory_space=pl.ANY)


def call(kernel, out_shape, scratch, in_specs, out_specs, aliases=None):
    return pl.pallas_call(
        kernel,
        out_shape=out_shape,
        in_specs=[IN_SMEM] + in_specs,
        out_specs=out_specs,
        scratch_shapes=scratch,
        input_output_aliases=aliases or {},
        compiler_params=pltpu.CompilerParams(vmem_limit_bytes=VMEM_LIMIT),
    )


def window_scratch(rows):
    return [vmem((rows, D), BF), vmem((rows, D), BF), vmem((rows, D), BF), vmem((rows, 128), F32)]


def attend_scratch(rows):
    return [
        vmem((rows, 4 * D), BF),
        vmem((rows, D), BF),
        vmem((rows, 3 * D), BF),
        vmem((GROUP, GROUP), BF),
    ]


def shift_to(value, d_lon, d_lat):
    pairs = []
    for a in range(16):
        for b in range(8):
            pairs.append((a * 8 + b, ((a + d_lon) % 16) * 8 + (b + d_lat) % 8))
    return lax.ppermute(value, ALL, pairs)


def scatter_sum(blocks, axes, count, beside=None):
    here = lax.axis_index(axes)
    parts = [lax.dynamic_index_in_dim(blocks, here, 0, keepdims=False)]
    for step in range(1, count):
        block = lax.dynamic_index_in_dim(blocks, (here + step) % count, 0, keepdims=False)
        pairs = [(n, (n + step) % count) for n in range(count)]
        parts.append(lax.ppermute(block, axes, pairs))
    extra = None
    if beside is not None:
        extra = beside(blocks)
        parts, extra = lax.optimization_barrier((parts, extra))
    total = parts[0].astype(F32)
    for part in parts[1:]:
        total = total + part.astype(F32)
    return total, extra


INNER, OUTER = 21 * CELLS, 12 * CELLS
GRID = sds((64, 32, D), BF)
DMA = pltpu.SemaphoreType.DMA


WEIGHTS = [vmem((D, 3 * D), BF), vmem((D, D), BF)]


def run_interior(*args):
    rows = vmem((64, 32, D), BF)
    return call(
        interior_kernel,
        [GRID, GRID, sds((D, 4 * D), F32), sds((32, 128), F32), sds((64, 512), F32)],
        [rows, rows, *WEIGHTS, vmem((72, 256), jnp.int32), rows, rows]
        + window_scratch(INNER)
        + attend_scratch(INNER)
        + [vmem((8, 256), F32), vmem((64, 128), jnp.int32), vmem((D, 4 * D), F32), DMA((6,))],
        [IN_HBM] * 3 + [IN_VMEM] * 2 + [IN_HBM] * 2,
        [IN_HBM] * 3 + [IN_VMEM] * 2,
    )(*args)


def run_edge(*args):
    lat, lon = (64, 16, D), (8, 32, D)
    far_lat, far_lon = (64, 8, 2 * D), (8, 32, 2 * D)
    return call(
        edge_kernel,
        [sds(shape, BF) for shape in (lat, lon, lat, lon, far_lat, far_lon, (8, 8, 2 * D))]
        + [sds((D // 2, 4 * D), BF)] * 2,
        [vmem(lat, BF), vmem(lat, BF), vmem(far_lat, BF)]
        + [vmem((16, 32, D), BF), vmem((16, 32, D), BF), vmem((16, 8, 2 * D), BF)]
        + WEIGHTS
        + [vmem((72, 8, 2 * D), BF), vmem(far_lon, BF)]
        + window_scratch(OUTER)
        + attend_scratch(OUTER)
        + [vmem((D, 4 * D), F32), DMA((12,))],
        [IN_HBM] * 5 + [IN_VMEM] * 2 + [IN_HBM] * 3,
        [IN_HBM] * 7 + [IN_VMEM] * 2,
    )(*args)


def run_edge_merge(*args):
    return call(
        edge_merge_kernel,
        [GRID, GRID],
        [vmem((2, 64, 16, D), BF), vmem((2, 8, 16, D), BF), DMA((4,))],
        [IN_HBM] * 2 + [IN_VMEM] * 4,
        [IN_HBM] * 2,
        {1: 0, 2: 1},
    )(*args)


def run_return(*args):
    return call(
        return_kernel,
        [GRID, GRID],
        [vmem((2, 64, 16, D), BF), vmem((2, 8, 16, D), BF), DMA((4,))],
        [IN_HBM] * 2 + [IN_VMEM] * 3,
        [IN_HBM] * 2,
        {1: 0, 2: 1},
    )(*args)


def local(tokens, pad_mask, shifts, bias_table, rel_index, w_qkv, w_out, grad_out):
    both = lambda a, b: jnp.concatenate([tokens[a, b], grad_out[a, b]], axis=-1)
    halo_lat = shift_to(both(slice(None), slice(0, 8)), 0, -1)
    halo_lon = shift_to(both(slice(0, 8), slice(None)), -1, 0)
    halo_cor = shift_to(both(slice(0, 8), slice(0, 8)), -1, -1)

    updated, tokens_grad, w_part, keys, bias = run_interior(
        shifts, tokens, grad_out, pad_mask, bias_table, rel_index, w_qkv, w_out
    )
    *edges, out_lat, out_lon, out_cor, w_mine, w_other = run_edge(
        shifts, tokens, grad_out, halo_lon, halo_lat, halo_cor, keys, bias, w_qkv, w_out, w_part
    )

    def merge_beside(blocks):
        _, *placed = lax.optimization_barrier((blocks, updated, tokens_grad))
        return run_edge_merge(shifts, *placed, *edges)

    w_got = lax.ppermute(w_other, "core", [(0, 1), (1, 0)])
    in_lat = shift_to(out_lat, 0, 1)
    in_lon = shift_to(out_lon, 1, 0)
    in_cor = shift_to(out_cor, 1, 1)
    total = (w_mine.astype(F32) + w_got.astype(F32)).astype(BF)
    total = total.reshape(2, 4, 32, 4 * D).transpose(1, 0, 2, 3)
    total, (updated, tokens_grad) = scatter_sum(total, "x", 4, merge_beside)
    total = total.astype(BF).reshape(2, 4, 8, 4 * D).transpose(1, 0, 2, 3)
    total, _ = scatter_sum(total, "y", 4)
    total, _ = scatter_sum(total.astype(BF).reshape(4, 4, 4 * D), ("zh", "zl"), 4)

    updated, tokens_grad = run_return(shifts, updated, tokens_grad, in_lat, in_lon, in_cor)
    return (updated, tokens_grad, total[:, : 3 * D], total[:, 3 * D :])


def solution(mesh):
    fine = Mesh(mesh.devices.reshape(2, 4, 2, 4, 2), ALL)
    in_specs = (P(LON, LAT, None), P(), P(), P(), P(), P(), P(), P(LON, LAT, None))
    out_specs = (P(LON, LAT, None), P(LON, LAT, None), P(ALL, None), P(ALL, None))
    return jax.shard_map(local, mesh=fine, in_specs=in_specs, out_specs=out_specs, check_vma=False)
```

```python
import jax
import jax.numpy as jnp
from jax import lax
from jax.experimental import pallas as pl
from jax.experimental.pallas import tpu as pltpu
from jax.sharding import Mesh, PartitionSpec as P

WIN = 8
CELLS = 64
D = 512
HEADS = 8
GROUP = 256
BF = jnp.bfloat16
F32 = jnp.float32
LOG2E = 1.4426950408889634
SCALE = 0.125
VMEM_LIMIT = 56 * 2**20
LON = ("zh", "x", "core")
LAT = ("y", "zl")
ALL = LON + LAT


def dot_nn(a, b):
    return lax.dot_general(a, b, (((1,), (0,)), ((), ())), preferred_element_type=F32)


def dot_nt(a, b):
    return lax.dot_general(a, b, (((1,), (1,)), ((), ())), preferred_element_type=F32)


def dot_tn(a, b):
    return lax.dot_general(a, b, (((0,), (0,)), ((), ())), preferred_element_type=F32)


def iota(shape, dim):
    return lax.broadcasted_iota(jnp.int32, shape, dim)


def keep_window(x, g, row, xt, xg, hid, istd):
    at = pl.ds(row, CELLS)
    center = x - jnp.mean(x, axis=-1, keepdims=True)
    inv = lax.rsqrt(jnp.mean(center * center, axis=-1, keepdims=True) + 1e-05)
    hid[at, :] = (center * inv).astype(BF)
    istd[at, :] = jnp.broadcast_to(inv, (CELLS, 128))
    xt[at, :] = x.astype(BF)
    xg[at, :] = g.astype(BF)


def project(rows, chunk, hid, xg, w_qkv, w_out, qkvg):
    def step(c, carry):
        at = pl.ds(pl.multiple_of(c * chunk, 64), chunk)
        qkvg[at, : 3 * D] = dot_nn(hid[at, :], w_qkv[...]).astype(BF)
        qkvg[at, 3 * D :] = dot_nt(xg[at, :], w_out[...]).astype(BF)
        return carry

    lax.fori_loop(0, rows // chunk, step, 0, unroll=True)


def fill_ones(ones):
    block = (iota((GROUP, GROUP), 0) >> 6) == (iota((GROUP, GROUP), 1) >> 6)
    ones[...] = jnp.where(block, 1.0, 0.0).astype(BF)


def attend(first, marks, thrs, bias, ones, qkvg, mix, dq):
    lane = iota((CELLS, 128), 1)
    cell = iota((CELLS, 128), 0)
    diag = (lane & 63) == cell
    low_half = lane < 64
    low_mask = jnp.where(low_half, 1.0, 0.0).astype(BF)
    high_mask = jnp.where(low_half, 0.0, 1.0).astype(BF)
    zero = jnp.zeros((CELLS, 128), BF)

    def by_head(x):
        a, b = x[:, :128], x[:, 128:]
        rows = [(a * low_mask, zero), (a * high_mask, zero), (zero, b * low_mask), (zero, b * high_mask)]
        return jnp.concatenate([jnp.concatenate(r, axis=1) for r in rows], axis=0)

    units = []
    for w, (mark, thr) in enumerate(zip(marks, thrs)):
        row = pl.multiple_of((first + w) * CELLS, CELLS)
        same = ((lane & 7) >= thr) == ((cell & 7) >= thr)
        valid = jnp.broadcast_to(mark, (CELLS, 128)) > 0.5
        ok = (valid & same) | diag
        ok = jnp.concatenate([ok, ok], axis=1)
        for h in range(2):
            c = h * GROUP
            at = pl.ds(row, CELLS)
            q = qkvg[at, c : c + GROUP]
            k = qkvg[at, D + c : D + c + GROUP]
            v = qkvg[at, 2 * D + c : 2 * D + c + GROUP]
            g = qkvg[at, 3 * D + c : 3 * D + c + GROUP]
            kbd, vbd = by_head(k), by_head(v)
            s = dot_nt(q, kbd)
            pg = dot_nt(g, vbd)
            e = jnp.where(ok, jnp.exp2(s * (SCALE * LOG2E) + bias[:, c : c + GROUP]), 0.0)
            units.append((at, c, q, g, kbd, vbd, e, pg))
    total = dot_nn(jnp.concatenate([u[6].astype(BF) for u in units], axis=0), ones[...])
    probs = []
    for n, u in enumerate(units):
        probs.append(u[6] / total[n * CELLS : (n + 1) * CELLS])
    dots = dot_nn(
        jnp.concatenate([(p * u[7]).astype(BF) for p, u in zip(probs, units)], axis=0), ones[...]
    )
    for n, (at, c, q, g, kbd, vbd, e, pg) in enumerate(units):
        p = probs[n]
        p_low = p.astype(BF)
        ds = (p * (pg - dots[n * CELLS : (n + 1) * CELLS]) * SCALE).astype(BF)
        mix[at, c : c + GROUP] = dot_nn(p_low, vbd).astype(BF)
        dq[at, c : c + GROUP] = dot_nn(ds, kbd).astype(BF)
        for t in range(2):
            lo, hi = t * 128, t * 128 + 128
            kg = dot_tn(ds[:, lo:hi], q[:, lo:hi])
            vg = dot_tn(p_low[:, lo:hi], g[:, lo:hi])
            dq[at, D + c + lo : D + c + hi] = jnp.where(low_half, kg[:64], kg[64:]).astype(BF)
            dq[at, 2 * D + c + lo : 2 * D + c + hi] = jnp.where(low_half, vg[:64], vg[64:]).astype(BF)


def finish(at, xt, xg, hid, istd, mix, dq, w_qkv, w_out):
    update = xt[at, :].astype(F32) + dot_nn(mix[at, :], w_out[...])
    normed_grad = dot_nt(dq[at, :], w_qkv[...])
    normed = hid[at, :].astype(F32)
    centred = normed_grad - jnp.mean(normed_grad, axis=-1, keepdims=True)
    centred = centred - normed * jnp.mean(normed_grad * normed, axis=-1, keepdims=True)
    inv = istd[at, :]
    return update, xg[at, :].astype(F32) + jnp.concatenate([inv] * 4, axis=1) * centred


def rows_of(strip):
    return strip.reshape(CELLS, D)


def strip_of(rows, count):
    parts = [rows[n * CELLS : (n + 1) * CELLS].reshape(WIN, WIN, D) for n in range(count)]
    return jnp.concatenate(parts + [jnp.zeros((WIN, WIN, D), F32)], axis=1)


def make_tables(marks_in, bias_table, rel_index, s0, s1, keys, bias, table, rel):
    rows = pltpu.roll(marks_in[...].astype(F32), 72 - s0, 0)[:64]
    lane = iota((256, 512), 1)
    place = (lax.axis_index(LAT) * 32 + s1 + (lane >> 7) * 8 + (lane & 7)) & 255
    pick = jnp.where(iota((256, 512), 0) == place, 1.0, 0.0).astype(BF)
    marks = dot_nn(rows.astype(BF), pick)
    own = (iota((64, 512), 0) & 7) == ((iota((64, 512), 1) & 63) >> 3)
    marks = jnp.sum(jnp.where(own, marks, 0.0).reshape(8, 8, 512), axis=1)
    for b in range(4):
        keys[8 * b : 8 * b + 8, :] = marks[:, 128 * b : 128 * b + 128]

    table[...] = jnp.zeros((8, 256), F32)
    table[:, :225] = bias_table[...] * LOG2E
    rel[:, :64] = rel_index[...]
    rel[:, 64:] = rel_index[...]
    at = rel[...]
    low = at < 128
    at = at & 127
    left = iota((CELLS, 128), 1) < 64
    for pair in range(4):
        found = []
        for h in (2 * pair, 2 * pair + 1):
            half = [
                jnp.take_along_axis(
                    jnp.broadcast_to(table[h : h + 1, c : c + 128], (CELLS, 128)), at, axis=1
                )
                for c in (0, 128)
            ]
            found.append(jnp.where(low, half[0], half[1]))
        bias[:, pair * 128 : pair * 128 + 128] = jnp.where(left, found[0], found[1])


def start_all(pairs, sems, first=0):
    copies = [pltpu.make_async_copy(a, b, sems.at[first + n]) for n, (a, b) in enumerate(pairs)]
    for copy in copies:
        copy.start()
    return copies


def wait_all(copies):
    for copy in copies:
        copy.wait()


def interior_kernel(
    shifts, tokens_in, grads_in, pad_in, bias_table, rel_index, w_qkv_in, w_out_in,
    updated_out, grad_out, w_part, keys, bias,
    tokens, grads, w_qkv, w_out, marks, updated, tokens_grad,
    xt, xg, hid, istd, qkvg, mix, dq, ones, table, rel, w_sum, sems,
):
    s0, s1 = shifts[0], shifts[1]
    base = lax.axis_index(LON) * 64
    mark_copies = start_all(
        [
            (pad_in.at[pl.ds(pl.multiple_of(base, 8), 64)], marks.at[0:64]),
            (pad_in.at[pl.ds(pl.multiple_of((base + 64) & 1023, 8), 8)], marks.at[64:72]),
        ],
        sems,
    )
    rows_in = start_all([(tokens_in, tokens), (grads_in, grads)], sems, 2)
    weights_in = start_all([(w_qkv_in, w_qkv), (w_out_in, w_out)], sems, 4)
    fill_ones(ones)
    wait_all(mark_copies)
    make_tables(marks, bias_table, rel_index, s0, s1, keys, bias, table, rel)
    wait_all(rows_in)

    def load(a, carry):
        at = pl.ds(s0 + a * WIN, WIN)
        x = pltpu.roll(tokens[at, :, :].astype(F32), 32 - s1, 1)
        g = pltpu.roll(grads[at, :, :].astype(F32), 32 - s1, 1)
        for b in range(3):
            row = pl.multiple_of((a * 3 + b) * CELLS, CELLS)
            c = slice(b * WIN, b * WIN + WIN)
            keep_window(rows_of(x[:, c]), rows_of(g[:, c]), row, xt, xg, hid, istd)
        return carry

    lax.fori_loop(0, 7, load, 0, unroll=True)
    wait_all(weights_in)
    project(21 * CELLS, 448, hid, xg, w_qkv, w_out, qkvg)

    def windows(a, carry):
        seen = [keys[pl.ds(8 * b + a, 1), :] for b in range(3)]
        attend(a * 3, seen, [8] * 3, bias, ones, qkvg, mix, dq)
        return carry

    lax.fori_loop(0, 7, windows, 0, unroll=True)
    copies = []
    for b in range(2):
        r = slice(b * 256, (b + 1) * 256)
        w_sum[r, : 3 * D] = dot_tn(hid[:, r], dq[...])
        w_sum[r, 3 * D :] = dot_tn(mix[:, r], xg[...])
        copies += start_all([(w_sum.at[r], w_part.at[r])], sems, b)

    def store(a, carry):
        at = pl.ds(pl.multiple_of(a * 192, 64), 192)
        to = pl.ds(s0 + a * WIN, WIN)
        for rows, out in zip(finish(at, xt, xg, hid, istd, mix, dq, w_qkv, w_out), (updated, tokens_grad)):
            out[to, :, :] = pltpu.roll(strip_of(rows, 3), s1, 1).astype(BF)
        return carry

    lax.fori_loop(0, 7, store, 0, unroll=True)
    copies += start_all([(updated, updated_out), (tokens_grad, grad_out)], sems, 2)
    wait_all(copies)


def edge_kernel(
    shifts, tokens_in, grads_in, halo_lon, halo_lat, halo_cor, keys, bias, w_qkv_in, w_out_in, w_part,
    lat_up, lon_up, lat_grad, lon_grad, out_lat, out_lon, out_cor, w_mine, w_other,
    tok, grad, far, low_tok, low_grad, low_far, w_qkv, w_out, to_lat, to_lon,
    xt, xg, hid, istd, qkvg, mix, dq, ones, w_sum, sems,
):
    s0, s1 = shifts[0], shifts[1]
    core = lax.axis_index("core")
    thr_edge = jnp.where(lax.axis_index(LAT) == 7, 8 - s1, 8)
    rows_in = start_all(
        [
            (tokens_in.at[:, 16:32, :], tok),
            (grads_in.at[:, 16:32, :], grad),
            (halo_lat, far),
            (tokens_in.at[56:64], low_tok.at[0:8]),
            (grads_in.at[56:64], low_grad.at[0:8]),
            (halo_lon.at[:, :, 0:D], low_tok.at[8:16]),
            (halo_lon.at[:, :, D : 2 * D], low_grad.at[8:16]),
            (halo_lat.at[56:64], low_far.at[0:8]),
            (halo_cor, low_far.at[8:16]),
        ],
        sems,
    )
    weights_in = start_all([(w_qkv_in, w_qkv), (w_out_in, w_out), (w_part, w_sum)], sems, 9)
    fill_ones(ones)
    tail = slice(11 * CELLS, 12 * CELLS)
    xg[tail, :] = jnp.zeros((CELLS, D), BF)
    hid[tail, :] = jnp.zeros((CELLS, D), BF)
    wait_all(rows_in)

    def load(a, carry):
        at = pl.ds(s0 + a * WIN, WIN)
        found = []
        for near, c in ((tok, 0), (grad, D)):
            rows = [near[at, 8:16, :].astype(F32), far[at, :, c : c + D].astype(F32)]
            found.append(rows_of(pltpu.roll(jnp.concatenate(rows, axis=1), 16 - s1, 1)[:, :8]))
        keep_window(*found, pl.multiple_of(a * CELLS, CELLS), xt, xg, hid, istd)
        return carry

    lax.fori_loop(0, 7, load, 0, unroll=True)
    at = pl.ds(s0, WIN)
    found = []
    for near, c in ((low_tok, 0), (low_grad, D)):
        rows = [near[at, :, :].astype(F32), low_far[at, :, c : c + D].astype(F32)]
        found.append(pltpu.roll(jnp.concatenate(rows, axis=1), 40 - s1, 1))
    for b in range(4):
        x, g = (rows_of(rows[:, b * WIN : b * WIN + WIN]) for rows in found)
        keep_window(x, g, (7 + b) * CELLS, xt, xg, hid, istd)
    wait_all(weights_in)
    project(12 * CELLS, 384, hid, xg, w_qkv, w_out, qkvg)

    def windows(a, carry):
        seen, thr = [], []
        for w in range(3):
            n = a * 3 + w
            row = jnp.where(n < 7, 24 + n, jnp.minimum(8 * n - 49, 31))
            seen.append(keys[pl.ds(row, 1), :])
            thr.append(jnp.where((n < 7) | (n == 10), thr_edge, 8))
        attend(a * 3, seen, thr, bias, ones, qkvg, mix, dq)
        return carry

    lax.fori_loop(0, 4, windows, 0, unroll=True)

    results = finish(slice(0, 7 * CELLS), xt, xg, hid, istd, mix, dq, w_qkv, w_out)
    for rows, near, c in zip(results, (tok, grad), (0, D)):
        for a in range(7):
            strip = strip_of(rows[a * CELLS : (a + 1) * CELLS], 1)
            strip = pltpu.roll(strip, s1, 1).astype(BF)
            near[pl.ds(s0 + a * WIN, WIN), 0:8, :] = strip[:, :8]
            to_lat[pl.ds(s0 + a * WIN, WIN), :, c : c + D] = strip[:, 8:]
    results = finish(slice(7 * CELLS, 11 * CELLS), xt, xg, hid, istd, mix, dq, w_qkv, w_out)
    for rows, low, c in zip(results, (low_tok, low_grad), (0, D)):
        strip = pltpu.roll(strip_of(rows, 4), s1, 1).astype(BF)
        low[pl.ds(s0, WIN), :, :] = strip[:, :32]
        to_lat[pl.ds(s0 + 56, WIN), :, c : c + D] = strip[:, 32:]
    to_lon[:, :, 0:D] = low_tok[8:16]
    to_lon[:, :, D : 2 * D] = low_grad[8:16]
    copies = start_all(
        [
            (tok, lat_up),
            (grad, lat_grad),
            (low_tok.at[0:8], lon_up),
            (low_grad.at[0:8], lon_grad),
            (to_lat.at[0:64], out_lat),
            (to_lat.at[64:72], out_cor),
            (to_lon, out_lon),
        ],
        sems,
    )
    for b in range(2):
        r = slice(b * 256, (b + 1) * 256)
        w_sum[r, : 3 * D] += dot_tn(hid[:, r], dq[...])
        w_sum[r, 3 * D :] += dot_tn(mix[:, r], xg[...])

    def split(n, carry):
        to = pl.ds(pl.multiple_of(n * 32, 32), 32)
        w_mine[to, :] = w_sum[pl.ds(pl.multiple_of((2 * n + core) * 32, 32), 32), :].astype(BF)
        w_other[to, :] = w_sum[pl.ds(pl.multiple_of((2 * n + 1 - core) * 32, 32), 32), :].astype(BF)
        return carry

    lax.fori_loop(0, 8, split, 0)
    wait_all(copies)


def edge_merge_kernel(
    shifts, updated, tokens_grad, lat_up, lon_up, lat_grad, lon_grad, out_updated, out_grad,
    side, low, sems,
):
    s0, s1 = shifts[0], shifts[1]
    pairs = []
    for n, out in enumerate((out_updated, out_grad)):
        pairs += [(out.at[:, 16:32, :], side.at[n]), (out.at[56:64, 0:16, :], low.at[n])]
    wait_all(start_all(pairs, sems))
    mark = iota((8, 8, D), 1) >= s1
    for n, (lat, lon) in enumerate(((lat_up, lon_up), (lat_grad, lon_grad))):

        def rest(r, carry, n=n, lat=lat):
            at = pl.ds(pl.multiple_of(r * 8, 8), 8)
            rows = side[n, at, 8:16, :].astype(F32)
            side[n, at, 8:16, :] = jnp.where(mark, lat[at, 0:8, :].astype(F32), rows).astype(BF)
            return carry

        lax.fori_loop(0, 8, rest, 0)
        later = iota((8, 16, D), 0) >= s0
        rows = side[n, 56:64, :, :].astype(F32)
        side[n, 56:64, :, :] = jnp.where(later, lon[:, 16:32, :].astype(F32), rows).astype(BF)
        later = later & (iota((8, 16, D), 1) >= s1)
        rows = low[n].astype(F32)
        low[n] = jnp.where(later, lon[:, 0:16, :].astype(F32), rows).astype(BF)
    wait_all(start_all([(b, a) for a, b in pairs], sems))


def lat_return_kernel(shifts, updated, tokens_grad, in_lat, out_updated, out_grad, side, sems):
    s1 = shifts[1]
    pairs = [(out.at[:, 0:16, :], side.at[n]) for n, out in enumerate((out_updated, out_grad))]
    wait_all(start_all(pairs, sems))
    mark = iota((8, 8, D), 1) < s1
    for n in range(2):

        def place(r, carry, n=n):
            at = pl.ds(pl.multiple_of(r * 8, 8), 8)
            rows = side[n, at, 0:8, :].astype(F32)
            came = in_lat[at, :, n * D : n * D + D].astype(F32)
            side[n, at, 0:8, :] = jnp.where(mark, came, rows).astype(BF)
            return carry

        lax.fori_loop(0, 8, place, 0)
    wait_all(start_all([(b, a) for a, b in pairs], sems))


def lon_return_kernel(shifts, updated, tokens_grad, in_lon, in_cor, out_updated, out_grad, top, sems):
    s0, s1 = shifts[0], shifts[1]
    pairs = [(out.at[0:8], top.at[n]) for n, out in enumerate((out_updated, out_grad))]
    wait_all(start_all(pairs, sems))
    early = iota((8, 32, D), 0) < s0
    first = iota((8, 8, D), 1) < s1
    for n in range(2):
        cols = slice(n * D, n * D + D)
        came = in_lon[:, :, cols].astype(F32)
        corner = jnp.where(first, in_cor[:, :, cols].astype(F32), came[:, 0:8])
        came = jnp.concatenate([corner, came[:, 8:]], axis=1)
        top[n] = jnp.where(early, came, top[n].astype(F32)).astype(BF)
    wait_all(start_all([(b, a) for a, b in pairs], sems))


def vmem(shape, dtype):
    return pltpu.VMEM(shape, dtype)


def sds(shape, dtype):
    return jax.ShapeDtypeStruct(shape, dtype)


IN_VMEM = pl.BlockSpec(memory_space=pltpu.VMEM)
IN_SMEM = pl.BlockSpec(memory_space=pltpu.SMEM)
IN_HBM = pl.BlockSpec(memory_space=pl.ANY)


def call(kernel, out_shape, scratch, in_specs, out_specs, aliases=None):
    return pl.pallas_call(
        kernel,
        out_shape=out_shape,
        in_specs=[IN_SMEM] + in_specs,
        out_specs=out_specs,
        scratch_shapes=scratch,
        input_output_aliases=aliases or {},
        compiler_params=pltpu.CompilerParams(vmem_limit_bytes=VMEM_LIMIT),
    )


def window_scratch(rows):
    return [vmem((rows, D), BF), vmem((rows, D), BF), vmem((rows, D), BF), vmem((rows, 128), F32)]


def attend_scratch(rows):
    return [
        vmem((rows, 4 * D), BF),
        vmem((rows, D), BF),
        vmem((rows, 3 * D), BF),
        vmem((GROUP, GROUP), BF),
    ]


def shift_to(value, d_lon, d_lat):
    pairs = []
    for a in range(16):
        for b in range(8):
            pairs.append((a * 8 + b, ((a + d_lon) % 16) * 8 + (b + d_lat) % 8))
    return lax.ppermute(value, ALL, pairs)


def scatter_sum(blocks, axes, count, beside=None):
    here = lax.axis_index(axes)
    parts = [lax.dynamic_index_in_dim(blocks, here, 0, keepdims=False)]
    for step in range(1, count):
        block = lax.dynamic_index_in_dim(blocks, (here + step) % count, 0, keepdims=False)
        pairs = [(n, (n + step) % count) for n in range(count)]
        parts.append(lax.ppermute(block, axes, pairs))
    extra = None
    if beside is not None:
        extra = beside(blocks)
        parts, extra = lax.optimization_barrier((parts, extra))
    total = parts[0].astype(F32)
    for part in parts[1:]:
        total = total + part.astype(F32)
    return total, extra


INNER, OUTER = 21 * CELLS, 12 * CELLS
GRID = sds((64, 32, D), BF)
DMA = pltpu.SemaphoreType.DMA


WEIGHTS = [vmem((D, 3 * D), BF), vmem((D, D), BF)]


def run_interior(*args):
    rows = vmem((64, 32, D), BF)
    return call(
        interior_kernel,
        [GRID, GRID, sds((D, 4 * D), F32), sds((32, 128), F32), sds((64, 512), F32)],
        [rows, rows, *WEIGHTS, vmem((72, 256), jnp.int32), rows, rows]
        + window_scratch(INNER)
        + attend_scratch(INNER)
        + [vmem((8, 256), F32), vmem((64, 128), jnp.int32), vmem((D, 4 * D), F32), DMA((6,))],
        [IN_HBM] * 3 + [IN_VMEM] * 2 + [IN_HBM] * 2,
        [IN_HBM] * 3 + [IN_VMEM] * 2,
    )(*args)


def run_edge(*args):
    lat, lon = (64, 16, D), (8, 32, D)
    far_lat, far_lon = (64, 8, 2 * D), (8, 32, 2 * D)
    return call(
        edge_kernel,
        [sds(shape, BF) for shape in (lat, lon, lat, lon, far_lat, far_lon, (8, 8, 2 * D))]
        + [sds((D // 2, 4 * D), BF)] * 2,
        [vmem(lat, BF), vmem(lat, BF), vmem(far_lat, BF)]
        + [vmem((16, 32, D), BF), vmem((16, 32, D), BF), vmem((16, 8, 2 * D), BF)]
        + WEIGHTS
        + [vmem((72, 8, 2 * D), BF), vmem(far_lon, BF)]
        + window_scratch(OUTER)
        + attend_scratch(OUTER)
        + [vmem((D, 4 * D), F32), DMA((12,))],
        [IN_HBM] * 5 + [IN_VMEM] * 2 + [IN_HBM] * 3,
        [IN_HBM] * 7 + [IN_VMEM] * 2,
    )(*args)


def run_edge_merge(*args):
    return call(
        edge_merge_kernel,
        [GRID, GRID],
        [vmem((2, 64, 16, D), BF), vmem((2, 8, 16, D), BF), DMA((4,))],
        [IN_HBM] * 2 + [IN_VMEM] * 4,
        [IN_HBM] * 2,
        {1: 0, 2: 1},
    )(*args)


def run_lat_return(*args):
    return call(
        lat_return_kernel,
        [GRID, GRID],
        [vmem((2, 64, 16, D), BF), DMA((2,))],
        [IN_HBM] * 2 + [IN_VMEM],
        [IN_HBM] * 2,
        {1: 0, 2: 1},
    )(*args)


def run_lon_return(*args):
    return call(
        lon_return_kernel,
        [GRID, GRID],
        [vmem((2, 8, 32, D), BF), DMA((2,))],
        [IN_HBM] * 2 + [IN_VMEM] * 2,
        [IN_HBM] * 2,
        {1: 0, 2: 1},
    )(*args)


def local(tokens, pad_mask, shifts, bias_table, rel_index, w_qkv, w_out, grad_out):
    both = lambda a, b: jnp.concatenate([tokens[a, b], grad_out[a, b]], axis=-1)
    halo_lat = shift_to(both(slice(None), slice(0, 8)), 0, -1)
    halo_lon = shift_to(both(slice(0, 8), slice(None)), -1, 0)
    halo_cor = shift_to(both(slice(0, 8), slice(0, 8)), -1, -1)

    updated, tokens_grad, w_part, keys, bias = run_interior(
        shifts, tokens, grad_out, pad_mask, bias_table, rel_index, w_qkv, w_out
    )
    *edges, out_lat, out_lon, out_cor, w_mine, w_other = run_edge(
        shifts, tokens, grad_out, halo_lon, halo_lat, halo_cor, keys, bias, w_qkv, w_out, w_part
    )

    def merge_beside(blocks):
        _, *placed = lax.optimization_barrier((blocks, updated, tokens_grad))
        return run_edge_merge(shifts, *placed, *edges)

    w_got = lax.ppermute(w_other, "core", [(0, 1), (1, 0)])
    in_lat = shift_to(out_lat, 0, 1)
    in_lon = shift_to(out_lon, 1, 0)
    in_cor = shift_to(out_cor, 1, 1)
    total = (w_mine.astype(F32) + w_got.astype(F32)).astype(BF)
    total = total.reshape(2, 4, 32, 4 * D).transpose(1, 0, 2, 3)
    total, (updated, tokens_grad) = scatter_sum(total, "x", 4, merge_beside)
    total = total.astype(BF).reshape(2, 4, 8, 4 * D).transpose(1, 0, 2, 3)
    lat_beside = lambda blocks: run_lat_return(shifts, updated, tokens_grad, in_lat)
    total, (updated, tokens_grad) = scatter_sum(total, "y", 4, lat_beside)
    total, _ = scatter_sum(total.astype(BF).reshape(4, 4, 4 * D), ("zh", "zl"), 4)

    updated, tokens_grad = run_lon_return(shifts, updated, tokens_grad, in_lon, in_cor)
    return (updated, tokens_grad, total[:, : 3 * D], total[:, 3 * D :])


def solution(mesh):
    fine = Mesh(mesh.devices.reshape(2, 4, 2, 4, 2), ALL)
    in_specs = (P(LON, LAT, None), P(), P(), P(), P(), P(), P(), P(LON, LAT, None))
    out_specs = (P(LON, LAT, None), P(LON, LAT, None), P(ALL, None), P(ALL, None))
    return jax.shard_map(local, mesh=fine, in_specs=in_specs, out_specs=out_specs, check_vma=False)
```

```python
import jax
import jax.numpy as jnp
from jax import lax
from jax.experimental import pallas as pl
from jax.experimental.pallas import tpu as pltpu
from jax.sharding import Mesh, PartitionSpec as P

WIN = 8
CELLS = 64
D = 512
HEADS = 8
GROUP = 256
BF = jnp.bfloat16
F32 = jnp.float32
LOG2E = 1.4426950408889634
SCALE = 0.125
VMEM_LIMIT = 56 * 2**20
LON = ("zh", "x", "core")
LAT = ("y", "zl")
ALL = LON + LAT


def dot_nn(a, b):
    return lax.dot_general(a, b, (((1,), (0,)), ((), ())), preferred_element_type=F32)


def dot_nt(a, b):
    return lax.dot_general(a, b, (((1,), (1,)), ((), ())), preferred_element_type=F32)


def dot_tn(a, b):
    return lax.dot_general(a, b, (((0,), (0,)), ((), ())), preferred_element_type=F32)


def iota(shape, dim):
    return lax.broadcasted_iota(jnp.int32, shape, dim)


def keep_window(x, g, row, xt, xg, hid, istd):
    at = pl.ds(row, CELLS)
    center = x - jnp.mean(x, axis=-1, keepdims=True)
    inv = lax.rsqrt(jnp.mean(center * center, axis=-1, keepdims=True) + 1e-05)
    hid[at, :] = (center * inv).astype(BF)
    istd[at, :] = jnp.broadcast_to(inv, (CELLS, 128))
    xt[at, :] = x.astype(BF)
    xg[at, :] = g.astype(BF)


def project_rows(first, count, hid, xg, w_qkv, w_out, qkvg):
    at = pl.ds(first, count)
    qkvg[at, : 3 * D] = dot_nn(hid[at, :], w_qkv[...]).astype(BF)
    qkvg[at, 3 * D :] = dot_nt(xg[at, :], w_out[...]).astype(BF)


def project(rows, chunk, hid, xg, w_qkv, w_out, qkvg):
    def step(c, carry):
        project_rows(pl.multiple_of(c * chunk, 64), chunk, hid, xg, w_qkv, w_out, qkvg)
        return carry

    lax.fori_loop(0, rows // chunk, step, 0)


def fill_ones(ones):
    block = (iota((GROUP, GROUP), 0) >> 6) == (iota((GROUP, GROUP), 1) >> 6)
    ones[...] = jnp.where(block, 1.0, 0.0).astype(BF)


def attend(first, marks, thrs, bias, ones, qkvg, mix, dq):
    lane = iota((CELLS, 128), 1)
    cell = iota((CELLS, 128), 0)
    diag = (lane & 63) == cell
    low_half = lane < 64
    low_mask = jnp.where(low_half, 1.0, 0.0).astype(BF)
    high_mask = jnp.where(low_half, 0.0, 1.0).astype(BF)
    zero = jnp.zeros((CELLS, 128), BF)

    def by_head(x):
        a, b = x[:, :128], x[:, 128:]
        rows = [(a * low_mask, zero), (a * high_mask, zero), (zero, b * low_mask), (zero, b * high_mask)]
        return jnp.concatenate([jnp.concatenate(r, axis=1) for r in rows], axis=0)

    units = []
    for w, (mark, thr) in enumerate(zip(marks, thrs)):
        row = pl.multiple_of((first + w) * CELLS, CELLS)
        same = ((lane & 7) >= thr) == ((cell & 7) >= thr)
        valid = jnp.broadcast_to(mark, (CELLS, 128)) > 0.5
        ok = (valid & same) | diag
        ok = jnp.concatenate([ok, ok], axis=1)
        for h in range(2):
            c = h * GROUP
            at = pl.ds(row, CELLS)
            q = qkvg[at, c : c + GROUP]
            k = qkvg[at, D + c : D + c + GROUP]
            v = qkvg[at, 2 * D + c : 2 * D + c + GROUP]
            g = qkvg[at, 3 * D + c : 3 * D + c + GROUP]
            kbd, vbd = by_head(k), by_head(v)
            s = dot_nt(q, kbd)
            pg = dot_nt(g, vbd)
            e = jnp.where(ok, jnp.exp2(s * (SCALE * LOG2E) + bias[:, c : c + GROUP]), 0.0)
            units.append((at, c, q, g, kbd, vbd, e, pg))
    total = dot_nn(jnp.concatenate([u[6].astype(BF) for u in units], axis=0), ones[...])
    probs = []
    for n, u in enumerate(units):
        probs.append(u[6] / total[n * CELLS : (n + 1) * CELLS])
    dots = dot_nn(
        jnp.concatenate([(p * u[7]).astype(BF) for p, u in zip(probs, units)], axis=0), ones[...]
    )
    for n, (at, c, q, g, kbd, vbd, e, pg) in enumerate(units):
        p = probs[n]
        p_low = p.astype(BF)
        ds = (p * (pg - dots[n * CELLS : (n + 1) * CELLS]) * SCALE).astype(BF)
        mix[at, c : c + GROUP] = dot_nn(p_low, vbd).astype(BF)
        dq[at, c : c + GROUP] = dot_nn(ds, kbd).astype(BF)
        for t in range(2):
            lo, hi = t * 128, t * 128 + 128
            kg = dot_tn(ds[:, lo:hi], q[:, lo:hi])
            vg = dot_tn(p_low[:, lo:hi], g[:, lo:hi])
            dq[at, D + c + lo : D + c + hi] = jnp.where(low_half, kg[:64], kg[64:]).astype(BF)
            dq[at, 2 * D + c + lo : 2 * D + c + hi] = jnp.where(low_half, vg[:64], vg[64:]).astype(BF)


def finish(at, xt, xg, hid, istd, mix, dq, w_qkv, w_out):
    update = xt[at, :].astype(F32) + dot_nn(mix[at, :], w_out[...])
    normed_grad = dot_nt(dq[at, :], w_qkv[...])
    normed = hid[at, :].astype(F32)
    centred = normed_grad - jnp.mean(normed_grad, axis=-1, keepdims=True)
    centred = centred - normed * jnp.mean(normed_grad * normed, axis=-1, keepdims=True)
    inv = istd[at, :]
    return update, xg[at, :].astype(F32) + jnp.concatenate([inv] * 4, axis=1) * centred


def rows_of(strip):
    return strip.reshape(CELLS, D)


def strip_of(rows, count):
    parts = [rows[n * CELLS : (n + 1) * CELLS].reshape(WIN, WIN, D) for n in range(count)]
    return jnp.concatenate(parts + [jnp.zeros((WIN, WIN, D), F32)], axis=1)


def make_tables(marks_in, bias_table, rel_index, s0, s1, keys, bias, table, rel):
    rows = pltpu.roll(marks_in[...].astype(F32), 72 - s0, 0)[:64]
    lane = iota((256, 512), 1)
    place = (lax.axis_index(LAT) * 32 + s1 + (lane >> 7) * 8 + (lane & 7)) & 255
    pick = jnp.where(iota((256, 512), 0) == place, 1.0, 0.0).astype(BF)
    marks = dot_nn(rows.astype(BF), pick)
    own = (iota((64, 512), 0) & 7) == ((iota((64, 512), 1) & 63) >> 3)
    marks = jnp.sum(jnp.where(own, marks, 0.0).reshape(8, 8, 512), axis=1)
    for b in range(4):
        keys[8 * b : 8 * b + 8, :] = marks[:, 128 * b : 128 * b + 128]

    table[...] = jnp.zeros((8, 256), F32)
    table[:, :225] = bias_table[...] * LOG2E
    rel[:, :64] = rel_index[...]
    rel[:, 64:] = rel_index[...]
    at = rel[...]
    low = at < 128
    at = at & 127
    left = iota((CELLS, 128), 1) < 64
    for pair in range(4):
        found = []
        for h in (2 * pair, 2 * pair + 1):
            half = [
                jnp.take_along_axis(
                    jnp.broadcast_to(table[h : h + 1, c : c + 128], (CELLS, 128)), at, axis=1
                )
                for c in (0, 128)
            ]
            found.append(jnp.where(low, half[0], half[1]))
        bias[:, pair * 128 : pair * 128 + 128] = jnp.where(left, found[0], found[1])


def start_all(pairs, sems, first=0):
    copies = [pltpu.make_async_copy(a, b, sems.at[first + n]) for n, (a, b) in enumerate(pairs)]
    for copy in copies:
        copy.start()
    return copies


def wait_all(copies):
    for copy in copies:
        copy.wait()


def interior_kernel(
    shifts, tokens_in, grads_in, pad_in, bias_table, rel_index, w_qkv_in, w_out_in,
    updated_out, grad_out, w_part, keys, bias,
    tokens, grads, w_qkv, w_out, marks, updated, tokens_grad,
    xt, xg, hid, istd, qkvg, mix, dq, ones, table, rel, w_sum, sems,
):
    s0, s1 = shifts[0], shifts[1]
    base = lax.axis_index(LON) * 64
    mark_copies = start_all(
        [
            (pad_in.at[pl.ds(pl.multiple_of(base, 8), 64)], marks.at[0:64]),
            (pad_in.at[pl.ds(pl.multiple_of((base + 64) & 1023, 8), 8)], marks.at[64:72]),
        ],
        sems,
    )
    rows_in = start_all([(tokens_in, tokens), (grads_in, grads)], sems, 2)
    weights_in = start_all([(w_qkv_in, w_qkv), (w_out_in, w_out)], sems, 4)
    fill_ones(ones)
    wait_all(mark_copies)
    make_tables(marks, bias_table, rel_index, s0, s1, keys, bias, table, rel)
    wait_all(rows_in)

    def load(a, carry):
        at = pl.ds(s0 + a * WIN, WIN)
        x = pltpu.roll(tokens[at, :, :].astype(F32), 32 - s1, 1)
        g = pltpu.roll(grads[at, :, :].astype(F32), 32 - s1, 1)
        for b in range(3):
            row = pl.multiple_of((a * 3 + b) * CELLS, CELLS)
            c = slice(b * WIN, b * WIN + WIN)
            keep_window(rows_of(x[:, c]), rows_of(g[:, c]), row, xt, xg, hid, istd)
        return carry

    lax.fori_loop(0, 7, load, 0)
    wait_all(weights_in)
    project(21 * CELLS, 448, hid, xg, w_qkv, w_out, qkvg)

    def windows(a):
        seen = [keys[pl.ds(8 * b + a, 1), :] for b in range(3)]
        attend(a * 3, seen, [8] * 3, bias, ones, qkvg, mix, dq)

    def store(a):
        at = pl.ds(pl.multiple_of(a * 192, 64), 192)
        to = pl.ds(s0 + a * WIN, WIN)
        for rows, out in zip(finish(at, xt, xg, hid, istd, mix, dq, w_qkv, w_out), (updated, tokens_grad)):
            out[to, :, :] = pltpu.roll(strip_of(rows, 3), s1, 1).astype(BF)

    def step(a, carry):
        store(a - 1)
        windows(a)
        return carry

    windows(0)
    lax.fori_loop(1, 7, step, 0)
    store(6)
    copies = start_all([(updated, updated_out), (tokens_grad, grad_out)], sems, 2)
    for b in range(2):
        r = slice(b * 256, (b + 1) * 256)
        w_sum[r, : 3 * D] = dot_tn(hid[:, r], dq[...])
        w_sum[r, 3 * D :] = dot_tn(mix[:, r], xg[...])
        copies += start_all([(w_sum.at[r], w_part.at[r])], sems, b)
    wait_all(copies)


def edge_kernel(
    shifts, tokens_in, grads_in, halo_lon, halo_lat, halo_cor, keys, bias, w_qkv_in, w_out_in, w_part,
    lat_up, lon_up, lat_grad, lon_grad, out_lat, out_lon, w_mine, w_other,
    tok, grad, far, low_tok, low_grad, low_far, w_qkv, w_out, to_lat, to_lon,
    xt, xg, hid, istd, qkvg, mix, dq, ones, w_sum, sems,
):
    s0, s1 = shifts[0], shifts[1]
    core = lax.axis_index("core")
    thr_edge = jnp.where(lax.axis_index(LAT) == 7, 8 - s1, 8)
    rows_in = start_all(
        [
            (tokens_in.at[:, 16:32, :], tok),
            (grads_in.at[:, 16:32, :], grad),
            (halo_lat, far),
            (tokens_in.at[56:64], low_tok.at[0:8]),
            (grads_in.at[56:64], low_grad.at[0:8]),
            (halo_lon.at[:, :, 0:D], low_tok.at[8:16]),
            (halo_lon.at[:, :, D : 2 * D], low_grad.at[8:16]),
            (halo_lat.at[56:64], low_far.at[0:8]),
            (halo_cor, low_far.at[8:16]),
        ],
        sems,
    )
    weights_in = start_all([(w_qkv_in, w_qkv), (w_out_in, w_out), (w_part, w_sum)], sems, 9)
    fill_ones(ones)
    tail = slice(11 * CELLS, 12 * CELLS)
    xg[tail, :] = jnp.zeros((CELLS, D), BF)
    hid[tail, :] = jnp.zeros((CELLS, D), BF)
    wait_all(rows_in)

    def load(a, carry):
        at = pl.ds(s0 + a * WIN, WIN)
        found = []
        for near, c in ((tok, 0), (grad, D)):
            rows = [near[at, 8:16, :].astype(F32), far[at, :, c : c + D].astype(F32)]
            found.append(rows_of(pltpu.roll(jnp.concatenate(rows, axis=1), 16 - s1, 1)[:, :8]))
        keep_window(*found, pl.multiple_of(a * CELLS, CELLS), xt, xg, hid, istd)
        return carry

    lax.fori_loop(0, 7, load, 0)
    at = pl.ds(s0, WIN)
    found = []
    for near, c in ((low_tok, 0), (low_grad, D)):
        rows = [near[at, :, :].astype(F32), low_far[at, :, c : c + D].astype(F32)]
        found.append(pltpu.roll(jnp.concatenate(rows, axis=1), 40 - s1, 1))
    for b in range(4):
        x, g = (rows_of(rows[:, b * WIN : b * WIN + WIN]) for rows in found)
        keep_window(x, g, (7 + b) * CELLS, xt, xg, hid, istd)
    wait_all(weights_in)
    project(12 * CELLS, 384, hid, xg, w_qkv, w_out, qkvg)

    def windows(a, carry):
        seen, thr = [], []
        for w in range(3):
            n = a * 3 + w
            row = jnp.where(n < 7, 24 + n, jnp.minimum(8 * n - 49, 31))
            seen.append(keys[pl.ds(row, 1), :])
            thr.append(jnp.where((n < 7) | (n == 10), thr_edge, 8))
        attend(a * 3, seen, thr, bias, ones, qkvg, mix, dq)
        return carry

    lax.fori_loop(0, 4, windows, 0)

    results = finish(slice(0, 7 * CELLS), xt, xg, hid, istd, mix, dq, w_qkv, w_out)
    for rows, near, c in zip(results, (tok, grad), (0, D)):
        for a in range(7):
            strip = strip_of(rows[a * CELLS : (a + 1) * CELLS], 1)
            strip = pltpu.roll(strip, s1, 1).astype(BF)
            near[pl.ds(s0 + a * WIN, WIN), 0:8, :] = strip[:, :8]
            to_lat[pl.ds(s0 + a * WIN, WIN), :, c : c + D] = strip[:, 8:]
    results = finish(slice(7 * CELLS, 11 * CELLS), xt, xg, hid, istd, mix, dq, w_qkv, w_out)
    for rows, low, c in zip(results, (low_tok, low_grad), (0, D)):
        strip = pltpu.roll(strip_of(rows, 4), s1, 1).astype(BF)
        low[pl.ds(s0, WIN), :, :] = strip[:, :32]
        to_lat[pl.ds(s0 + 56, WIN), :, c : c + D] = strip[:, 32:]
    to_lon[:, :, 0:D] = low_tok[8:16]
    to_lon[:, :, D : 2 * D] = low_grad[8:16]
    copies = start_all(
        [
            (tok, lat_up),
            (grad, lat_grad),
            (low_tok.at[0:8], lon_up),
            (low_grad.at[0:8], lon_grad),
            (to_lat, out_lat),
            (to_lon, out_lon),
        ],
        sems,
    )
    for b in range(2):
        r = slice(b * 256, (b + 1) * 256)
        w_sum[r, : 3 * D] += dot_tn(hid[:, r], dq[...])
        w_sum[r, 3 * D :] += dot_tn(mix[:, r], xg[...])

    def split(n, carry):
        to = pl.ds(pl.multiple_of(n * 32, 32), 32)
        w_mine[to, :] = w_sum[pl.ds(pl.multiple_of((2 * n + core) * 32, 32), 32), :].astype(BF)
        w_other[to, :] = w_sum[pl.ds(pl.multiple_of((2 * n + 1 - core) * 32, 32), 32), :].astype(BF)
        return carry

    lax.fori_loop(0, 8, split, 0)
    wait_all(copies)


def edge_merge_kernel(
    shifts, updated, tokens_grad, lat_up, lon_up, lat_grad, lon_grad, out_updated, out_grad,
    side, low, sems,
):
    s0, s1 = shifts[0], shifts[1]
    pairs = []
    for n, out in enumerate((out_updated, out_grad)):
        pairs += [(out.at[:, 16:32, :], side.at[n]), (out.at[56:64, 0:16, :], low.at[n])]
    wait_all(start_all(pairs, sems))
    mark = iota((8, 8, D), 1) >= s1
    for n, (lat, lon) in enumerate(((lat_up, lon_up), (lat_grad, lon_grad))):

        def rest(r, carry, n=n, lat=lat):
            at = pl.ds(pl.multiple_of(r * 8, 8), 8)
            rows = side[n, at, 8:16, :].astype(F32)
            side[n, at, 8:16, :] = jnp.where(mark, lat[at, 0:8, :].astype(F32), rows).astype(BF)
            return carry

        lax.fori_loop(0, 8, rest, 0)
        later = iota((8, 16, D), 0) >= s0
        rows = side[n, 56:64, :, :].astype(F32)
        side[n, 56:64, :, :] = jnp.where(later, lon[:, 16:32, :].astype(F32), rows).astype(BF)
        later = later & (iota((8, 16, D), 1) >= s1)
        rows = low[n].astype(F32)
        low[n] = jnp.where(later, lon[:, 0:16, :].astype(F32), rows).astype(BF)
    wait_all(start_all([(b, a) for a, b in pairs], sems))


def lat_return_kernel(
    shifts, updated, tokens_grad, in_lat, out_lon, out_updated, out_grad, to_lon, side, sems
):
    s1 = shifts[1]
    pairs = [(out.at[:, 0:16, :], side.at[n]) for n, out in enumerate((out_updated, out_grad))]
    copies = start_all(pairs, sems)
    mark = iota((8, 8, D), 1) < s1
    for n in range(2):
        cols = slice(n * D, n * D + D)
        first = jnp.where(mark, in_lat[64:72, :, cols].astype(F32), out_lon[:, 0:8, cols].astype(F32))
        to_lon[:, 0:8, cols] = first.astype(BF)
        to_lon[:, 8:32, cols] = out_lon[:, 8:32, cols]
    wait_all(copies)
    for n in range(2):

        def place(r, carry, n=n):
            at = pl.ds(pl.multiple_of(r * 8, 8), 8)
            rows = side[n, at, 0:8, :].astype(F32)
            came = in_lat[at, :, n * D : n * D + D].astype(F32)
            side[n, at, 0:8, :] = jnp.where(mark, came, rows).astype(BF)
            return carry

        lax.fori_loop(0, 8, place, 0)
    wait_all(start_all([(b, a) for a, b in pairs], sems))


def lon_return_kernel(shifts, updated, tokens_grad, in_lon, out_updated, out_grad, top, sems):
    s0 = shifts[0]
    pairs = [(out.at[0:8], top.at[n]) for n, out in enumerate((out_updated, out_grad))]
    wait_all(start_all(pairs, sems))
    early = iota((8, 32, D), 0) < s0
    for n in range(2):
        came = in_lon[:, :, n * D : n * D + D].astype(F32)
        top[n] = jnp.where(early, came, top[n].astype(F32)).astype(BF)
    wait_all(start_all([(b, a) for a, b in pairs], sems))


def vmem(shape, dtype):
    return pltpu.VMEM(shape, dtype)


def sds(shape, dtype):
    return jax.ShapeDtypeStruct(shape, dtype)


IN_VMEM = pl.BlockSpec(memory_space=pltpu.VMEM)
IN_SMEM = pl.BlockSpec(memory_space=pltpu.SMEM)
IN_HBM = pl.BlockSpec(memory_space=pl.ANY)


def call(kernel, out_shape, scratch, in_specs, out_specs, aliases=None):
    return pl.pallas_call(
        kernel,
        out_shape=out_shape,
        in_specs=[IN_SMEM] + in_specs,
        out_specs=out_specs,
        scratch_shapes=scratch,
        input_output_aliases=aliases or {},
        compiler_params=pltpu.CompilerParams(vmem_limit_bytes=VMEM_LIMIT),
    )


def window_scratch(rows):
    return [vmem((rows, D), BF), vmem((rows, D), BF), vmem((rows, D), BF), vmem((rows, 128), F32)]


def attend_scratch(rows):
    return [
        vmem((rows, 4 * D), BF),
        vmem((rows, D), BF),
        vmem((rows, 3 * D), BF),
        vmem((GROUP, GROUP), BF),
    ]


def shift_to(value, d_lon, d_lat):
    pairs = []
    for a in range(16):
        for b in range(8):
            pairs.append((a * 8 + b, ((a + d_lon) % 16) * 8 + (b + d_lat) % 8))
    return lax.ppermute(value, ALL, pairs)


def scatter_sum(blocks, axes, count, beside=None):
    here = lax.axis_index(axes)
    parts = [lax.dynamic_index_in_dim(blocks, here, 0, keepdims=False)]
    for step in range(1, count):
        block = lax.dynamic_index_in_dim(blocks, (here + step) % count, 0, keepdims=False)
        pairs = [(n, (n + step) % count) for n in range(count)]
        parts.append(lax.ppermute(block, axes, pairs))
    extra = None
    if beside is not None:
        extra = beside(blocks)
        parts, extra = lax.optimization_barrier((parts, extra))
    total = parts[0].astype(F32)
    for part in parts[1:]:
        total = total + part.astype(F32)
    return total, extra


INNER, OUTER = 21 * CELLS, 12 * CELLS
GRID = sds((64, 32, D), BF)
DMA = pltpu.SemaphoreType.DMA


WEIGHTS = [vmem((D, 3 * D), BF), vmem((D, D), BF)]


def run_interior(*args):
    rows = vmem((64, 32, D), BF)
    return call(
        interior_kernel,
        [GRID, GRID, sds((D, 4 * D), F32), sds((32, 128), F32), sds((64, 512), F32)],
        [rows, rows, *WEIGHTS, vmem((72, 256), jnp.int32), rows, rows]
        + window_scratch(INNER)
        + attend_scratch(INNER)
        + [vmem((8, 256), F32), vmem((64, 128), jnp.int32), vmem((D, 4 * D), F32), DMA((6,))],
        [IN_HBM] * 3 + [IN_VMEM] * 2 + [IN_HBM] * 2,
        [IN_HBM] * 3 + [IN_VMEM] * 2,
    )(*args)


def run_edge(*args):
    lat, lon = (64, 16, D), (8, 32, D)
    far_lat, far_lon = (64, 8, 2 * D), (8, 32, 2 * D)
    return call(
        edge_kernel,
        [sds(shape, BF) for shape in (lat, lon, lat, lon, (72, 8, 2 * D), far_lon)]
        + [sds((D // 2, 4 * D), BF)] * 2,
        [vmem(lat, BF), vmem(lat, BF), vmem(far_lat, BF)]
        + [vmem((16, 32, D), BF), vmem((16, 32, D), BF), vmem((16, 8, 2 * D), BF)]
        + WEIGHTS
        + [vmem((72, 8, 2 * D), BF), vmem(far_lon, BF)]
        + window_scratch(OUTER)
        + attend_scratch(OUTER)
        + [vmem((D, 4 * D), F32), DMA((12,))],
        [IN_HBM] * 5 + [IN_VMEM] * 2 + [IN_HBM] * 3,
        [IN_HBM] * 6 + [IN_VMEM] * 2,
    )(*args)


def run_edge_merge(*args):
    return call(
        edge_merge_kernel,
        [GRID, GRID],
        [vmem((2, 64, 16, D), BF), vmem((2, 8, 16, D), BF), DMA((4,))],
        [IN_HBM] * 2 + [IN_VMEM] * 4,
        [IN_HBM] * 2,
        {1: 0, 2: 1},
    )(*args)


def run_lat_return(*args):
    return call(
        lat_return_kernel,
        [GRID, GRID, sds((8, 32, 2 * D), BF)],
        [vmem((2, 64, 16, D), BF), DMA((2,))],
        [IN_HBM] * 2 + [IN_VMEM] * 2,
        [IN_HBM] * 2 + [IN_VMEM],
        {1: 0, 2: 1},
    )(*args)


def run_lon_return(*args):
    return call(
        lon_return_kernel,
        [GRID, GRID],
        [vmem((2, 8, 32, D), BF), DMA((2,))],
        [IN_HBM] * 2 + [IN_VMEM],
        [IN_HBM] * 2,
        {1: 0, 2: 1},
    )(*args)


def local(tokens, pad_mask, shifts, bias_table, rel_index, w_qkv, w_out, grad_out):
    both = lambda a, b: jnp.concatenate([tokens[a, b], grad_out[a, b]], axis=-1)
    halo_lat = shift_to(both(slice(None), slice(0, 8)), 0, -1)
    halo_lon = shift_to(both(slice(0, 8), slice(None)), -1, 0)
    halo_cor = shift_to(both(slice(0, 8), slice(0, 8)), -1, -1)

    updated, tokens_grad, w_part, keys, bias = run_interior(
        shifts, tokens, grad_out, pad_mask, bias_table, rel_index, w_qkv, w_out
    )
    *edges, out_lat, out_lon, w_mine, w_other = run_edge(
        shifts, tokens, grad_out, halo_lon, halo_lat, halo_cor, keys, bias, w_qkv, w_out, w_part
    )

    def merge_beside(blocks):
        _, *placed = lax.optimization_barrier((blocks, updated, tokens_grad))
        return run_edge_merge(shifts, *placed, *edges)

    in_lat = shift_to(out_lat, 0, 1)
    w_got = lax.ppermute(w_other, "core", [(0, 1), (1, 0)])
    total = (w_mine.astype(F32) + w_got.astype(F32)).astype(BF)
    total = total.reshape(2, 4, 32, 4 * D).transpose(1, 0, 2, 3)
    total, (updated, tokens_grad) = scatter_sum(total, "x", 4, merge_beside)
    total = total.astype(BF).reshape(2, 4, 8, 4 * D).transpose(1, 0, 2, 3)
    lat_beside = lambda blocks: run_lat_return(shifts, updated, tokens_grad, in_lat, out_lon)
    total, (updated, tokens_grad, out_lon) = scatter_sum(total, "y", 4, lat_beside)
    in_lon = shift_to(out_lon, 1, 0)
    total, _ = scatter_sum(total.astype(BF).reshape(4, 4, 4 * D), ("zh", "zl"), 4)

    updated, tokens_grad = run_lon_return(shifts, updated, tokens_grad, in_lon)
    return (updated, tokens_grad, total[:, : 3 * D], total[:, 3 * D :])


def solution(mesh):
    fine = Mesh(mesh.devices.reshape(2, 4, 2, 4, 2), ALL)
    in_specs = (P(LON, LAT, None), P(), P(), P(), P(), P(), P(), P(LON, LAT, None))
    out_specs = (P(LON, LAT, None), P(LON, LAT, None), P(ALL, None), P(ALL, None))
    return jax.shard_map(local, mesh=fine, in_specs=in_specs, out_specs=out_specs, check_vma=False)
```

```python
import jax
import jax.numpy as jnp
from jax import lax
from jax.experimental import pallas as pl
from jax.experimental.pallas import tpu as pltpu
from jax.sharding import Mesh, PartitionSpec as P

WIN = 8
CELLS = 64
D = 512
HEADS = 8
GROUP = 256
BF = jnp.bfloat16
F32 = jnp.float32
LOG2E = 1.4426950408889634
SCALE = 0.125
VMEM_LIMIT = 56 * 2**20
LON = ("zh", "x", "core")
LAT = ("y", "zl")
ALL = LON + LAT


def dot_nn(a, b):
    return lax.dot_general(a, b, (((1,), (0,)), ((), ())), preferred_element_type=F32)


def dot_nt(a, b):
    return lax.dot_general(a, b, (((1,), (1,)), ((), ())), preferred_element_type=F32)


def dot_tn(a, b):
    return lax.dot_general(a, b, (((0,), (0,)), ((), ())), preferred_element_type=F32)


def iota(shape, dim):
    return lax.broadcasted_iota(jnp.int32, shape, dim)


def keep_window(x, g, row, xt, xg, hid, istd):
    at = pl.ds(row, CELLS)
    center = x - jnp.mean(x, axis=-1, keepdims=True)
    inv = lax.rsqrt(jnp.mean(center * center, axis=-1, keepdims=True) + 1e-05)
    hid[at, :] = (center * inv).astype(BF)
    istd[at, :] = jnp.broadcast_to(inv, (CELLS, 128))
    xt[at, :] = x.astype(BF)
    xg[at, :] = g.astype(BF)


def project(rows, chunk, hid, xg, w_qkv, w_out, qkvg):
    def step(c, carry):
        at = pl.ds(pl.multiple_of(c * chunk, 64), chunk)
        qkvg[at, : 3 * D] = dot_nn(hid[at, :], w_qkv[...]).astype(BF)
        qkvg[at, 3 * D :] = dot_nt(xg[at, :], w_out[...]).astype(BF)
        return carry

    lax.fori_loop(0, rows // chunk, step, 0)


def fill_ones(ones):
    block = (iota((GROUP, GROUP), 0) >> 6) == (iota((GROUP, GROUP), 1) >> 6)
    ones[...] = jnp.where(block, 1.0, 0.0).astype(BF)


def attend(first, marks, thrs, bias, ones, qkvg, mix, dq):
    lane = iota((CELLS, 128), 1)
    cell = iota((CELLS, 128), 0)
    diag = (lane & 63) == cell
    low_half = lane < 64
    low_mask = jnp.where(low_half, 1.0, 0.0).astype(BF)
    high_mask = jnp.where(low_half, 0.0, 1.0).astype(BF)
    zero = jnp.zeros((CELLS, 128), BF)

    def by_head(x):
        a, b = x[:, :128], x[:, 128:]
        rows = [(a * low_mask, zero), (a * high_mask, zero), (zero, b * low_mask), (zero, b * high_mask)]
        return jnp.concatenate([jnp.concatenate(r, axis=1) for r in rows], axis=0)

    units = []
    for w, (mark, thr) in enumerate(zip(marks, thrs)):
        row = pl.multiple_of((first + w) * CELLS, CELLS)
        same = ((lane & 7) >= thr) == ((cell & 7) >= thr)
        valid = jnp.broadcast_to(mark, (CELLS, 128)) > 0.5
        ok = (valid & same) | diag
        ok = jnp.concatenate([ok, ok], axis=1)
        for h in range(2):
            c = h * GROUP
            at = pl.ds(row, CELLS)
            q = qkvg[at, c : c + GROUP]
            k = qkvg[at, D + c : D + c + GROUP]
            v = qkvg[at, 2 * D + c : 2 * D + c + GROUP]
            g = qkvg[at, 3 * D + c : 3 * D + c + GROUP]
            kbd, vbd = by_head(k), by_head(v)
            s = dot_nt(q, kbd)
            pg = dot_nt(g, vbd)
            e = jnp.where(ok, jnp.exp2(s * (SCALE * LOG2E) + bias[:, c : c + GROUP]), 0.0)
            units.append((at, c, q, g, kbd, vbd, e, pg))
    total = dot_nn(jnp.concatenate([u[6].astype(BF) for u in units], axis=0), ones[...])
    probs = []
    for n, u in enumerate(units):
        probs.append(u[6] / total[n * CELLS : (n + 1) * CELLS])
    dots = dot_nn(
        jnp.concatenate([(p * u[7]).astype(BF) for p, u in zip(probs, units)], axis=0), ones[...]
    )
    for n, (at, c, q, g, kbd, vbd, e, pg) in enumerate(units):
        p = probs[n]
        p_low = p.astype(BF)
        ds = (p * (pg - dots[n * CELLS : (n + 1) * CELLS]) * SCALE).astype(BF)
        mix[at, c : c + GROUP] = dot_nn(p_low, vbd).astype(BF)
        dq[at, c : c + GROUP] = dot_nn(ds, kbd).astype(BF)
        for t in range(2):
            lo, hi = t * 128, t * 128 + 128
            kg = dot_tn(ds[:, lo:hi], q[:, lo:hi])
            vg = dot_tn(p_low[:, lo:hi], g[:, lo:hi])
            dq[at, D + c + lo : D + c + hi] = jnp.where(low_half, kg[:64], kg[64:]).astype(BF)
            dq[at, 2 * D + c + lo : 2 * D + c + hi] = jnp.where(low_half, vg[:64], vg[64:]).astype(BF)


def finish(at, xt, xg, hid, istd, mix, dq, w_qkv, w_out):
    update = xt[at, :].astype(F32) + dot_nn(mix[at, :], w_out[...])
    normed_grad = dot_nt(dq[at, :], w_qkv[...])
    normed = hid[at, :].astype(F32)
    centred = normed_grad - jnp.mean(normed_grad, axis=-1, keepdims=True)
    centred = centred - normed * jnp.mean(normed_grad * normed, axis=-1, keepdims=True)
    inv = istd[at, :]
    return update, xg[at, :].astype(F32) + jnp.concatenate([inv] * 4, axis=1) * centred


def rows_of(strip):
    return strip.reshape(CELLS, D)


def strip_of(rows, count):
    parts = [rows[n * CELLS : (n + 1) * CELLS].reshape(WIN, WIN, D) for n in range(count)]
    return jnp.concatenate(parts + [jnp.zeros((WIN, WIN, D), F32)], axis=1)


def make_tables(marks_in, bias_table, rel_index, s0, s1, keys, bias, table, rel):
    rows = pltpu.roll(marks_in[...].astype(F32), 72 - s0, 0)[:64]
    lane = iota((256, 512), 1)
    place = (lax.axis_index(LAT) * 32 + s1 + (lane >> 7) * 8 + (lane & 7)) & 255
    pick = jnp.where(iota((256, 512), 0) == place, 1.0, 0.0).astype(BF)
    marks = dot_nn(rows.astype(BF), pick)
    own = (iota((64, 512), 0) & 7) == ((iota((64, 512), 1) & 63) >> 3)
    marks = jnp.sum(jnp.where(own, marks, 0.0).reshape(8, 8, 512), axis=1)
    for b in range(4):
        keys[8 * b : 8 * b + 8, :] = marks[:, 128 * b : 128 * b + 128]

    table[...] = jnp.zeros((8, 256), F32)
    table[:, :225] = bias_table[...] * LOG2E
    rel[:, :64] = rel_index[...]
    rel[:, 64:] = rel_index[...]
    at = rel[...]
    low = at < 128
    at = at & 127
    left = iota((CELLS, 128), 1) < 64
    for pair in range(4):
        found = []
        for h in (2 * pair, 2 * pair + 1):
            half = [
                jnp.take_along_axis(
                    jnp.broadcast_to(table[h : h + 1, c : c + 128], (CELLS, 128)), at, axis=1
                )
                for c in (0, 128)
            ]
            found.append(jnp.where(low, half[0], half[1]))
        bias[:, pair * 128 : pair * 128 + 128] = jnp.where(left, found[0], found[1])


def start_all(pairs, sems, first=0):
    copies = [pltpu.make_async_copy(a, b, sems.at[first + n]) for n, (a, b) in enumerate(pairs)]
    for copy in copies:
        copy.start()
    return copies


def wait_all(copies):
    for copy in copies:
        copy.wait()


def interior_kernel(
    shifts, tokens_in, grads_in, pad_in, bias_table, rel_index, w_qkv_in, w_out_in,
    updated_out, grad_out, w_part, keys, bias,
    tokens, grads, w_qkv, w_out, marks, updated, tokens_grad,
    xt, xg, hid, istd, qkvg, mix, dq, ones, table, rel, w_sum, sems,
):
    s0, s1 = shifts[0], shifts[1]
    base = lax.axis_index(LON) * 64
    mark_copies = start_all(
        [
            (pad_in.at[pl.ds(pl.multiple_of(base, 8), 64)], marks.at[0:64]),
            (pad_in.at[pl.ds(pl.multiple_of((base + 64) & 1023, 8), 8)], marks.at[64:72]),
        ],
        sems,
    )
    rows_in = start_all([(tokens_in, tokens), (grads_in, grads)], sems, 2)
    weights_in = start_all([(w_qkv_in, w_qkv), (w_out_in, w_out)], sems, 4)
    fill_ones(ones)
    wait_all(mark_copies)
    make_tables(marks, bias_table, rel_index, s0, s1, keys, bias, table, rel)
    wait_all(rows_in)

    def load(a, carry):
        at = pl.ds(s0 + a * WIN, WIN)
        x = pltpu.roll(tokens[at, :, :].astype(F32), 32 - s1, 1)
        g = pltpu.roll(grads[at, :, :].astype(F32), 32 - s1, 1)
        for b in range(3):
            row = pl.multiple_of((a * 3 + b) * CELLS, CELLS)
            c = slice(b * WIN, b * WIN + WIN)
            keep_window(rows_of(x[:, c]), rows_of(g[:, c]), row, xt, xg, hid, istd)
        return carry

    lax.fori_loop(0, 7, load, 0)
    wait_all(weights_in)
    project(21 * CELLS, 448, hid, xg, w_qkv, w_out, qkvg)

    def windows(a):
        seen = [keys[pl.ds(8 * b + a, 1), :] for b in range(3)]
        attend(a * 3, seen, [8] * 3, bias, ones, qkvg, mix, dq)

    def store(a):
        at = pl.ds(pl.multiple_of(a * 192, 64), 192)
        to = pl.ds(s0 + a * WIN, WIN)
        for rows, out in zip(finish(at, xt, xg, hid, istd, mix, dq, w_qkv, w_out), (updated, tokens_grad)):
            out[to, :, :] = pltpu.roll(strip_of(rows, 3), s1, 1).astype(BF)

    def step(a, carry):
        store(a - 1)
        windows(a)
        return carry

    windows(0)
    lax.fori_loop(1, 7, step, 0)
    store(6)
    copies = start_all([(updated, updated_out), (tokens_grad, grad_out)], sems, 2)
    for b in range(2):
        r = slice(b * 256, (b + 1) * 256)
        w_sum[r, : 3 * D] = dot_tn(hid[:, r], dq[...])
        w_sum[r, 3 * D :] = dot_tn(mix[:, r], xg[...])
        copies += start_all([(w_sum.at[r], w_part.at[r])], sems, b)
    wait_all(copies)


def edge_kernel(
    shifts, tokens_in, grads_in, halo_lon, halo_lat, halo_cor, keys, bias, w_qkv_in, w_out_in, w_part,
    lat_up, lon_up, lat_grad, lon_grad, out_up, out_grad, out_lon, out_cor, w_mine, w_other,
    tok, grad, far, low_tok, low_grad, low_far, w_qkv, w_out, to_lat, to_lon,
    xt, xg, hid, istd, qkvg, mix, dq, ones, w_sum, sems,
):
    s0, s1 = shifts[0], shifts[1]
    core = lax.axis_index("core")
    thr_edge = jnp.where(lax.axis_index(LAT) == 7, 8 - s1, 8)
    rows_in = start_all(
        [
            (tokens_in.at[:, 16:32, :], tok),
            (grads_in.at[:, 16:32, :], grad),
            (halo_lat, far),
            (tokens_in.at[56:64], low_tok.at[0:8]),
            (grads_in.at[56:64], low_grad.at[0:8]),
            (halo_lon.at[:, :, 0:D], low_tok.at[8:16]),
            (halo_lon.at[:, :, D : 2 * D], low_grad.at[8:16]),
            (halo_lat.at[56:64], low_far.at[0:8]),
            (halo_cor, low_far.at[8:16]),
        ],
        sems,
    )
    weights_in = start_all([(w_qkv_in, w_qkv), (w_out_in, w_out), (w_part, w_sum)], sems, 9)
    fill_ones(ones)
    tail = slice(11 * CELLS, 12 * CELLS)
    xg[tail, :] = jnp.zeros((CELLS, D), BF)
    hid[tail, :] = jnp.zeros((CELLS, D), BF)
    wait_all(rows_in)

    def load(a, carry):
        at = pl.ds(s0 + a * WIN, WIN)
        found = []
        for near, c in ((tok, 0), (grad, D)):
            rows = [near[at, 8:16, :].astype(F32), far[at, :, c : c + D].astype(F32)]
            found.append(rows_of(pltpu.roll(jnp.concatenate(rows, axis=1), 16 - s1, 1)[:, :8]))
        keep_window(*found, pl.multiple_of(a * CELLS, CELLS), xt, xg, hid, istd)
        return carry

    lax.fori_loop(0, 7, load, 0)
    at = pl.ds(s0, WIN)
    found = []
    for near, c in ((low_tok, 0), (low_grad, D)):
        rows = [near[at, :, :].astype(F32), low_far[at, :, c : c + D].astype(F32)]
        found.append(pltpu.roll(jnp.concatenate(rows, axis=1), 40 - s1, 1))
    for b in range(4):
        x, g = (rows_of(rows[:, b * WIN : b * WIN + WIN]) for rows in found)
        keep_window(x, g, (7 + b) * CELLS, xt, xg, hid, istd)
    wait_all(weights_in)
    project(12 * CELLS, 384, hid, xg, w_qkv, w_out, qkvg)

    def windows(a, carry):
        seen, thr = [], []
        for w in range(3):
            n = a * 3 + w
            row = jnp.where(n < 7, 24 + n, jnp.minimum(8 * n - 49, 31))
            seen.append(keys[pl.ds(row, 1), :])
            thr.append(jnp.where((n < 7) | (n == 10), thr_edge, 8))
        attend(a * 3, seen, thr, bias, ones, qkvg, mix, dq)
        return carry

    lax.fori_loop(0, 4, windows, 0)

    results = finish(slice(0, 7 * CELLS), xt, xg, hid, istd, mix, dq, w_qkv, w_out)
    for rows, near, c in zip(results, (tok, grad), (0, D)):
        for a in range(7):
            strip = strip_of(rows[a * CELLS : (a + 1) * CELLS], 1)
            strip = pltpu.roll(strip, s1, 1).astype(BF)
            near[pl.ds(s0 + a * WIN, WIN), 0:8, :] = strip[:, :8]
            to_lat[pl.ds(s0 + a * WIN, WIN), :, c : c + D] = strip[:, 8:]
    results = finish(slice(7 * CELLS, 11 * CELLS), xt, xg, hid, istd, mix, dq, w_qkv, w_out)
    for rows, low, c in zip(results, (low_tok, low_grad), (0, D)):
        strip = pltpu.roll(strip_of(rows, 4), s1, 1).astype(BF)
        low[pl.ds(s0, WIN), :, :] = strip[:, :32]
        to_lat[pl.ds(s0 + 56, WIN), :, c : c + D] = strip[:, 32:]
    to_lon[:, :, 0:D] = low_tok[8:16]
    to_lon[:, :, D : 2 * D] = low_grad[8:16]
    copies = start_all(
        [
            (tok, lat_up),
            (grad, lat_grad),
            (low_tok.at[0:8], lon_up),
            (low_grad.at[0:8], lon_grad),
            (to_lat.at[0:64, :, 0:D], out_up),
            (to_lat.at[0:64, :, D : 2 * D], out_grad),
            (to_lat.at[64:72], out_cor),
            (to_lon, out_lon),
        ],
        sems,
    )
    for b in range(2):
        r = slice(b * 256, (b + 1) * 256)
        w_sum[r, : 3 * D] += dot_tn(hid[:, r], dq[...])
        w_sum[r, 3 * D :] += dot_tn(mix[:, r], xg[...])

    def split(n, carry):
        to = pl.ds(pl.multiple_of(n * 32, 32), 32)
        w_mine[to, :] = w_sum[pl.ds(pl.multiple_of((2 * n + core) * 32, 32), 32), :].astype(BF)
        w_other[to, :] = w_sum[pl.ds(pl.multiple_of((2 * n + 1 - core) * 32, 32), 32), :].astype(BF)
        return carry

    lax.fori_loop(0, 8, split, 0)
    wait_all(copies)


def edge_merge_kernel(
    shifts, updated, tokens_grad, lat_up, lon_up, lat_grad, lon_grad, out_updated, out_grad,
    side, low, sems,
):
    s0, s1 = shifts[0], shifts[1]
    pairs = []
    for n, out in enumerate((out_updated, out_grad)):
        pairs += [(out.at[:, 16:32, :], side.at[n]), (out.at[56:64, 0:16, :], low.at[n])]
    wait_all(start_all(pairs, sems))
    mark = iota((8, 8, D), 1) >= s1
    for n, (lat, lon) in enumerate(((lat_up, lon_up), (lat_grad, lon_grad))):

        def rest(r, carry, n=n, lat=lat):
            at = pl.ds(pl.multiple_of(r * 8, 8), 8)
            rows = side[n, at, 8:16, :].astype(F32)
            side[n, at, 8:16, :] = jnp.where(mark, lat[at, 0:8, :].astype(F32), rows).astype(BF)
            return carry

        lax.fori_loop(0, 8, rest, 0)
        later = iota((8, 16, D), 0) >= s0
        rows = side[n, 56:64, :, :].astype(F32)
        side[n, 56:64, :, :] = jnp.where(later, lon[:, 16:32, :].astype(F32), rows).astype(BF)
        later = later & (iota((8, 16, D), 1) >= s1)
        rows = low[n].astype(F32)
        low[n] = jnp.where(later, lon[:, 0:16, :].astype(F32), rows).astype(BF)
    wait_all(start_all([(b, a) for a, b in pairs], sems))


def place_lat(s1, came, side):
    mark = iota((8, 8, D), 1) < s1

    def place(r, carry):
        at = pl.ds(pl.multiple_of(r * 8, 8), 8)
        rows = side[at, 0:8, :].astype(F32)
        side[at, 0:8, :] = jnp.where(mark, came[at, :, :].astype(F32), rows).astype(BF)
        return carry

    lax.fori_loop(0, 8, place, 0)


def updated_return_kernel(shifts, updated, in_up, out_updated, side, sems):
    pairs = [(out_updated.at[:, 0:16, :], side)]
    wait_all(start_all(pairs, sems))
    place_lat(shifts[1], in_up, side)
    wait_all(start_all([(b, a) for a, b in pairs], sems))


def return_kernel(
    shifts, updated, tokens_grad, in_grad, in_lon, in_cor, out_updated, out_grad, side, top, sems
):
    s0, s1 = shifts[0], shifts[1]
    pairs = [(out_grad.at[8:64, 0:16, :], side.at[8:64])]
    pairs += [(out.at[0:8], top.at[n]) for n, out in enumerate((out_updated, out_grad))]
    wait_all(start_all(pairs, sems))
    place_lat(s1, in_grad, side)
    early = iota((8, 32, D), 0) < s0
    first = iota((8, 8, D), 1) < s1
    for n in range(2):
        cols = slice(n * D, n * D + D)
        came = in_lon[:, :, cols].astype(F32)
        corner = jnp.where(first, in_cor[:, :, cols].astype(F32), came[:, 0:8])
        came = jnp.concatenate([corner, came[:, 8:]], axis=1)
        old = top[n].astype(F32)
        if n == 1:
            back = jnp.where(first, in_grad[0:8, :, :].astype(F32), old[:, 0:8])
            old = jnp.concatenate([back, old[:, 8:]], axis=1)
        top[n] = jnp.where(early, came, old).astype(BF)
    wait_all(start_all([(b, a) for a, b in pairs], sems))


def vmem(shape, dtype):
    return pltpu.VMEM(shape, dtype)


def sds(shape, dtype):
    return jax.ShapeDtypeStruct(shape, dtype)


IN_VMEM = pl.BlockSpec(memory_space=pltpu.VMEM)
IN_SMEM = pl.BlockSpec(memory_space=pltpu.SMEM)
IN_HBM = pl.BlockSpec(memory_space=pl.ANY)


def call(kernel, out_shape, scratch, in_specs, out_specs, aliases=None):
    return pl.pallas_call(
        kernel,
        out_shape=out_shape,
        in_specs=[IN_SMEM] + in_specs,
        out_specs=out_specs,
        scratch_shapes=scratch,
        input_output_aliases=aliases or {},
        compiler_params=pltpu.CompilerParams(vmem_limit_bytes=VMEM_LIMIT),
    )


def window_scratch(rows):
    return [vmem((rows, D), BF), vmem((rows, D), BF), vmem((rows, D), BF), vmem((rows, 128), F32)]


def attend_scratch(rows):
    return [
        vmem((rows, 4 * D), BF),
        vmem((rows, D), BF),
        vmem((rows, 3 * D), BF),
        vmem((GROUP, GROUP), BF),
    ]


def shift_to(value, d_lon, d_lat):
    pairs = []
    for a in range(16):
        for b in range(8):
            pairs.append((a * 8 + b, ((a + d_lon) % 16) * 8 + (b + d_lat) % 8))
    return lax.ppermute(value, ALL, pairs)


def scatter_sum(blocks, axes, count, beside=None):
    here = lax.axis_index(axes)
    parts = [lax.dynamic_index_in_dim(blocks, here, 0, keepdims=False)]
    for step in range(1, count):
        block = lax.dynamic_index_in_dim(blocks, (here + step) % count, 0, keepdims=False)
        pairs = [(n, (n + step) % count) for n in range(count)]
        parts.append(lax.ppermute(block, axes, pairs))
    extra = None
    if beside is not None:
        extra = beside(blocks)
        parts, extra = lax.optimization_barrier((parts, extra))
    total = parts[0].astype(F32)
    for part in parts[1:]:
        total = total + part.astype(F32)
    return total, extra


INNER, OUTER = 21 * CELLS, 12 * CELLS
GRID = sds((64, 32, D), BF)
DMA = pltpu.SemaphoreType.DMA


WEIGHTS = [vmem((D, 3 * D), BF), vmem((D, D), BF)]


def run_interior(*args):
    rows = vmem((64, 32, D), BF)
    return call(
        interior_kernel,
        [GRID, GRID, sds((D, 4 * D), F32), sds((32, 128), F32), sds((64, 512), F32)],
        [rows, rows, *WEIGHTS, vmem((72, 256), jnp.int32), rows, rows]
        + window_scratch(INNER)
        + attend_scratch(INNER)
        + [vmem((8, 256), F32), vmem((64, 128), jnp.int32), vmem((D, 4 * D), F32), DMA((6,))],
        [IN_HBM] * 3 + [IN_VMEM] * 2 + [IN_HBM] * 2,
        [IN_HBM] * 3 + [IN_VMEM] * 2,
    )(*args)


def run_edge(*args):
    lat, lon = (64, 16, D), (8, 32, D)
    near, far_lat, far_lon = (64, 8, D), (64, 8, 2 * D), (8, 32, 2 * D)
    return call(
        edge_kernel,
        [sds(shape, BF) for shape in (lat, lon, lat, lon, near, near, far_lon, (8, 8, 2 * D))]
        + [sds((D // 2, 4 * D), BF)] * 2,
        [vmem(lat, BF), vmem(lat, BF), vmem(far_lat, BF)]
        + [vmem((16, 32, D), BF), vmem((16, 32, D), BF), vmem((16, 8, 2 * D), BF)]
        + WEIGHTS
        + [vmem((72, 8, 2 * D), BF), vmem(far_lon, BF)]
        + window_scratch(OUTER)
        + attend_scratch(OUTER)
        + [vmem((D, 4 * D), F32), DMA((12,))],
        [IN_HBM] * 5 + [IN_VMEM] * 2 + [IN_HBM] * 3,
        [IN_HBM] * 8 + [IN_VMEM] * 2,
    )(*args)


def run_edge_merge(*args):
    return call(
        edge_merge_kernel,
        [GRID, GRID],
        [vmem((2, 64, 16, D), BF), vmem((2, 8, 16, D), BF), DMA((4,))],
        [IN_HBM] * 2 + [IN_VMEM] * 4,
        [IN_HBM] * 2,
        {1: 0, 2: 1},
    )(*args)


def run_updated_return(*args):
    scratch = [vmem((64, 16, D), BF), DMA((1,))]
    return call(updated_return_kernel, GRID, scratch, [IN_HBM, IN_VMEM], IN_HBM, {1: 0})(*args)


def run_return(*args):
    return call(
        return_kernel,
        [GRID, GRID],
        [vmem((64, 16, D), BF), vmem((2, 8, 32, D), BF), DMA((3,))],
        [IN_HBM] * 2 + [IN_VMEM] * 3,
        [IN_HBM] * 2,
        {1: 0, 2: 1},
    )(*args)


def local(tokens, pad_mask, shifts, bias_table, rel_index, w_qkv, w_out, grad_out):
    both = lambda a, b: jnp.concatenate([tokens[a, b], grad_out[a, b]], axis=-1)
    halo_lat = shift_to(both(slice(None), slice(0, 8)), 0, -1)
    halo_lon = shift_to(both(slice(0, 8), slice(None)), -1, 0)
    halo_cor = shift_to(both(slice(0, 8), slice(0, 8)), -1, -1)

    updated, tokens_grad, w_part, keys, bias = run_interior(
        shifts, tokens, grad_out, pad_mask, bias_table, rel_index, w_qkv, w_out
    )
    *edges, out_up, out_grad, out_lon, out_cor, w_mine, w_other = run_edge(
        shifts, tokens, grad_out, halo_lon, halo_lat, halo_cor, keys, bias, w_qkv, w_out, w_part
    )

    def merge_beside(blocks):
        _, *placed = lax.optimization_barrier((blocks, updated, tokens_grad))
        placed, grad = run_edge_merge(shifts, *placed, *edges)
        return run_updated_return(shifts, placed, in_up), grad

    w_got = lax.ppermute(w_other, "core", [(0, 1), (1, 0)])
    in_up = shift_to(out_up, 0, 1)
    in_grad = shift_to(out_grad, 0, 1)
    in_lon = shift_to(out_lon, 1, 0)
    in_cor = shift_to(out_cor, 1, 1)
    total = (w_mine.astype(F32) + w_got.astype(F32)).astype(BF)
    total = total.reshape(2, 4, 32, 4 * D).transpose(1, 0, 2, 3)
    total, (updated, tokens_grad) = scatter_sum(total, "x", 4, merge_beside)
    total = total.astype(BF).reshape(2, 4, 8, 4 * D).transpose(1, 0, 2, 3)
    total, (in_grad, in_cor) = scatter_sum(total, "y", 4, lambda blocks: (in_grad, in_cor))
    total, _ = scatter_sum(total.astype(BF).reshape(4, 4, 4 * D), ("zh", "zl"), 4)

    updated, tokens_grad = run_return(shifts, updated, tokens_grad, in_grad, in_lon, in_cor)
    return (updated, tokens_grad, total[:, : 3 * D], total[:, 3 * D :])


def solution(mesh):
    fine = Mesh(mesh.devices.reshape(2, 4, 2, 4, 2), ALL)
    in_specs = (P(LON, LAT, None), P(), P(), P(), P(), P(), P(), P(LON, LAT, None))
    out_specs = (P(LON, LAT, None), P(LON, LAT, None), P(ALL, None), P(ALL, None))
    return jax.shard_map(local, mesh=fine, in_specs=in_specs, out_specs=out_specs, check_vma=False)
```

```python
import jax
import jax.numpy as jnp
from jax import lax
from jax.experimental import pallas as pl
from jax.experimental.pallas import tpu as pltpu
from jax.sharding import Mesh, PartitionSpec as P

WIN = 8
CELLS = 64
D = 512
HEADS = 8
GROUP = 256
BF = jnp.bfloat16
F32 = jnp.float32
LOG2E = 1.4426950408889634
SCALE = 0.125
VMEM_LIMIT = 56 * 2**20
LON = ("zh", "x", "core")
LAT = ("y", "zl")
ALL = LON + LAT


def dot_nn(a, b):
    return lax.dot_general(a, b, (((1,), (0,)), ((), ())), preferred_element_type=F32)


def dot_nt(a, b):
    return lax.dot_general(a, b, (((1,), (1,)), ((), ())), preferred_element_type=F32)


def dot_tn(a, b):
    return lax.dot_general(a, b, (((0,), (0,)), ((), ())), preferred_element_type=F32)


def iota(shape, dim):
    return lax.broadcasted_iota(jnp.int32, shape, dim)


def keep_window(x, g, row, xt, xg, hid, istd):
    at = pl.ds(row, CELLS)
    center = x - jnp.mean(x, axis=-1, keepdims=True)
    inv = lax.rsqrt(jnp.mean(center * center, axis=-1, keepdims=True) + 1e-05)
    hid[at, :] = (center * inv).astype(BF)
    istd[at, :] = jnp.broadcast_to(inv, (CELLS, 128))
    xt[at, :] = x.astype(BF)
    xg[at, :] = g.astype(BF)


def project(rows, chunk, hid, xg, w_qkv, w_out, qkvg):
    def step(c, carry):
        at = pl.ds(pl.multiple_of(c * chunk, 64), chunk)
        qkvg[at, : 3 * D] = dot_nn(hid[at, :], w_qkv[...]).astype(BF)
        qkvg[at, 3 * D :] = dot_nt(xg[at, :], w_out[...]).astype(BF)
        return carry

    lax.fori_loop(0, rows // chunk, step, 0)


def fill_ones(ones):
    block = (iota((GROUP, GROUP), 0) >> 6) == (iota((GROUP, GROUP), 1) >> 6)
    ones[...] = jnp.where(block, 1.0, 0.0).astype(BF)


def attend(first, marks, thrs, bias, ones, qkvg, mix, dq):
    lane = iota((CELLS, 128), 1)
    cell = iota((CELLS, 128), 0)
    diag = (lane & 63) == cell
    low_half = lane < 64
    low_mask = jnp.where(low_half, 1.0, 0.0).astype(BF)
    high_mask = jnp.where(low_half, 0.0, 1.0).astype(BF)
    zero = jnp.zeros((CELLS, 128), BF)

    def by_head(x):
        a, b = x[:, :128], x[:, 128:]
        rows = [(a * low_mask, zero), (a * high_mask, zero), (zero, b * low_mask), (zero, b * high_mask)]
        return jnp.concatenate([jnp.concatenate(r, axis=1) for r in rows], axis=0)

    units = []
    for w, (mark, thr) in enumerate(zip(marks, thrs)):
        row = pl.multiple_of((first + w) * CELLS, CELLS)
        same = ((lane & 7) >= thr) == ((cell & 7) >= thr)
        valid = jnp.broadcast_to(mark, (CELLS, 128)) > 0.5
        ok = (valid & same) | diag
        ok = jnp.concatenate([ok, ok], axis=1)
        for h in range(2):
            c = h * GROUP
            at = pl.ds(row, CELLS)
            q = qkvg[at, c : c + GROUP]
            k = qkvg[at, D + c : D + c + GROUP]
            v = qkvg[at, 2 * D + c : 2 * D + c + GROUP]
            g = qkvg[at, 3 * D + c : 3 * D + c + GROUP]
            kbd, vbd = by_head(k), by_head(v)
            s = dot_nt(q, kbd)
            pg = dot_nt(g, vbd)
            e = jnp.where(ok, jnp.exp2(s * (SCALE * LOG2E) + bias[:, c : c + GROUP]), 0.0)
            units.append((at, c, q, g, kbd, vbd, e, pg))
    total = dot_nn(jnp.concatenate([u[6].astype(BF) for u in units], axis=0), ones[...])
    probs = []
    for n, u in enumerate(units):
        probs.append(u[6] / total[n * CELLS : (n + 1) * CELLS])
    dots = dot_nn(
        jnp.concatenate([(p * u[7]).astype(BF) for p, u in zip(probs, units)], axis=0), ones[...]
    )
    for n, (at, c, q, g, kbd, vbd, e, pg) in enumerate(units):
        p = probs[n]
        p_low = p.astype(BF)
        ds = (p * (pg - dots[n * CELLS : (n + 1) * CELLS]) * SCALE).astype(BF)
        mix[at, c : c + GROUP] = dot_nn(p_low, vbd).astype(BF)
        dq[at, c : c + GROUP] = dot_nn(ds, kbd).astype(BF)
        for t in range(2):
            lo, hi = t * 128, t * 128 + 128
            kg = dot_tn(ds[:, lo:hi], q[:, lo:hi])
            vg = dot_tn(p_low[:, lo:hi], g[:, lo:hi])
            dq[at, D + c + lo : D + c + hi] = jnp.where(low_half, kg[:64], kg[64:]).astype(BF)
            dq[at, 2 * D + c + lo : 2 * D + c + hi] = jnp.where(low_half, vg[:64], vg[64:]).astype(BF)


def finish(at, xt, xg, hid, istd, mix, dq, w_qkv, w_out):
    update = xt[at, :].astype(F32) + dot_nn(mix[at, :], w_out[...])
    normed_grad = dot_nt(dq[at, :], w_qkv[...])
    normed = hid[at, :].astype(F32)
    centred = normed_grad - jnp.mean(normed_grad, axis=-1, keepdims=True)
    centred = centred - normed * jnp.mean(normed_grad * normed, axis=-1, keepdims=True)
    inv = istd[at, :]
    return update, xg[at, :].astype(F32) + jnp.concatenate([inv] * 4, axis=1) * centred


def rows_of(strip):
    return strip.reshape(CELLS, D)


def strip_of(rows, count):
    parts = [rows[n * CELLS : (n + 1) * CELLS].reshape(WIN, WIN, D) for n in range(count)]
    return jnp.concatenate(parts + [jnp.zeros((WIN, WIN, D), F32)], axis=1)


def make_tables(marks_in, bias_table, rel_index, s0, s1, keys, bias, table, rel):
    rows = pltpu.roll(marks_in[...].astype(F32), 72 - s0, 0)[:64]
    lane = iota((256, 512), 1)
    place = (lax.axis_index(LAT) * 32 + s1 + (lane >> 7) * 8 + (lane & 7)) & 255
    pick = jnp.where(iota((256, 512), 0) == place, 1.0, 0.0).astype(BF)
    marks = dot_nn(rows.astype(BF), pick)
    own = (iota((64, 512), 0) & 7) == ((iota((64, 512), 1) & 63) >> 3)
    marks = jnp.sum(jnp.where(own, marks, 0.0).reshape(8, 8, 512), axis=1)
    for b in range(4):
        keys[8 * b : 8 * b + 8, :] = marks[:, 128 * b : 128 * b + 128]

    table[...] = jnp.zeros((8, 256), F32)
    table[:, :225] = bias_table[...] * LOG2E
    rel[:, :64] = rel_index[...]
    rel[:, 64:] = rel_index[...]
    at = rel[...]
    low = at < 128
    at = at & 127
    left = iota((CELLS, 128), 1) < 64
    for pair in range(4):
        found = []
        for h in (2 * pair, 2 * pair + 1):
            half = [
                jnp.take_along_axis(
                    jnp.broadcast_to(table[h : h + 1, c : c + 128], (CELLS, 128)), at, axis=1
                )
                for c in (0, 128)
            ]
            found.append(jnp.where(low, half[0], half[1]))
        bias[:, pair * 128 : pair * 128 + 128] = jnp.where(left, found[0], found[1])


def start_all(pairs, sems, first=0):
    copies = [pltpu.make_async_copy(a, b, sems.at[first + n]) for n, (a, b) in enumerate(pairs)]
    for copy in copies:
        copy.start()
    return copies


def wait_all(copies):
    for copy in copies:
        copy.wait()


def interior_kernel(
    shifts, tokens_in, grads_in, pad_in, bias_table, rel_index, w_qkv_in, w_out_in,
    updated_out, grad_out, w_part, keys, bias,
    tokens, grads, w_qkv, w_out, marks, updated, tokens_grad,
    xt, xg, hid, istd, qkvg, mix, dq, ones, table, rel, w_sum, sems,
):
    s0, s1 = shifts[0], shifts[1]
    base = lax.axis_index(LON) * 64
    mark_copies = start_all(
        [
            (pad_in.at[pl.ds(pl.multiple_of(base, 8), 64)], marks.at[0:64]),
            (pad_in.at[pl.ds(pl.multiple_of((base + 64) & 1023, 8), 8)], marks.at[64:72]),
        ],
        sems,
    )
    rows_in = start_all([(tokens_in, tokens), (grads_in, grads)], sems, 2)
    weights_in = start_all([(w_qkv_in, w_qkv), (w_out_in, w_out)], sems, 4)
    fill_ones(ones)
    wait_all(mark_copies)
    make_tables(marks, bias_table, rel_index, s0, s1, keys, bias, table, rel)
    wait_all(rows_in)

    def load(a, carry):
        at = pl.ds(s0 + a * WIN, WIN)
        x = pltpu.roll(tokens[at, :, :].astype(F32), 32 - s1, 1)
        g = pltpu.roll(grads[at, :, :].astype(F32), 32 - s1, 1)
        for b in range(3):
            row = pl.multiple_of((a * 3 + b) * CELLS, CELLS)
            c = slice(b * WIN, b * WIN + WIN)
            keep_window(rows_of(x[:, c]), rows_of(g[:, c]), row, xt, xg, hid, istd)
        return carry

    lax.fori_loop(0, 7, load, 0)
    wait_all(weights_in)
    project(21 * CELLS, 448, hid, xg, w_qkv, w_out, qkvg)

    def windows(a):
        seen = [keys[pl.ds(8 * b + a, 1), :] for b in range(3)]
        attend(a * 3, seen, [8] * 3, bias, ones, qkvg, mix, dq)

    def store(a):
        at = pl.ds(pl.multiple_of(a * 192, 64), 192)
        to = pl.ds(s0 + a * WIN, WIN)
        for rows, out in zip(finish(at, xt, xg, hid, istd, mix, dq, w_qkv, w_out), (updated, tokens_grad)):
            out[to, :, :] = pltpu.roll(strip_of(rows, 3), s1, 1).astype(BF)

    def step(a, carry):
        store(a - 1)
        windows(a)
        return carry

    windows(0)
    lax.fori_loop(1, 7, step, 0)
    store(6)
    copies = start_all([(updated, updated_out), (tokens_grad, grad_out)], sems, 2)
    for b in range(2):
        r = slice(b * 256, (b + 1) * 256)
        w_sum[r, : 3 * D] = dot_tn(hid[:, r], dq[...])
        w_sum[r, 3 * D :] = dot_tn(mix[:, r], xg[...])
        copies += start_all([(w_sum.at[r], w_part.at[r])], sems, b)
    wait_all(copies)


def edge_kernel(
    shifts, tokens_in, grads_in, halo_lon, halo_lat, halo_cor, keys, bias, w_qkv_in, w_out_in, w_part,
    lat_up, lon_up, lat_grad, lon_grad, out_up, out_grad, out_lon, out_cor, w_mine, w_other,
    tok, grad, far, low_tok, low_grad, low_far, w_qkv, w_out, to_lat, to_lon,
    xt, xg, hid, istd, qkvg, mix, dq, ones, w_sum, sems,
):
    s0, s1 = shifts[0], shifts[1]
    core = lax.axis_index("core")
    thr_edge = jnp.where(lax.axis_index(LAT) == 7, 8 - s1, 8)
    rows_in = start_all(
        [
            (tokens_in.at[:, 16:32, :], tok),
            (grads_in.at[:, 16:32, :], grad),
            (halo_lat, far),
            (tokens_in.at[56:64], low_tok.at[0:8]),
            (grads_in.at[56:64], low_grad.at[0:8]),
            (halo_lon.at[:, :, 0:D], low_tok.at[8:16]),
            (halo_lon.at[:, :, D : 2 * D], low_grad.at[8:16]),
            (halo_lat.at[56:64], low_far.at[0:8]),
            (halo_cor, low_far.at[8:16]),
        ],
        sems,
    )
    weights_in = start_all([(w_qkv_in, w_qkv), (w_out_in, w_out), (w_part, w_sum)], sems, 9)
    fill_ones(ones)
    tail = slice(11 * CELLS, 12 * CELLS)
    xg[tail, :] = jnp.zeros((CELLS, D), BF)
    hid[tail, :] = jnp.zeros((CELLS, D), BF)
    wait_all(rows_in)

    def load(a, carry):
        at = pl.ds(s0 + a * WIN, WIN)
        found = []
        for near, c in ((tok, 0), (grad, D)):
            rows = [near[at, 8:16, :].astype(F32), far[at, :, c : c + D].astype(F32)]
            found.append(rows_of(pltpu.roll(jnp.concatenate(rows, axis=1), 16 - s1, 1)[:, :8]))
        keep_window(*found, pl.multiple_of(a * CELLS, CELLS), xt, xg, hid, istd)
        return carry

    lax.fori_loop(0, 7, load, 0)
    at = pl.ds(s0, WIN)
    found = []
    for near, c in ((low_tok, 0), (low_grad, D)):
        rows = [near[at, :, :].astype(F32), low_far[at, :, c : c + D].astype(F32)]
        found.append(pltpu.roll(jnp.concatenate(rows, axis=1), 40 - s1, 1))
    for b in range(4):
        x, g = (rows_of(rows[:, b * WIN : b * WIN + WIN]) for rows in found)
        keep_window(x, g, (7 + b) * CELLS, xt, xg, hid, istd)
    wait_all(weights_in)
    project(12 * CELLS, 384, hid, xg, w_qkv, w_out, qkvg)

    def windows(a, carry):
        seen, thr = [], []
        for w in range(3):
            n = a * 3 + w
            row = jnp.where(n < 7, 24 + n, jnp.minimum(8 * n - 49, 31))
            seen.append(keys[pl.ds(row, 1), :])
            thr.append(jnp.where((n < 7) | (n == 10), thr_edge, 8))
        attend(a * 3, seen, thr, bias, ones, qkvg, mix, dq)
        return carry

    lax.fori_loop(0, 4, windows, 0)

    results = finish(slice(0, 7 * CELLS), xt, xg, hid, istd, mix, dq, w_qkv, w_out)
    for rows, near, c in zip(results, (tok, grad), (0, D)):
        for a in range(7):
            strip = strip_of(rows[a * CELLS : (a + 1) * CELLS], 1)
            strip = pltpu.roll(strip, s1, 1).astype(BF)
            near[pl.ds(s0 + a * WIN, WIN), 0:8, :] = strip[:, :8]
            to_lat[pl.ds(s0 + a * WIN, WIN), :, c : c + D] = strip[:, 8:]
    results = finish(slice(7 * CELLS, 11 * CELLS), xt, xg, hid, istd, mix, dq, w_qkv, w_out)
    for rows, low, c in zip(results, (low_tok, low_grad), (0, D)):
        strip = pltpu.roll(strip_of(rows, 4), s1, 1).astype(BF)
        low[pl.ds(s0, WIN), :, :] = strip[:, :32]
        to_lat[pl.ds(s0 + 56, WIN), :, c : c + D] = strip[:, 32:]
    to_lon[:, :, 0:D] = low_tok[8:16]
    to_lon[:, :, D : 2 * D] = low_grad[8:16]
    copies = start_all(
        [
            (tok, lat_up),
            (grad, lat_grad),
            (low_tok.at[0:8], lon_up),
            (low_grad.at[0:8], lon_grad),
            (to_lat.at[0:64, :, 0:D], out_up),
            (to_lat.at[0:64, :, D : 2 * D], out_grad),
            (to_lat.at[64:72], out_cor),
            (to_lon, out_lon),
        ],
        sems,
    )
    for b in range(2):
        r = slice(b * 256, (b + 1) * 256)
        w_sum[r, : 3 * D] += dot_tn(hid[:, r], dq[...])
        w_sum[r, 3 * D :] += dot_tn(mix[:, r], xg[...])

    def split(n, carry):
        to = pl.ds(pl.multiple_of(n * 32, 32), 32)
        w_mine[to, :] = w_sum[pl.ds(pl.multiple_of((2 * n + core) * 32, 32), 32), :].astype(BF)
        w_other[to, :] = w_sum[pl.ds(pl.multiple_of((2 * n + 1 - core) * 32, 32), 32), :].astype(BF)
        return carry

    lax.fori_loop(0, 8, split, 0)
    wait_all(copies)


def edge_merge_kernel(
    shifts, updated, tokens_grad, lat_up, lon_up, lat_grad, lon_grad, out_updated, out_grad,
    side, low, sems,
):
    s0, s1 = shifts[0], shifts[1]
    pairs = []
    for n, out in enumerate((out_updated, out_grad)):
        pairs += [(out.at[:, 16:32, :], side.at[n]), (out.at[56:64, 0:16, :], low.at[n])]
    wait_all(start_all(pairs, sems))
    mark = iota((8, 8, D), 1) >= s1
    for n, (lat, lon) in enumerate(((lat_up, lon_up), (lat_grad, lon_grad))):

        def rest(r, carry, n=n, lat=lat):
            at = pl.ds(pl.multiple_of(r * 8, 8), 8)
            rows = side[n, at, 8:16, :].astype(F32)
            side[n, at, 8:16, :] = jnp.where(mark, lat[at, 0:8, :].astype(F32), rows).astype(BF)
            return carry

        lax.fori_loop(0, 8, rest, 0)
        later = iota((8, 16, D), 0) >= s0
        rows = side[n, 56:64, :, :].astype(F32)
        side[n, 56:64, :, :] = jnp.where(later, lon[:, 16:32, :].astype(F32), rows).astype(BF)
        later = later & (iota((8, 16, D), 1) >= s1)
        rows = low[n].astype(F32)
        low[n] = jnp.where(later, lon[:, 0:16, :].astype(F32), rows).astype(BF)
    wait_all(start_all([(b, a) for a, b in pairs], sems))


def return_kernel(
    shifts, updated, tokens_grad, in_up, in_grad, in_lon, in_cor, out_updated, out_grad, side, top, sems
):
    s0, s1 = shifts[0], shifts[1]
    outs = (out_updated, out_grad)
    tops = [(out.at[0:8], top.at[n]) for n, out in enumerate(outs)]
    sides = [(out.at[8:64, 0:16, :], side.at[n, 8:64]) for n, out in enumerate(outs)]
    tops_in, sides_in = start_all(tops, sems), start_all(sides, sems, 2)
    wait_all(tops_in)
    early = iota((8, 32, D), 0) < s0
    first = iota((8, 8, D), 1) < s1
    for n, in_lat in enumerate((in_up, in_grad)):
        cols = slice(n * D, n * D + D)
        came = in_lon[:, :, cols].astype(F32)
        corner = jnp.where(first, in_cor[:, :, cols].astype(F32), came[:, 0:8])
        came = jnp.concatenate([corner, came[:, 8:]], axis=1)
        old = top[n].astype(F32)
        back = jnp.where(first, in_lat[0:8, :, :].astype(F32), old[:, 0:8])
        old = jnp.concatenate([back, old[:, 8:]], axis=1)
        top[n] = jnp.where(early, came, old).astype(BF)
    wait_all(sides_in)
    copies = start_all([(b, a) for a, b in tops], sems)
    for n, in_lat in enumerate((in_up, in_grad)):

        def place(r, carry, n=n, in_lat=in_lat):
            at = pl.ds(pl.multiple_of(r * 8, 8), 8)
            rows = side[n, at, 0:8, :].astype(F32)
            side[n, at, 0:8, :] = jnp.where(first, in_lat[at, :, :].astype(F32), rows).astype(BF)
            return carry

        lax.fori_loop(1, 8, place, 0)
        copies += start_all([sides[n][::-1]], sems, 2 + n)
    wait_all(copies)


def vmem(shape, dtype):
    return pltpu.VMEM(shape, dtype)


def sds(shape, dtype):
    return jax.ShapeDtypeStruct(shape, dtype)


IN_VMEM = pl.BlockSpec(memory_space=pltpu.VMEM)
IN_SMEM = pl.BlockSpec(memory_space=pltpu.SMEM)
IN_HBM = pl.BlockSpec(memory_space=pl.ANY)


def call(kernel, out_shape, scratch, in_specs, out_specs, aliases=None):
    return pl.pallas_call(
        kernel,
        out_shape=out_shape,
        in_specs=[IN_SMEM] + in_specs,
        out_specs=out_specs,
        scratch_shapes=scratch,
        input_output_aliases=aliases or {},
        compiler_params=pltpu.CompilerParams(vmem_limit_bytes=VMEM_LIMIT),
    )


def window_scratch(rows):
    return [vmem((rows, D), BF), vmem((rows, D), BF), vmem((rows, D), BF), vmem((rows, 128), F32)]


def attend_scratch(rows):
    return [
        vmem((rows, 4 * D), BF),
        vmem((rows, D), BF),
        vmem((rows, 3 * D), BF),
        vmem((GROUP, GROUP), BF),
    ]


def shift_to(value, d_lon, d_lat):
    pairs = []
    for a in range(16):
        for b in range(8):
            pairs.append((a * 8 + b, ((a + d_lon) % 16) * 8 + (b + d_lat) % 8))
    return lax.ppermute(value, ALL, pairs)


def scatter_sum(blocks, axes, count, beside=None):
    here = lax.axis_index(axes)
    parts = [lax.dynamic_index_in_dim(blocks, here, 0, keepdims=False)]
    for step in range(1, count):
        block = lax.dynamic_index_in_dim(blocks, (here + step) % count, 0, keepdims=False)
        pairs = [(n, (n + step) % count) for n in range(count)]
        parts.append(lax.ppermute(block, axes, pairs))
    extra = None
    if beside is not None:
        extra = beside(blocks)
        parts, extra = lax.optimization_barrier((parts, extra))
    total = parts[0].astype(F32)
    for part in parts[1:]:
        total = total + part.astype(F32)
    return total, extra


INNER, OUTER = 21 * CELLS, 12 * CELLS
GRID = sds((64, 32, D), BF)
DMA = pltpu.SemaphoreType.DMA


WEIGHTS = [vmem((D, 3 * D), BF), vmem((D, D), BF)]


def run_interior(*args):
    rows = vmem((64, 32, D), BF)
    return call(
        interior_kernel,
        [GRID, GRID, sds((D, 4 * D), F32), sds((32, 128), F32), sds((64, 512), F32)],
        [rows, rows, *WEIGHTS, vmem((72, 256), jnp.int32), rows, rows]
        + window_scratch(INNER)
        + attend_scratch(INNER)
        + [vmem((8, 256), F32), vmem((64, 128), jnp.int32), vmem((D, 4 * D), F32), DMA((6,))],
        [IN_HBM] * 3 + [IN_VMEM] * 2 + [IN_HBM] * 2,
        [IN_HBM] * 3 + [IN_VMEM] * 2,
    )(*args)


def run_edge(*args):
    lat, lon = (64, 16, D), (8, 32, D)
    near, far_lat, far_lon = (64, 8, D), (64, 8, 2 * D), (8, 32, 2 * D)
    return call(
        edge_kernel,
        [sds(shape, BF) for shape in (lat, lon, lat, lon, near, near, far_lon, (8, 8, 2 * D))]
        + [sds((D // 2, 4 * D), BF)] * 2,
        [vmem(lat, BF), vmem(lat, BF), vmem(far_lat, BF)]
        + [vmem((16, 32, D), BF), vmem((16, 32, D), BF), vmem((16, 8, 2 * D), BF)]
        + WEIGHTS
        + [vmem((72, 8, 2 * D), BF), vmem(far_lon, BF)]
        + window_scratch(OUTER)
        + attend_scratch(OUTER)
        + [vmem((D, 4 * D), F32), DMA((12,))],
        [IN_HBM] * 5 + [IN_VMEM] * 2 + [IN_HBM] * 3,
        [IN_HBM] * 8 + [IN_VMEM] * 2,
    )(*args)


def run_edge_merge(*args):
    return call(
        edge_merge_kernel,
        [GRID, GRID],
        [vmem((2, 64, 16, D), BF), vmem((2, 8, 16, D), BF), DMA((4,))],
        [IN_HBM] * 2 + [IN_VMEM] * 4,
        [IN_HBM] * 2,
        {1: 0, 2: 1},
    )(*args)


def run_return(*args):
    return call(
        return_kernel,
        [GRID, GRID],
        [vmem((2, 64, 16, D), BF), vmem((2, 8, 32, D), BF), DMA((4,))],
        [IN_HBM] * 2 + [IN_VMEM] * 4,
        [IN_HBM] * 2,
        {1: 0, 2: 1},
    )(*args)


def local(tokens, pad_mask, shifts, bias_table, rel_index, w_qkv, w_out, grad_out):
    both = lambda a, b: jnp.concatenate([tokens[a, b], grad_out[a, b]], axis=-1)
    halo_lat = shift_to(both(slice(None), slice(0, 8)), 0, -1)
    halo_lon = shift_to(both(slice(0, 8), slice(None)), -1, 0)
    halo_cor = shift_to(both(slice(0, 8), slice(0, 8)), -1, -1)

    updated, tokens_grad, w_part, keys, bias = run_interior(
        shifts, tokens, grad_out, pad_mask, bias_table, rel_index, w_qkv, w_out
    )
    *edges, out_up, out_grad, out_lon, out_cor, w_mine, w_other = run_edge(
        shifts, tokens, grad_out, halo_lon, halo_lat, halo_cor, keys, bias, w_qkv, w_out, w_part
    )

    def merge_beside(blocks):
        _, *placed = lax.optimization_barrier((blocks, updated, tokens_grad))
        return *run_edge_merge(shifts, *placed, *edges), in_up

    w_got = lax.ppermute(w_other, "core", [(0, 1), (1, 0)])
    in_up = shift_to(out_up, 0, 1)
    in_grad = shift_to(out_grad, 0, 1)
    in_lon = shift_to(out_lon, 1, 0)
    in_cor = shift_to(out_cor, 1, 1)
    total = (w_mine.astype(F32) + w_got.astype(F32)).astype(BF)
    total = total.reshape(2, 4, 32, 4 * D).transpose(1, 0, 2, 3)
    total, (updated, tokens_grad, in_up) = scatter_sum(total, "x", 4, merge_beside)
    total = total.astype(BF).reshape(2, 4, 8, 4 * D).transpose(1, 0, 2, 3)
    total, (in_grad, in_lon) = scatter_sum(total, "y", 4, lambda blocks: (in_grad, in_lon))
    total, _ = scatter_sum(total.astype(BF).reshape(4, 4, 4 * D), ("zh", "zl"), 4)

    updated, tokens_grad = run_return(shifts, updated, tokens_grad, in_up, in_grad, in_lon, in_cor)
    return (updated, tokens_grad, total[:, : 3 * D], total[:, 3 * D :])


def solution(mesh):
    fine = Mesh(mesh.devices.reshape(2, 4, 2, 4, 2), ALL)
    in_specs = (P(LON, LAT, None), P(), P(), P(), P(), P(), P(), P(LON, LAT, None))
    out_specs = (P(LON, LAT, None), P(LON, LAT, None), P(ALL, None), P(ALL, None))
    return jax.shard_map(local, mesh=fine, in_specs=in_specs, out_specs=out_specs, check_vma=False)
```

```python
import jax
import jax.numpy as jnp
from jax import lax
from jax.experimental import pallas as pl
from jax.experimental.pallas import tpu as pltpu
from jax.sharding import Mesh, PartitionSpec as P

WIN = 8
CELLS = 64
D = 512
HEADS = 8
GROUP = 256
BF = jnp.bfloat16
F32 = jnp.float32
LOG2E = 1.4426950408889634
SCALE = 0.125
VMEM_LIMIT = 56 * 2**20
LON = ("zh", "x", "core")
LAT = ("y", "zl")
ALL = LON + LAT


def dot_nn(a, b):
    return lax.dot_general(a, b, (((1,), (0,)), ((), ())), preferred_element_type=F32)


def dot_nt(a, b):
    return lax.dot_general(a, b, (((1,), (1,)), ((), ())), preferred_element_type=F32)


def dot_tn(a, b):
    return lax.dot_general(a, b, (((0,), (0,)), ((), ())), preferred_element_type=F32)


def iota(shape, dim):
    return lax.broadcasted_iota(jnp.int32, shape, dim)


def keep_window(x, g, row, xt, xg, hid, istd):
    at = pl.ds(row, CELLS)
    center = x - jnp.mean(x, axis=-1, keepdims=True)
    inv = lax.rsqrt(jnp.mean(center * center, axis=-1, keepdims=True) + 1e-05)
    hid[at, :] = (center * inv).astype(BF)
    istd[at, :] = jnp.broadcast_to(inv, (CELLS, 128))
    xt[at, :] = x.astype(BF)
    xg[at, :] = g.astype(BF)


def project(rows, chunk, hid, xg, w_qkv, w_out, qkvg):
    def step(c, carry):
        at = pl.ds(pl.multiple_of(c * chunk, 64), chunk)
        qkvg[at, : 3 * D] = dot_nn(hid[at, :], w_qkv[...]).astype(BF)
        qkvg[at, 3 * D :] = dot_nt(xg[at, :], w_out[...]).astype(BF)
        return carry

    lax.fori_loop(0, rows // chunk, step, 0)


def fill_ones(ones):
    block = (iota((GROUP, GROUP), 0) >> 6) == (iota((GROUP, GROUP), 1) >> 6)
    ones[...] = jnp.where(block, 1.0, 0.0).astype(BF)


def attend(first, marks, thrs, bias, ones, qkvg, mix, dq):
    lane = iota((CELLS, 128), 1)
    cell = iota((CELLS, 128), 0)
    diag = (lane & 63) == cell
    low_half = lane < 64
    low_mask = jnp.where(low_half, 1.0, 0.0).astype(BF)
    high_mask = jnp.where(low_half, 0.0, 1.0).astype(BF)
    zero = jnp.zeros((CELLS, 128), BF)

    def by_head(x):
        a, b = x[:, :128], x[:, 128:]
        rows = [(a * low_mask, zero), (a * high_mask, zero), (zero, b * low_mask), (zero, b * high_mask)]
        return jnp.concatenate([jnp.concatenate(r, axis=1) for r in rows], axis=0)

    units = []
    for w, (mark, thr) in enumerate(zip(marks, thrs)):
        row = pl.multiple_of((first + w) * CELLS, CELLS)
        same = ((lane & 7) >= thr) == ((cell & 7) >= thr)
        valid = jnp.broadcast_to(mark, (CELLS, 128)) > 0.5
        ok = (valid & same) | diag
        ok = jnp.concatenate([ok, ok], axis=1)
        for h in range(2):
            c = h * GROUP
            at = pl.ds(row, CELLS)
            q = qkvg[at, c : c + GROUP]
            k = qkvg[at, D + c : D + c + GROUP]
            v = qkvg[at, 2 * D + c : 2 * D + c + GROUP]
            g = qkvg[at, 3 * D + c : 3 * D + c + GROUP]
            kbd, vbd = by_head(k), by_head(v)
            s = dot_nt(q, kbd)
            pg = dot_nt(g, vbd)
            e = jnp.where(ok, jnp.exp2(s * (SCALE * LOG2E) + bias[:, c : c + GROUP]), 0.0)
            units.append((at, c, q, g, kbd, vbd, e, pg))
    total = dot_nn(jnp.concatenate([u[6].astype(BF) for u in units], axis=0), ones[...])
    probs = []
    for n, u in enumerate(units):
        probs.append(u[6] / total[n * CELLS : (n + 1) * CELLS])
    dots = dot_nn(
        jnp.concatenate([(p * u[7]).astype(BF) for p, u in zip(probs, units)], axis=0), ones[...]
    )
    for n, (at, c, q, g, kbd, vbd, e, pg) in enumerate(units):
        p = probs[n]
        p_low = p.astype(BF)
        ds = (p * (pg - dots[n * CELLS : (n + 1) * CELLS]) * SCALE).astype(BF)
        mix[at, c : c + GROUP] = dot_nn(p_low, vbd).astype(BF)
        dq[at, c : c + GROUP] = dot_nn(ds, kbd).astype(BF)
        for t in range(2):
            lo, hi = t * 128, t * 128 + 128
            kg = dot_tn(ds[:, lo:hi], q[:, lo:hi])
            vg = dot_tn(p_low[:, lo:hi], g[:, lo:hi])
            dq[at, D + c + lo : D + c + hi] = jnp.where(low_half, kg[:64], kg[64:]).astype(BF)
            dq[at, 2 * D + c + lo : 2 * D + c + hi] = jnp.where(low_half, vg[:64], vg[64:]).astype(BF)


def finish(at, xt, xg, hid, istd, mix, dq, w_qkv, w_out):
    update = xt[at, :].astype(F32) + dot_nn(mix[at, :], w_out[...])
    normed_grad = dot_nt(dq[at, :], w_qkv[...])
    normed = hid[at, :].astype(F32)
    centred = normed_grad - jnp.mean(normed_grad, axis=-1, keepdims=True)
    centred = centred - normed * jnp.mean(normed_grad * normed, axis=-1, keepdims=True)
    inv = istd[at, :]
    return update, xg[at, :].astype(F32) + jnp.concatenate([inv] * 4, axis=1) * centred


def rows_of(strip):
    return strip.reshape(CELLS, D)


def strip_of(rows, count):
    parts = [rows[n * CELLS : (n + 1) * CELLS].reshape(WIN, WIN, D) for n in range(count)]
    return jnp.concatenate(parts + [jnp.zeros((WIN, WIN, D), F32)], axis=1)


def make_tables(marks_in, bias_table, rel_index, s0, s1, keys, bias, table, rel):
    rows = pltpu.roll(marks_in[...].astype(F32), 72 - s0, 0)[:64]
    lane = iota((256, 512), 1)
    place = (lax.axis_index(LAT) * 32 + s1 + (lane >> 7) * 8 + (lane & 7)) & 255
    pick = jnp.where(iota((256, 512), 0) == place, 1.0, 0.0).astype(BF)
    marks = dot_nn(rows.astype(BF), pick)
    own = (iota((64, 512), 0) & 7) == ((iota((64, 512), 1) & 63) >> 3)
    marks = jnp.sum(jnp.where(own, marks, 0.0).reshape(8, 8, 512), axis=1)
    for b in range(4):
        keys[8 * b : 8 * b + 8, :] = marks[:, 128 * b : 128 * b + 128]

    table[...] = jnp.zeros((8, 256), F32)
    table[:, :225] = bias_table[...] * LOG2E
    rel[:, :64] = rel_index[...]
    rel[:, 64:] = rel_index[...]
    at = rel[...]
    low = at < 128
    at = at & 127
    left = iota((CELLS, 128), 1) < 64
    for pair in range(4):
        found = []
        for h in (2 * pair, 2 * pair + 1):
            half = [
                jnp.take_along_axis(
                    jnp.broadcast_to(table[h : h + 1, c : c + 128], (CELLS, 128)), at, axis=1
                )
                for c in (0, 128)
            ]
            found.append(jnp.where(low, half[0], half[1]))
        bias[:, pair * 128 : pair * 128 + 128] = jnp.where(left, found[0], found[1])


def start_all(pairs, sems, first=0):
    copies = [pltpu.make_async_copy(a, b, sems.at[first + n]) for n, (a, b) in enumerate(pairs)]
    for copy in copies:
        copy.start()
    return copies


def wait_all(copies):
    for copy in copies:
        copy.wait()


def interior_kernel(
    shifts, tokens_in, grads_in, pad_in, bias_table, rel_index, w_qkv_in, w_out_in,
    updated_out, grad_out, w_part, keys, bias,
    tokens, grads, w_qkv, w_out, marks, updated, tokens_grad,
    xt, xg, hid, istd, qkvg, mix, dq, ones, table, rel, w_sum, sems,
):
    s0, s1 = shifts[0], shifts[1]
    base = lax.axis_index(LON) * 64
    mark_copies = start_all(
        [
            (pad_in.at[pl.ds(pl.multiple_of(base, 8), 64)], marks.at[0:64]),
            (pad_in.at[pl.ds(pl.multiple_of((base + 64) & 1023, 8), 8)], marks.at[64:72]),
        ],
        sems,
    )
    rows_in = start_all([(tokens_in, tokens), (grads_in, grads)], sems, 2)
    weights_in = start_all([(w_qkv_in, w_qkv), (w_out_in, w_out)], sems, 4)
    fill_ones(ones)
    wait_all(mark_copies)
    make_tables(marks, bias_table, rel_index, s0, s1, keys, bias, table, rel)
    wait_all(rows_in)

    def load(a, carry):
        at = pl.ds(s0 + a * WIN, WIN)
        x = pltpu.roll(tokens[at, :, :].astype(F32), 32 - s1, 1)
        g = pltpu.roll(grads[at, :, :].astype(F32), 32 - s1, 1)
        for b in range(3):
            row = pl.multiple_of((a * 3 + b) * CELLS, CELLS)
            c = slice(b * WIN, b * WIN + WIN)
            keep_window(rows_of(x[:, c]), rows_of(g[:, c]), row, xt, xg, hid, istd)
        return carry

    lax.fori_loop(0, 7, load, 0)
    wait_all(weights_in)
    project(21 * CELLS, 448, hid, xg, w_qkv, w_out, qkvg)

    def windows(a):
        seen = [keys[pl.ds(8 * b + a, 1), :] for b in range(3)]
        attend(a * 3, seen, [8] * 3, bias, ones, qkvg, mix, dq)

    def store(a):
        at = pl.ds(pl.multiple_of(a * 192, 64), 192)
        to = pl.ds(s0 + a * WIN, WIN)
        for rows, out in zip(finish(at, xt, xg, hid, istd, mix, dq, w_qkv, w_out), (updated, tokens_grad)):
            out[to, :, :] = pltpu.roll(strip_of(rows, 3), s1, 1).astype(BF)

    def step(a, carry):
        store(a - 1)
        windows(a)
        return carry

    windows(0)
    lax.fori_loop(1, 7, step, 0)
    store(6)
    copies = start_all([(updated, updated_out), (tokens_grad, grad_out)], sems, 2)
    for b in range(2):
        r = slice(b * 256, (b + 1) * 256)
        w_sum[r, : 3 * D] = dot_tn(hid[:, r], dq[...])
        w_sum[r, 3 * D :] = dot_tn(mix[:, r], xg[...])
        copies += start_all([(w_sum.at[r], w_part.at[r])], sems, b)
    wait_all(copies)


def edge_kernel(
    shifts, tokens_in, grads_in, halo_lon, halo_lat, halo_cor, keys, bias, w_qkv_in, w_out_in, w_part,
    lat_up, lon_up, lat_grad, lon_grad, out_lat, out_lon, out_cor, w_mine, w_other,
    tok, grad, far, low_tok, low_grad, low_far, w_qkv, w_out, to_lat, to_lon,
    xt, xg, hid, istd, qkvg, mix, dq, ones, w_sum, sems,
):
    s0, s1 = shifts[0], shifts[1]
    core = lax.axis_index("core")
    thr_edge = jnp.where(lax.axis_index(LAT) == 7, 8 - s1, 8)
    rows_in = start_all(
        [
            (tokens_in.at[:, 16:32, :], tok),
            (grads_in.at[:, 16:32, :], grad),
            (halo_lat, far),
            (tokens_in.at[56:64], low_tok.at[0:8]),
            (grads_in.at[56:64], low_grad.at[0:8]),
            (halo_lon.at[:, :, 0:D], low_tok.at[8:16]),
            (halo_lon.at[:, :, D : 2 * D], low_grad.at[8:16]),
            (halo_lat.at[56:64], low_far.at[0:8]),
            (halo_cor, low_far.at[8:16]),
        ],
        sems,
    )
    weights_in = start_all([(w_qkv_in, w_qkv), (w_out_in, w_out), (w_part, w_sum)], sems, 9)
    fill_ones(ones)
    tail = slice(11 * CELLS, 12 * CELLS)
    xg[tail, :] = jnp.zeros((CELLS, D), BF)
    hid[tail, :] = jnp.zeros((CELLS, D), BF)
    wait_all(rows_in)

    def load(a, carry):
        at = pl.ds(s0 + a * WIN, WIN)
        found = []
        for near, c in ((tok, 0), (grad, D)):
            rows = [near[at, 8:16, :].astype(F32), far[at, :, c : c + D].astype(F32)]
            found.append(rows_of(pltpu.roll(jnp.concatenate(rows, axis=1), 16 - s1, 1)[:, :8]))
        keep_window(*found, pl.multiple_of(a * CELLS, CELLS), xt, xg, hid, istd)
        return carry

    lax.fori_loop(0, 7, load, 0)
    at = pl.ds(s0, WIN)
    found = []
    for near, c in ((low_tok, 0), (low_grad, D)):
        rows = [near[at, :, :].astype(F32), low_far[at, :, c : c + D].astype(F32)]
        found.append(pltpu.roll(jnp.concatenate(rows, axis=1), 40 - s1, 1))
    for b in range(4):
        x, g = (rows_of(rows[:, b * WIN : b * WIN + WIN]) for rows in found)
        keep_window(x, g, (7 + b) * CELLS, xt, xg, hid, istd)
    wait_all(weights_in)
    project(12 * CELLS, 384, hid, xg, w_qkv, w_out, qkvg)

    def windows(a, carry):
        seen, thr = [], []
        for w in range(3):
            n = a * 3 + w
            row = jnp.where(n < 7, 24 + n, jnp.minimum(8 * n - 49, 31))
            seen.append(keys[pl.ds(row, 1), :])
            thr.append(jnp.where((n < 7) | (n == 10), thr_edge, 8))
        attend(a * 3, seen, thr, bias, ones, qkvg, mix, dq)
        return carry

    lax.fori_loop(0, 4, windows, 0)

    results = finish(slice(0, 7 * CELLS), xt, xg, hid, istd, mix, dq, w_qkv, w_out)
    for rows, near, c in zip(results, (tok, grad), (0, D)):
        for a in range(7):
            strip = strip_of(rows[a * CELLS : (a + 1) * CELLS], 1)
            strip = pltpu.roll(strip, s1, 1).astype(BF)
            near[pl.ds(s0 + a * WIN, WIN), 0:8, :] = strip[:, :8]
            to_lat[pl.ds(s0 + a * WIN, WIN), :, c : c + D] = strip[:, 8:]
    results = finish(slice(7 * CELLS, 11 * CELLS), xt, xg, hid, istd, mix, dq, w_qkv, w_out)
    for rows, low, c in zip(results, (low_tok, low_grad), (0, D)):
        strip = pltpu.roll(strip_of(rows, 4), s1, 1).astype(BF)
        low[pl.ds(s0, WIN), :, :] = strip[:, :32]
        to_lat[pl.ds(s0 + 56, WIN), :, c : c + D] = strip[:, 32:]
    to_lon[:, :, 0:D] = low_tok[8:16]
    to_lon[:, :, D : 2 * D] = low_grad[8:16]
    copies = start_all(
        [
            (tok, lat_up),
            (grad, lat_grad),
            (low_tok.at[0:8], lon_up),
            (low_grad.at[0:8], lon_grad),
            (to_lat.at[0:64], out_lat),
            (to_lat.at[64:72], out_cor),
            (to_lon, out_lon),
        ],
        sems,
    )
    for b in range(2):
        r = slice(b * 256, (b + 1) * 256)
        w_sum[r, : 3 * D] += dot_tn(hid[:, r], dq[...])
        w_sum[r, 3 * D :] += dot_tn(mix[:, r], xg[...])

    def split(n, carry):
        to = pl.ds(pl.multiple_of(n * 32, 32), 32)
        w_mine[to, :] = w_sum[pl.ds(pl.multiple_of((2 * n + core) * 32, 32), 32), :].astype(BF)
        w_other[to, :] = w_sum[pl.ds(pl.multiple_of((2 * n + 1 - core) * 32, 32), 32), :].astype(BF)
        return carry

    lax.fori_loop(0, 8, split, 0)
    wait_all(copies)


def edge_merge_kernel(
    shifts, updated, tokens_grad, lat_up, lon_up, lat_grad, lon_grad, out_updated, out_grad,
    side, low, sems,
):
    s0, s1 = shifts[0], shifts[1]
    pairs = []
    for n, out in enumerate((out_updated, out_grad)):
        pairs += [(out.at[:, 16:32, :], side.at[n]), (out.at[56:64, 0:16, :], low.at[n])]
    wait_all(start_all(pairs, sems))
    mark = iota((8, 8, D), 1) >= s1
    for n, (lat, lon) in enumerate(((lat_up, lon_up), (lat_grad, lon_grad))):

        def rest(r, carry, n=n, lat=lat):
            at = pl.ds(pl.multiple_of(r * 8, 8), 8)
            rows = side[n, at, 8:16, :].astype(F32)
            side[n, at, 8:16, :] = jnp.where(mark, lat[at, 0:8, :].astype(F32), rows).astype(BF)
            return carry

        lax.fori_loop(0, 8, rest, 0)
        later = iota((8, 16, D), 0) >= s0
        rows = side[n, 56:64, :, :].astype(F32)
        side[n, 56:64, :, :] = jnp.where(later, lon[:, 16:32, :].astype(F32), rows).astype(BF)
        later = later & (iota((8, 16, D), 1) >= s1)
        rows = low[n].astype(F32)
        low[n] = jnp.where(later, lon[:, 0:16, :].astype(F32), rows).astype(BF)
    wait_all(start_all([(b, a) for a, b in pairs], sems))


def return_kernel(
    shifts, updated, tokens_grad, in_lat, in_lon, in_cor, out_updated, out_grad, side, top, sems
):
    s0, s1 = shifts[0], shifts[1]
    outs = (out_updated, out_grad)
    tops = [(out.at[0:8], top.at[n]) for n, out in enumerate(outs)]
    sides = [(out.at[8:64, 0:16, :], side.at[n, 8:64]) for n, out in enumerate(outs)]
    tops_in, sides_in = start_all(tops, sems), start_all(sides, sems, 2)
    wait_all(tops_in)
    early = iota((8, 32, D), 0) < s0
    first = iota((8, 8, D), 1) < s1
    for n in range(2):
        cols = slice(n * D, n * D + D)
        came = in_lon[:, :, cols].astype(F32)
        corner = jnp.where(first, in_cor[:, :, cols].astype(F32), came[:, 0:8])
        came = jnp.concatenate([corner, came[:, 8:]], axis=1)
        old = top[n].astype(F32)
        back = jnp.where(first, in_lat[0:8, :, cols].astype(F32), old[:, 0:8])
        old = jnp.concatenate([back, old[:, 8:]], axis=1)
        top[n] = jnp.where(early, came, old).astype(BF)
    wait_all(sides_in)
    copies = start_all([(b, a) for a, b in tops], sems)
    for n in range(2):

        def place(r, carry, n=n):
            at = pl.ds(pl.multiple_of(r * 8, 8), 8)
            rows = side[n, at, 0:8, :].astype(F32)
            side[n, at, 0:8, :] = jnp.where(first, in_lat[at, :, n * D : n * D + D].astype(F32), rows).astype(BF)
            return carry

        lax.fori_loop(1, 8, place, 0)
        copies += start_all([sides[n][::-1]], sems, 2 + n)
    wait_all(copies)


def vmem(shape, dtype):
    return pltpu.VMEM(shape, dtype)


def sds(shape, dtype):
    return jax.ShapeDtypeStruct(shape, dtype)


IN_VMEM = pl.BlockSpec(memory_space=pltpu.VMEM)
IN_SMEM = pl.BlockSpec(memory_space=pltpu.SMEM)
IN_HBM = pl.BlockSpec(memory_space=pl.ANY)


def call(kernel, out_shape, scratch, in_specs, out_specs, aliases=None):
    return pl.pallas_call(
        kernel,
        out_shape=out_shape,
        in_specs=[IN_SMEM] + in_specs,
        out_specs=out_specs,
        scratch_shapes=scratch,
        input_output_aliases=aliases or {},
        compiler_params=pltpu.CompilerParams(vmem_limit_bytes=VMEM_LIMIT),
    )


def window_scratch(rows):
    return [vmem((rows, D), BF), vmem((rows, D), BF), vmem((rows, D), BF), vmem((rows, 128), F32)]


def attend_scratch(rows):
    return [
        vmem((rows, 4 * D), BF),
        vmem((rows, D), BF),
        vmem((rows, 3 * D), BF),
        vmem((GROUP, GROUP), BF),
    ]


def shift_to(value, d_lon, d_lat):
    pairs = []
    for a in range(16):
        for b in range(8):
            pairs.append((a * 8 + b, ((a + d_lon) % 16) * 8 + (b + d_lat) % 8))
    return lax.ppermute(value, ALL, pairs)


def scatter_sum(blocks, axes, count, beside=None):
    here = lax.axis_index(axes)
    parts = [lax.dynamic_index_in_dim(blocks, here, 0, keepdims=False)]
    for step in range(1, count):
        block = lax.dynamic_index_in_dim(blocks, (here + step) % count, 0, keepdims=False)
        pairs = [(n, (n + step) % count) for n in range(count)]
        parts.append(lax.ppermute(block, axes, pairs))
    extra = None
    if beside is not None:
        extra = beside(blocks)
        parts, extra = lax.optimization_barrier((parts, extra))
    total = parts[0].astype(F32)
    for part in parts[1:]:
        total = total + part.astype(F32)
    return total, extra


INNER, OUTER = 21 * CELLS, 12 * CELLS
GRID = sds((64, 32, D), BF)
DMA = pltpu.SemaphoreType.DMA


WEIGHTS = [vmem((D, 3 * D), BF), vmem((D, D), BF)]


def run_interior(*args):
    rows = vmem((64, 32, D), BF)
    return call(
        interior_kernel,
        [GRID, GRID, sds((D, 4 * D), F32), sds((32, 128), F32), sds((64, 512), F32)],
        [rows, rows, *WEIGHTS, vmem((72, 256), jnp.int32), rows, rows]
        + window_scratch(INNER)
        + attend_scratch(INNER)
        + [vmem((8, 256), F32), vmem((64, 128), jnp.int32), vmem((D, 4 * D), F32), DMA((6,))],
        [IN_HBM] * 3 + [IN_VMEM] * 2 + [IN_HBM] * 2,
        [IN_HBM] * 3 + [IN_VMEM] * 2,
    )(*args)


def run_edge(*args):
    lat, lon = (64, 16, D), (8, 32, D)
    far_lat, far_lon = (64, 8, 2 * D), (8, 32, 2 * D)
    return call(
        edge_kernel,
        [sds(shape, BF) for shape in (lat, lon, lat, lon, far_lat, far_lon, (8, 8, 2 * D))]
        + [sds((D // 2, 4 * D), BF)] * 2,
        [vmem(lat, BF), vmem(lat, BF), vmem(far_lat, BF)]
        + [vmem((16, 32, D), BF), vmem((16, 32, D), BF), vmem((16, 8, 2 * D), BF)]
        + WEIGHTS
        + [vmem((72, 8, 2 * D), BF), vmem(far_lon, BF)]
        + window_scratch(OUTER)
        + attend_scratch(OUTER)
        + [vmem((D, 4 * D), F32), DMA((12,))],
        [IN_HBM] * 5 + [IN_VMEM] * 2 + [IN_HBM] * 3,
        [IN_HBM] * 7 + [IN_VMEM] * 2,
    )(*args)


def run_edge_merge(*args):
    return call(
        edge_merge_kernel,
        [GRID, GRID],
        [vmem((2, 64, 16, D), BF), vmem((2, 8, 16, D), BF), DMA((4,))],
        [IN_HBM] * 2 + [IN_VMEM] * 4,
        [IN_HBM] * 2,
        {1: 0, 2: 1},
    )(*args)


def run_return(*args):
    return call(
        return_kernel,
        [GRID, GRID],
        [vmem((2, 64, 16, D), BF), vmem((2, 8, 32, D), BF), DMA((4,))],
        [IN_HBM] * 2 + [IN_VMEM] * 3,
        [IN_HBM] * 2,
        {1: 0, 2: 1},
    )(*args)


def local(tokens, pad_mask, shifts, bias_table, rel_index, w_qkv, w_out, grad_out):
    both = lambda a, b: jnp.concatenate([tokens[a, b], grad_out[a, b]], axis=-1)
    halo_lat = shift_to(both(slice(None), slice(0, 8)), 0, -1)
    halo_lon = shift_to(both(slice(0, 8), slice(None)), -1, 0)
    halo_cor = shift_to(both(slice(0, 8), slice(0, 8)), -1, -1)

    updated, tokens_grad, w_part, keys, bias = run_interior(
        shifts, tokens, grad_out, pad_mask, bias_table, rel_index, w_qkv, w_out
    )
    *edges, out_lat, out_lon, out_cor, w_mine, w_other = run_edge(
        shifts, tokens, grad_out, halo_lon, halo_lat, halo_cor, keys, bias, w_qkv, w_out, w_part
    )

    def merge_beside(blocks):
        _, *placed = lax.optimization_barrier((blocks, updated, tokens_grad))
        return *run_edge_merge(shifts, *placed, *edges), in_cor

    w_got = lax.ppermute(w_other, "core", [(0, 1), (1, 0)])
    in_lat = shift_to(out_lat, 0, 1)
    in_lon = shift_to(out_lon, 1, 0)
    in_cor = shift_to(out_cor, 1, 1)
    total = (w_mine.astype(F32) + w_got.astype(F32)).astype(BF)
    total = total.reshape(2, 4, 32, 4 * D).transpose(1, 0, 2, 3)
    total, (updated, tokens_grad, in_cor) = scatter_sum(total, "x", 4, merge_beside)
    total = total.astype(BF).reshape(2, 4, 8, 4 * D).transpose(1, 0, 2, 3)
    total, (in_lat, in_lon) = scatter_sum(total, "y", 4, lambda blocks: (in_lat, in_lon))
    total, _ = scatter_sum(total.astype(BF).reshape(4, 4, 4 * D), ("zh", "zl"), 4)

    updated, tokens_grad = run_return(shifts, updated, tokens_grad, in_lat, in_lon, in_cor)
    return (updated, tokens_grad, total[:, : 3 * D], total[:, 3 * D :])


def solution(mesh):
    fine = Mesh(mesh.devices.reshape(2, 4, 2, 4, 2), ALL)
    in_specs = (P(LON, LAT, None), P(), P(), P(), P(), P(), P(), P(LON, LAT, None))
    out_specs = (P(LON, LAT, None), P(LON, LAT, None), P(ALL, None), P(ALL, None))
    return jax.shard_map(local, mesh=fine, in_specs=in_specs, out_specs=out_specs, check_vma=False)
```

```python
import jax
import jax.numpy as jnp
from jax import lax
from jax.experimental import pallas as pl
from jax.experimental.pallas import tpu as pltpu
from jax.sharding import Mesh, PartitionSpec as P

WIN = 8
CELLS = 64
D = 512
HEADS = 8
GROUP = 256
BF = jnp.bfloat16
F32 = jnp.float32
LOG2E = 1.4426950408889634
SCALE = 0.125
VMEM_LIMIT = 56 * 2**20
LON = ("zh", "x", "core")
LAT = ("y", "zl")
ALL = LON + LAT


def dot_nn(a, b):
    return lax.dot_general(a, b, (((1,), (0,)), ((), ())), preferred_element_type=F32)


def dot_nt(a, b):
    return lax.dot_general(a, b, (((1,), (1,)), ((), ())), preferred_element_type=F32)


def dot_tn(a, b):
    return lax.dot_general(a, b, (((0,), (0,)), ((), ())), preferred_element_type=F32)


def iota(shape, dim):
    return lax.broadcasted_iota(jnp.int32, shape, dim)


def keep_window(x, g, row, xt, xg, hid, istd):
    at = pl.ds(row, CELLS)
    center = x - jnp.mean(x, axis=-1, keepdims=True)
    inv = lax.rsqrt(jnp.mean(center * center, axis=-1, keepdims=True) + 1e-05)
    hid[at, :] = (center * inv).astype(BF)
    istd[at, :] = jnp.broadcast_to(inv, (CELLS, 128))
    xt[at, :] = x.astype(BF)
    xg[at, :] = g.astype(BF)


def project(rows, chunk, hid, xg, w_qkv, w_out, qkvg):
    def step(c, carry):
        at = pl.ds(pl.multiple_of(c * chunk, 64), chunk)
        qkvg[at, : 3 * D] = dot_nn(hid[at, :], w_qkv[...]).astype(BF)
        qkvg[at, 3 * D :] = dot_nt(xg[at, :], w_out[...]).astype(BF)
        return carry

    lax.fori_loop(0, rows // chunk, step, 0)


def fill_ones(ones):
    block = (iota((GROUP, GROUP), 0) >> 6) == (iota((GROUP, GROUP), 1) >> 6)
    ones[...] = jnp.where(block, 1.0, 0.0).astype(BF)


def attend(first, marks, thrs, bias, ones, qkvg, mix, dq):
    lane = iota((CELLS, 128), 1)
    cell = iota((CELLS, 128), 0)
    diag = (lane & 63) == cell
    low_half = lane < 64
    low_mask = jnp.where(low_half, 1.0, 0.0).astype(BF)
    high_mask = jnp.where(low_half, 0.0, 1.0).astype(BF)
    zero = jnp.zeros((CELLS, 128), BF)

    def by_head(x):
        a, b = x[:, :128], x[:, 128:]
        rows = [(a * low_mask, zero), (a * high_mask, zero), (zero, b * low_mask), (zero, b * high_mask)]
        return jnp.concatenate([jnp.concatenate(r, axis=1) for r in rows], axis=0)

    units = []
    for w, (mark, thr) in enumerate(zip(marks, thrs)):
        row = pl.multiple_of((first + w) * CELLS, CELLS)
        same = ((lane & 7) >= thr) == ((cell & 7) >= thr)
        valid = jnp.broadcast_to(mark, (CELLS, 128)) > 0.5
        ok = (valid & same) | diag
        ok = jnp.concatenate([ok, ok], axis=1)
        for h in range(2):
            c = h * GROUP
            at = pl.ds(row, CELLS)
            q = qkvg[at, c : c + GROUP]
            k = qkvg[at, D + c : D + c + GROUP]
            v = qkvg[at, 2 * D + c : 2 * D + c + GROUP]
            g = qkvg[at, 3 * D + c : 3 * D + c + GROUP]
            kbd, vbd = by_head(k), by_head(v)
            s = dot_nt(q, kbd)
            pg = dot_nt(g, vbd)
            e = jnp.where(ok, jnp.exp2(s * (SCALE * LOG2E) + bias[:, c : c + GROUP]), 0.0)
            units.append((at, c, q, g, kbd, vbd, e, pg))
    total = dot_nn(jnp.concatenate([u[6].astype(BF) for u in units], axis=0), ones[...])
    probs = []
    for n, u in enumerate(units):
        probs.append(u[6] / total[n * CELLS : (n + 1) * CELLS])
    dots = dot_nn(
        jnp.concatenate([(p * u[7]).astype(BF) for p, u in zip(probs, units)], axis=0), ones[...]
    )
    for n, (at, c, q, g, kbd, vbd, e, pg) in enumerate(units):
        p = probs[n]
        p_low = p.astype(BF)
        ds = (p * (pg - dots[n * CELLS : (n + 1) * CELLS]) * SCALE).astype(BF)
        mix[at, c : c + GROUP] = dot_nn(p_low, vbd).astype(BF)
        dq[at, c : c + GROUP] = dot_nn(ds, kbd).astype(BF)
        for t in range(2):
            lo, hi = t * 128, t * 128 + 128
            kg = dot_tn(ds[:, lo:hi], q[:, lo:hi])
            vg = dot_tn(p_low[:, lo:hi], g[:, lo:hi])
            dq[at, D + c + lo : D + c + hi] = jnp.where(low_half, kg[:64], kg[64:]).astype(BF)
            dq[at, 2 * D + c + lo : 2 * D + c + hi] = jnp.where(low_half, vg[:64], vg[64:]).astype(BF)


def finish(at, xt, xg, hid, istd, mix, dq, w_qkv, w_out):
    update = xt[at, :].astype(F32) + dot_nn(mix[at, :], w_out[...])
    normed_grad = dot_nt(dq[at, :], w_qkv[...])
    normed = hid[at, :].astype(F32)
    centred = normed_grad - jnp.mean(normed_grad, axis=-1, keepdims=True)
    centred = centred - normed * jnp.mean(normed_grad * normed, axis=-1, keepdims=True)
    inv = istd[at, :]
    return update, xg[at, :].astype(F32) + jnp.concatenate([inv] * 4, axis=1) * centred


def rows_of(strip):
    return strip.reshape(CELLS, D)


def strip_of(rows, count):
    parts = [rows[n * CELLS : (n + 1) * CELLS].reshape(WIN, WIN, D) for n in range(count)]
    return jnp.concatenate(parts + [jnp.zeros((WIN, WIN, D), F32)], axis=1)


def make_tables(marks_in, bias_table, rel_index, s0, s1, keys, bias, table, rel):
    rows = pltpu.roll(marks_in[...].astype(F32), 72 - s0, 0)[:64]
    lane = iota((256, 512), 1)
    place = (lax.axis_index(LAT) * 32 + s1 + (lane >> 7) * 8 + (lane & 7)) & 255
    pick = jnp.where(iota((256, 512), 0) == place, 1.0, 0.0).astype(BF)
    marks = dot_nn(rows.astype(BF), pick)
    own = (iota((64, 512), 0) & 7) == ((iota((64, 512), 1) & 63) >> 3)
    marks = jnp.sum(jnp.where(own, marks, 0.0).reshape(8, 8, 512), axis=1)
    for b in range(4):
        keys[8 * b : 8 * b + 8, :] = marks[:, 128 * b : 128 * b + 128]

    table[...] = jnp.zeros((8, 256), F32)
    table[:, :225] = bias_table[...] * LOG2E
    rel[:, :64] = rel_index[...]
    rel[:, 64:] = rel_index[...]
    at = rel[...]
    low = at < 128
    at = at & 127
    left = iota((CELLS, 128), 1) < 64
    for pair in range(4):
        found = []
        for h in (2 * pair, 2 * pair + 1):
            half = [
                jnp.take_along_axis(
                    jnp.broadcast_to(table[h : h + 1, c : c + 128], (CELLS, 128)), at, axis=1
                )
                for c in (0, 128)
            ]
            found.append(jnp.where(low, half[0], half[1]))
        bias[:, pair * 128 : pair * 128 + 128] = jnp.where(left, found[0], found[1])


def start_all(pairs, sems, first=0):
    copies = [pltpu.make_async_copy(a, b, sems.at[first + n]) for n, (a, b) in enumerate(pairs)]
    for copy in copies:
        copy.start()
    return copies


def wait_all(copies):
    for copy in copies:
        copy.wait()


def interior_kernel(
    shifts, tokens_in, grads_in, pad_in, bias_table, rel_index, w_qkv_in, w_out_in,
    updated_out, grad_out, w_part, keys, bias,
    tokens, grads, w_qkv, w_out, marks, updated, tokens_grad,
    xt, xg, hid, istd, qkvg, mix, dq, ones, table, rel, w_sum, sems,
):
    s0, s1 = shifts[0], shifts[1]
    base = lax.axis_index(LON) * 64
    mark_copies = start_all(
        [
            (pad_in.at[pl.ds(pl.multiple_of(base, 8), 64)], marks.at[0:64]),
            (pad_in.at[pl.ds(pl.multiple_of((base + 64) & 1023, 8), 8)], marks.at[64:72]),
        ],
        sems,
    )
    rows_in = start_all([(tokens_in, tokens), (grads_in, grads)], sems, 2)
    weights_in = start_all([(w_qkv_in, w_qkv), (w_out_in, w_out)], sems, 4)
    fill_ones(ones)
    wait_all(mark_copies)
    make_tables(marks, bias_table, rel_index, s0, s1, keys, bias, table, rel)
    wait_all(rows_in)

    def load(a, carry):
        at = pl.ds(s0 + a * WIN, WIN)
        x = pltpu.roll(tokens[at, :, :].astype(F32), 32 - s1, 1)
        g = pltpu.roll(grads[at, :, :].astype(F32), 32 - s1, 1)
        for b in range(3):
            row = pl.multiple_of((a * 3 + b) * CELLS, CELLS)
            c = slice(b * WIN, b * WIN + WIN)
            keep_window(rows_of(x[:, c]), rows_of(g[:, c]), row, xt, xg, hid, istd)
        return carry

    lax.fori_loop(0, 7, load, 0)
    wait_all(weights_in)
    project(21 * CELLS, 448, hid, xg, w_qkv, w_out, qkvg)

    def windows(a):
        seen = [keys[pl.ds(8 * b + a, 1), :] for b in range(3)]
        attend(a * 3, seen, [8] * 3, bias, ones, qkvg, mix, dq)

    def store(a):
        at = pl.ds(pl.multiple_of(a * 192, 64), 192)
        to = pl.ds(s0 + a * WIN, WIN)
        for rows, out in zip(finish(at, xt, xg, hid, istd, mix, dq, w_qkv, w_out), (updated, tokens_grad)):
            out[to, :, :] = pltpu.roll(strip_of(rows, 3), s1, 1).astype(BF)

    def step(a, carry):
        store(a - 1)
        windows(a)
        return carry

    windows(0)
    lax.fori_loop(1, 7, step, 0)
    store(6)
    copies = start_all([(updated, updated_out), (tokens_grad, grad_out)], sems, 2)
    for b in range(2):
        r = slice(b * 256, (b + 1) * 256)
        w_sum[r, : 3 * D] = dot_tn(hid[:, r], dq[...])
        w_sum[r, 3 * D :] = dot_tn(mix[:, r], xg[...])
        copies += start_all([(w_sum.at[r], w_part.at[r])], sems, b)
    wait_all(copies)


def edge_kernel(
    shifts, tokens_in, grads_in, halo_lon, halo_lat, halo_cor, keys, bias, w_qkv_in, w_out_in, w_part,
    lat_up, lon_up, lat_grad, lon_grad, out_lat, out_lon, out_cor, w_mine, w_other,
    tok, grad, far, low_tok, low_grad, low_far, w_qkv, w_out, to_lat, to_lon,
    xt, xg, hid, istd, qkvg, mix, dq, ones, w_sum, sems,
):
    s0, s1 = shifts[0], shifts[1]
    core = lax.axis_index("core")
    thr_edge = jnp.where(lax.axis_index(LAT) == 7, 8 - s1, 8)
    rows_in = start_all(
        [
            (tokens_in.at[:, 16:32, :], tok),
            (grads_in.at[:, 16:32, :], grad),
            (halo_lat, far),
            (tokens_in.at[56:64], low_tok.at[0:8]),
            (grads_in.at[56:64], low_grad.at[0:8]),
            (halo_lon.at[:, :, 0:D], low_tok.at[8:16]),
            (halo_lon.at[:, :, D : 2 * D], low_grad.at[8:16]),
            (halo_lat.at[56:64], low_far.at[0:8]),
            (halo_cor, low_far.at[8:16]),
        ],
        sems,
    )
    weights_in = start_all([(w_qkv_in, w_qkv), (w_out_in, w_out), (w_part, w_sum)], sems, 9)
    fill_ones(ones)
    tail = slice(11 * CELLS, 12 * CELLS)
    xg[tail, :] = jnp.zeros((CELLS, D), BF)
    hid[tail, :] = jnp.zeros((CELLS, D), BF)
    wait_all(rows_in)

    def load(a, carry):
        at = pl.ds(s0 + a * WIN, WIN)
        found = []
        for near, c in ((tok, 0), (grad, D)):
            rows = [near[at, 8:16, :].astype(F32), far[at, :, c : c + D].astype(F32)]
            found.append(rows_of(pltpu.roll(jnp.concatenate(rows, axis=1), 16 - s1, 1)[:, :8]))
        keep_window(*found, pl.multiple_of(a * CELLS, CELLS), xt, xg, hid, istd)
        return carry

    lax.fori_loop(0, 7, load, 0)
    at = pl.ds(s0, WIN)
    found = []
    for near, c in ((low_tok, 0), (low_grad, D)):
        rows = [near[at, :, :].astype(F32), low_far[at, :, c : c + D].astype(F32)]
        found.append(pltpu.roll(jnp.concatenate(rows, axis=1), 40 - s1, 1))
    for b in range(4):
        x, g = (rows_of(rows[:, b * WIN : b * WIN + WIN]) for rows in found)
        keep_window(x, g, (7 + b) * CELLS, xt, xg, hid, istd)
    wait_all(weights_in)
    project(12 * CELLS, 384, hid, xg, w_qkv, w_out, qkvg)

    def windows(a, carry):
        seen, thr = [], []
        for w in range(3):
            n = a * 3 + w
            row = jnp.where(n < 7, 24 + n, jnp.minimum(8 * n - 49, 31))
            seen.append(keys[pl.ds(row, 1), :])
            thr.append(jnp.where((n < 7) | (n == 10), thr_edge, 8))
        attend(a * 3, seen, thr, bias, ones, qkvg, mix, dq)
        return carry

    lax.fori_loop(0, 4, windows, 0)

    results = finish(slice(0, 7 * CELLS), xt, xg, hid, istd, mix, dq, w_qkv, w_out)
    for rows, near, c in zip(results, (tok, grad), (0, D)):
        for a in range(7):
            strip = strip_of(rows[a * CELLS : (a + 1) * CELLS], 1)
            strip = pltpu.roll(strip, s1, 1).astype(BF)
            near[pl.ds(s0 + a * WIN, WIN), 0:8, :] = strip[:, :8]
            to_lat[pl.ds(s0 + a * WIN, WIN), :, c : c + D] = strip[:, 8:]
    results = finish(slice(7 * CELLS, 11 * CELLS), xt, xg, hid, istd, mix, dq, w_qkv, w_out)
    for rows, low, c in zip(results, (low_tok, low_grad), (0, D)):
        strip = pltpu.roll(strip_of(rows, 4), s1, 1).astype(BF)
        low[pl.ds(s0, WIN), :, :] = strip[:, :32]
        to_lat[pl.ds(s0 + 56, WIN), :, c : c + D] = strip[:, 32:]
    to_lon[:, :, 0:D] = low_tok[8:16]
    to_lon[:, :, D : 2 * D] = low_grad[8:16]
    copies = start_all(
        [
            (tok, lat_up),
            (grad, lat_grad),
            (low_tok.at[0:8], lon_up),
            (low_grad.at[0:8], lon_grad),
            (to_lat.at[0:64], out_lat),
            (to_lat.at[64:72], out_cor),
            (to_lon, out_lon),
        ],
        sems,
    )
    for b in range(2):
        r = slice(b * 256, (b + 1) * 256)
        w_sum[r, : 3 * D] += dot_tn(hid[:, r], dq[...])
        w_sum[r, 3 * D :] += dot_tn(mix[:, r], xg[...])

    def split(n, carry):
        to = pl.ds(pl.multiple_of(n * 32, 32), 32)
        w_mine[to, :] = w_sum[pl.ds(pl.multiple_of((2 * n + core) * 32, 32), 32), :].astype(BF)
        w_other[to, :] = w_sum[pl.ds(pl.multiple_of((2 * n + 1 - core) * 32, 32), 32), :].astype(BF)
        return carry

    lax.fori_loop(0, 8, split, 0)
    wait_all(copies)


def edge_merge_kernel(
    shifts, updated, tokens_grad, lat_up, lon_up, lat_grad, lon_grad, out_updated, out_grad,
    side, low, sems,
):
    s0, s1 = shifts[0], shifts[1]
    pairs = []
    for n, out in enumerate((out_updated, out_grad)):
        pairs += [(out.at[:, 16:32, :], side.at[n]), (out.at[56:64, 0:16, :], low.at[n])]
    wait_all(start_all(pairs, sems))
    mark = iota((8, 8, D), 1) >= s1
    for n, (lat, lon) in enumerate(((lat_up, lon_up), (lat_grad, lon_grad))):

        def rest(r, carry, n=n, lat=lat):
            at = pl.ds(pl.multiple_of(r * 8, 8), 8)
            rows = side[n, at, 8:16, :].astype(F32)
            side[n, at, 8:16, :] = jnp.where(mark, lat[at, 0:8, :].astype(F32), rows).astype(BF)
            return carry

        lax.fori_loop(0, 8, rest, 0)
        later = iota((8, 16, D), 0) >= s0
        rows = side[n, 56:64, :, :].astype(F32)
        side[n, 56:64, :, :] = jnp.where(later, lon[:, 16:32, :].astype(F32), rows).astype(BF)
        later = later & (iota((8, 16, D), 1) >= s1)
        rows = low[n].astype(F32)
        low[n] = jnp.where(later, lon[:, 0:16, :].astype(F32), rows).astype(BF)
    wait_all(start_all([(b, a) for a, b in pairs], sems))


def return_kernel(
    shifts, updated, tokens_grad, in_lat, in_lon, in_cor, out_updated, out_grad, side, top, sems
):
    s0, s1 = shifts[0], shifts[1]
    outs = (out_updated, out_grad)
    tops = [(out.at[0:8], top.at[n]) for n, out in enumerate(outs)]
    sides = [(out.at[8:64, 0:16, :], side.at[n, 8:64]) for n, out in enumerate(outs)]
    tops_in, sides_in = start_all(tops, sems), start_all(sides, sems, 2)
    wait_all(tops_in)
    early = iota((8, 32, D), 0) < s0
    first = iota((8, 8, D), 1) < s1
    for n in range(2):
        cols = slice(n * D, n * D + D)
        came = in_lon[:, :, cols].astype(F32)
        corner = jnp.where(first, in_cor[:, :, cols].astype(F32), came[:, 0:8])
        came = jnp.concatenate([corner, came[:, 8:]], axis=1)
        old = top[n].astype(F32)
        back = jnp.where(first, in_lat[0:8, :, cols].astype(F32), old[:, 0:8])
        old = jnp.concatenate([back, old[:, 8:]], axis=1)
        top[n] = jnp.where(early, came, old).astype(BF)
    wait_all(sides_in)
    copies = start_all([(b, a) for a, b in tops], sems)
    for n in range(2):

        def place(r, carry, n=n):
            at = pl.ds(pl.multiple_of(r * 8, 8), 8)
            rows = side[n, at, 0:8, :].astype(F32)
            side[n, at, 0:8, :] = jnp.where(first, in_lat[at, :, n * D : n * D + D].astype(F32), rows).astype(BF)
            return carry

        lax.fori_loop(1, 8, place, 0)
        copies += start_all([sides[n][::-1]], sems, 2 + n)
    wait_all(copies)


def vmem(shape, dtype):
    return pltpu.VMEM(shape, dtype)


def sds(shape, dtype):
    return jax.ShapeDtypeStruct(shape, dtype)


IN_VMEM = pl.BlockSpec(memory_space=pltpu.VMEM)
IN_SMEM = pl.BlockSpec(memory_space=pltpu.SMEM)
IN_HBM = pl.BlockSpec(memory_space=pl.ANY)


def call(kernel, out_shape, scratch, in_specs, out_specs, aliases=None):
    return pl.pallas_call(
        kernel,
        out_shape=out_shape,
        in_specs=[IN_SMEM] + in_specs,
        out_specs=out_specs,
        scratch_shapes=scratch,
        input_output_aliases=aliases or {},
        compiler_params=pltpu.CompilerParams(vmem_limit_bytes=VMEM_LIMIT),
    )


def window_scratch(rows):
    return [vmem((rows, D), BF), vmem((rows, D), BF), vmem((rows, D), BF), vmem((rows, 128), F32)]


def attend_scratch(rows):
    return [
        vmem((rows, 4 * D), BF),
        vmem((rows, D), BF),
        vmem((rows, 3 * D), BF),
        vmem((GROUP, GROUP), BF),
    ]


def shift_to(value, d_lon, d_lat):
    pairs = []
    for a in range(16):
        for b in range(8):
            pairs.append((a * 8 + b, ((a + d_lon) % 16) * 8 + (b + d_lat) % 8))
    return lax.ppermute(value, ALL, pairs)


def scatter_sum(blocks, axes, count, beside=None):
    here = lax.axis_index(axes)
    parts = [lax.dynamic_index_in_dim(blocks, here, 0, keepdims=False)]
    for step in range(1, count):
        block = lax.dynamic_index_in_dim(blocks, (here + step) % count, 0, keepdims=False)
        pairs = [(n, (n + step) % count) for n in range(count)]
        parts.append(lax.ppermute(block, axes, pairs))
    extra = None
    if beside is not None:
        extra = beside(blocks)
        parts, extra = lax.optimization_barrier((parts, extra))
    total = parts[0].astype(F32)
    for part in parts[1:]:
        total = total + part.astype(F32)
    return total, extra


INNER, OUTER = 21 * CELLS, 12 * CELLS
GRID = sds((64, 32, D), BF)
DMA = pltpu.SemaphoreType.DMA


WEIGHTS = [vmem((D, 3 * D), BF), vmem((D, D), BF)]


def run_interior(*args):
    rows = vmem((64, 32, D), BF)
    return call(
        interior_kernel,
        [GRID, GRID, sds((D, 4 * D), F32), sds((32, 128), F32), sds((64, 512), F32)],
        [rows, rows, *WEIGHTS, vmem((72, 256), jnp.int32), rows, rows]
        + window_scratch(INNER)
        + attend_scratch(INNER)
        + [vmem((8, 256), F32), vmem((64, 128), jnp.int32), vmem((D, 4 * D), F32), DMA((6,))],
        [IN_HBM] * 3 + [IN_VMEM] * 2 + [IN_HBM] * 2,
        [IN_HBM] * 3 + [IN_VMEM] * 2,
    )(*args)


def run_edge(*args):
    lat, lon = (64, 16, D), (8, 32, D)
    far_lat, far_lon = (64, 8, 2 * D), (8, 32, 2 * D)
    return call(
        edge_kernel,
        [sds(shape, BF) for shape in (lat, lon, lat, lon, far_lat, far_lon, (8, 8, 2 * D))]
        + [sds((D // 2, 4 * D), BF)] * 2,
        [vmem(lat, BF), vmem(lat, BF), vmem(far_lat, BF)]
        + [vmem((16, 32, D), BF), vmem((16, 32, D), BF), vmem((16, 8, 2 * D), BF)]
        + WEIGHTS
        + [vmem((72, 8, 2 * D), BF), vmem(far_lon, BF)]
        + window_scratch(OUTER)
        + attend_scratch(OUTER)
        + [vmem((D, 4 * D), F32), DMA((12,))],
        [IN_HBM] * 5 + [IN_VMEM] * 2 + [IN_HBM] * 3,
        [IN_HBM] * 7 + [IN_VMEM] * 2,
    )(*args)


def run_edge_merge(*args):
    return call(
        edge_merge_kernel,
        [GRID, GRID],
        [vmem((2, 64, 16, D), BF), vmem((2, 8, 16, D), BF), DMA((4,))],
        [IN_HBM] * 2 + [IN_VMEM] * 4,
        [IN_HBM] * 2,
        {1: 0, 2: 1},
    )(*args)


def run_return(*args):
    return call(
        return_kernel,
        [GRID, GRID],
        [vmem((2, 64, 16, D), BF), vmem((2, 8, 32, D), BF), DMA((4,))],
        [IN_HBM] * 2 + [IN_VMEM] * 3,
        [IN_HBM] * 2,
        {1: 0, 2: 1},
    )(*args)


def local(tokens, pad_mask, shifts, bias_table, rel_index, w_qkv, w_out, grad_out):
    both = lambda a, b: jnp.concatenate([tokens[a, b], grad_out[a, b]], axis=-1)
    halo_lat = shift_to(both(slice(None), slice(0, 8)), 0, -1)
    halo_lon = shift_to(both(slice(0, 8), slice(None)), -1, 0)
    halo_cor = shift_to(both(slice(0, 8), slice(0, 8)), -1, -1)

    updated, tokens_grad, w_part, keys, bias = run_interior(
        shifts, tokens, grad_out, pad_mask, bias_table, rel_index, w_qkv, w_out
    )
    *edges, out_lat, out_lon, out_cor, w_mine, w_other = run_edge(
        shifts, tokens, grad_out, halo_lon, halo_lat, halo_cor, keys, bias, w_qkv, w_out, w_part
    )

    def merge_beside(blocks):
        _, *placed = lax.optimization_barrier((blocks, updated, tokens_grad))
        return run_edge_merge(shifts, *placed, *edges)

    w_got = lax.ppermute(w_other, "core", [(0, 1), (1, 0)])
    in_lat = shift_to(out_lat, 0, 1)
    in_lon = shift_to(out_lon, 1, 0)
    in_cor = shift_to(out_cor, 1, 1)
    total = (w_mine.astype(F32) + w_got.astype(F32)).astype(BF)
    total = total.reshape(2, 4, 32, 4 * D).transpose(1, 0, 2, 3)
    total, (updated, tokens_grad) = scatter_sum(total, "x", 4, merge_beside)
    total = total.astype(BF).reshape(2, 4, 8, 4 * D).transpose(1, 0, 2, 3)
    total, (in_lat, in_lon) = scatter_sum(total, "y", 4, lambda blocks: (in_lat, in_lon))
    total, _ = scatter_sum(total.astype(BF).reshape(4, 4, 4 * D), ("zh", "zl"), 4)

    updated, tokens_grad = run_return(shifts, updated, tokens_grad, in_lat, in_lon, in_cor)
    return (updated, tokens_grad, total[:, : 3 * D], total[:, 3 * D :])


def solution(mesh):
    fine = Mesh(mesh.devices.reshape(2, 4, 2, 4, 2), ALL)
    in_specs = (P(LON, LAT, None), P(), P(), P(), P(), P(), P(), P(LON, LAT, None))
    out_specs = (P(LON, LAT, None), P(LON, LAT, None), P(ALL, None), P(ALL, None))
    return jax.shard_map(local, mesh=fine, in_specs=in_specs, out_specs=out_specs, check_vma=False)
```
